32 devices in a mesh: ctx: 8 (over y, x, core), fsdp: 4 (over z).
Axes of the slice: x: 2, y: 2, z: 4, core: 2. Of those that a mesh axis runs over, the one named last changes fastest.
Arguments:
- tokens: bfloat16 [4, 1024, 1024], P('fsdp', 'ctx'), may hold values from -6 to 6
- segment_ids: int32 [4, 1024], P('fsdp', 'ctx'), may hold values from 0 to 3, never falling along the last dimension, each value on 1 to 512 neighbouring positions
- random_blocks: int32 [4, 16, 16, 3], P('fsdp', 'ctx'), may hold values from 0 to 15, as said below
- global_blocks: int32 [4, 2], P('fsdp'), may hold values from 0 to 15, as said below
- first_gain: bfloat16 [1024], P('fsdp'), may hold values from 0.5 to 1.5
- first_bias: bfloat16 [1024], P('fsdp'), may hold values from -1.796875 to 1.796875
- joint_weight: bfloat16 [1024, 3072], P('fsdp'), may hold values from -0.1875 to 0.1875
- output_weight: bfloat16 [1024, 1024], P('fsdp'), may hold values from -2 to 2
- second_gain: bfloat16 [1024], P('fsdp'), may hold values from 0.5 to 1.5
- second_bias: bfloat16 [1024], P('fsdp'), may hold values from -1.796875 to 1.796875
- up_weight: bfloat16 [1024, 4096], P('fsdp'), may hold values from -0.1875 to 0.1875
- up_bias: bfloat16 [4096], P('fsdp'), may hold values from -3 to 3
- down_weight: bfloat16 [4096, 1024], P('fsdp'), may hold values from -0.09375 to 0.09375
- down_bias: bfloat16 [1024], P('fsdp'), may hold values from -1.796875 to 1.796875
- cotangent: bfloat16 [4, 1024, 1024], P('fsdp', 'ctx'), may hold values from -6 to 6
Outputs:
- layer_out: bfloat16 [4, 1024, 1024], P('fsdp', 'ctx')
- tokens_grad: float32 [4, 1024, 1024], P('fsdp', 'ctx')
- first_gain_grad: float32 [1024], P('fsdp')
- first_bias_grad: float32 [1024], P('fsdp')
- joint_weight_grad: float32 [1024, 3072], P('fsdp')
- output_weight_grad: float32 [1024, 1024], P('fsdp')
- second_gain_grad: float32 [1024], P('fsdp')
- second_bias_grad: float32 [1024], P('fsdp')
- up_weight_grad: float32 [1024, 4096], P('fsdp')
- up_bias_grad: float32 [4096], P('fsdp')
- down_weight_grad: float32 [4096, 1024], P('fsdp')
- down_bias_grad: float32 [1024], P('fsdp')
The draws below stay inside these ranges and needn't reach their ends.
Inputs may be any that keep to these rules, and one draw needn't show every extreme that they name: `random_blocks`: for each sequence, query block and head, 3 different blocks of the sequence, none of them the query block, a neighbour of it or a global block of the sequence. `global_blocks`: 2 different blocks of each sequence.
All inputs are finite; a program needn't handle non-finite values.
Results may differ from the reference program's by a relative error of at most 0.02.
Values may be sent and summed in bfloat16 or wider, within the bound.
A program may use at most 192 MiB of HBM per device.

```python
import math
import jax
import jax.numpy as jnp
import numpy as np
from jax import lax

D = 1024
FF = 4096
H = 16
HS = 64
BLOCK = 64
RANDOM = 3
GLOBAL = 2
SEQ = 1024
NB = 16
SEQS = 4


def pick_globals(key):
    sub_key = jax.random.fold_in(key, 11)
    scores = jax.random.randint(sub_key, (SEQS, NB), 0, 1 << 20, dtype=jnp.int32) * NB + jnp.arange(NB, dtype=jnp.int32)[None, :]
    return jnp.argsort(scores, axis=1)[:, :GLOBAL].astype(jnp.int32)


def draw_global_blocks(key, part):
    return pick_globals(key)


def draw_random_blocks(key, part):
    chosen = pick_globals(key)
    sub_key = jax.random.fold_in(key, 23)
    candidates = jnp.arange(NB, dtype=jnp.int32)
    scores = jax.random.randint(sub_key, (SEQS, NB, H, NB), 0, 1 << 20, dtype=jnp.int32) * NB + candidates[None, None, None, :]
    near = jnp.abs(candidates[None, :] - candidates[:, None]) <= 1
    is_global = jnp.any(candidates[None, :, None] == chosen[:, None, :], axis=2)
    excluded = near[None, :, :] | is_global[:, None, :]
    scores = scores + excluded[:, :, None, :].astype(jnp.int32) * (1 << 28)
    return jnp.argsort(scores, axis=3)[..., :RANDOM].astype(jnp.int32)


def levels(key, shape, shards, smallest, high):
    level = 1.0
    for dim, parts in shards:
        heights = jax.random.uniform(jax.random.fold_in(jax.random.fold_in(key, 6), dim), (parts,), jnp.float32, smallest / len(shards), high / len(shards))
        level = level * jnp.repeat(jnp.exp(heights), shape[dim] // parts).reshape((-1,) + (1,) * (len(shape) - 1 - dim))
    return level


def length_profile(count, total, limit, lean):
    weights = [(1 << 20) // math.isqrt(grade ** lean) + 1 for grade in range(2, count + 1)]
    surplus, counts = total - limit - (count - 1), [1] * (count - 1)
    while surplus > 0:
        movable = [i for i in range(count - 1) if counts[i] < limit]
        mass, budget = sum([weights[i] for i in movable]), surplus
        for i in movable:
            more = min(limit - counts[i], max(1, budget * weights[i] // mass), surplus)
            counts[i] = counts[i] + more
            surplus = surplus - more
    return np.array([limit] + counts)


def ragged_sizes(key, number_of, total, reach, slope):
    if number_of == 2:
        one = jax.random.randint(key, (), max(1, total - reach), min(reach, total - 1) + 1)
        return jnp.stack([one, total - one])
    tallies = jnp.asarray(length_profile(number_of, total, reach, slope), jnp.int32)
    twos = (number_of - 1) // 2
    giver, sink = tallies[1:1 + 2 * twos:2], tallies[2:2 + 2 * twos:2]
    room = jnp.minimum(giver - 1, reach - sink)
    passed = jax.random.randint(jax.random.fold_in(key, 1), (twos,), 0, 1 << 20) % (room + 1)
    tallies = tallies.at[1:1 + 2 * twos:2].set(giver - passed).at[2:2 + 2 * twos:2].set(sink + passed)
    return tallies[jax.random.permutation(jax.random.fold_in(key, 2), number_of)]


def centred(own_key, shape, scale, limit, cuts=(), kind=jnp.bfloat16):
    drawn = jax.random.normal(own_key, shape, jnp.float32) * scale
    if len(cuts) > 0:
        drawn = levels(own_key, shape, cuts, -0.22, 0.18) * drawn
    return jnp.clip(drawn, min=-limit, max=limit).astype(kind)


def setup_inputs(seed: int = 0) -> dict:
    key_of = jax.random.split(jax.random.key(seed), 16)
    tokens = centred(key_of[0], (SEQS, SEQ, D), 1.0, 6.0, ((0, 4), (1, 8)))
    segment_ids = jax.vmap(lambda own: jnp.searchsorted(jnp.cumsum(ragged_sizes(own, max(2, SEQ // 256), SEQ, SEQ // 2, 2)), jnp.arange(SEQ), side="right"))(jax.random.split(key_of[1], SEQS)).reshape((SEQS, SEQ)).astype(jnp.int32)
    random_blocks = draw_random_blocks(jax.random.fold_in(key_of[15], 71), 0)
    global_blocks = draw_global_blocks(jax.random.fold_in(key_of[15], 71), 0)
    first_gain = jnp.clip(1.0 + 0.1 * jax.random.normal(key_of[4], (D,), jnp.float32), 0.5, 1.5).astype(jnp.bfloat16)
    first_bias = centred(key_of[5], (D,), 0.3, 1.796875, ((0, 4),))
    joint_weight = centred(key_of[6], (D, 3 * D), D ** -0.5, 0.1875, ((0, 4),))
    output_weight = centred(key_of[7], (D, D), (max(1, D // 128)) ** -0.5, 2.0, ((0, 4),))
    second_gain = jnp.clip(1.0 + 0.1 * jax.random.normal(key_of[8], (D,), jnp.float32), 0.5, 1.5).astype(jnp.bfloat16)
    second_bias = centred(key_of[9], (D,), 0.3, 1.796875, ((0, 4),))
    up_weight = centred(key_of[10], (D, FF), D ** -0.5, 0.1875, ((0, 4),))
    up_bias = centred(key_of[11], (FF,), 0.5, 3.0, ((0, 4),))
    down_weight = centred(key_of[12], (FF, D), FF ** -0.5, 0.09375, ((0, 4),))
    down_bias = centred(key_of[13], (D,), 0.3, 1.796875, ((0, 4),))
    cotangent = centred(key_of[14], (SEQS, SEQ, D), 1.0, 6.0, ((0, 4), (1, 8)))
    return dict(tokens=tokens, segment_ids=segment_ids, random_blocks=random_blocks, global_blocks=global_blocks, first_gain=first_gain, first_bias=first_bias, joint_weight=joint_weight, output_weight=output_weight, second_gain=second_gain, second_bias=second_bias, up_weight=up_weight, up_bias=up_bias, down_weight=down_weight, down_bias=down_bias, cotangent=cotangent)


@jax.custom_vjp
def low(v):
    return lax.optimization_barrier(v.astype(jnp.bfloat16)).astype(jnp.float32)

@jax.custom_vjp
def low_back(v):
    return v

def low_keep(v):
    return (low(v), None)

def low_pass(kept, grad):
    return (grad,)

def back_keep(v):
    return (v, None)

def back_low(kept, grad):
    return (low(grad),)
low.defvjp(low_keep, low_pass)
low_back.defvjp(back_keep, back_low)
HIGH = lax.Precision.HIGHEST
SCALE_QK = 0.125
NEG_FILL = -1e+30

def normalize(values, gain, shift):
    centre = lax.optimization_barrier(jnp.mean(values, axis=-1, keepdims=True))
    offset = values - centre
    spread = lax.optimization_barrier(jnp.mean(offset * offset, axis=-1, keepdims=True))
    return offset * lax.rsqrt(spread + 1e-05) * gain + shift

def key_lists(block_ids, random_part, global_pair, block_count):
    heads = random_part.shape[1]
    number = block_ids.shape[0]
    window = block_ids[:, None] + jnp.arange(-1, 2, dtype=jnp.int32)[None, :]
    window_ok = (window >= 0) & (window < block_count)
    near = jnp.abs(global_pair[None, :] - block_ids[:, None]) <= 1
    indices = jnp.concatenate([jnp.broadcast_to(window[:, None, :], (number, heads, 3)), random_part, jnp.broadcast_to(global_pair[None, None, :], (number, heads, global_pair.shape[0]))], axis=2)
    valid = jnp.concatenate([jnp.broadcast_to(window_ok[:, None, :], (number, heads, 3)), jnp.ones(random_part.shape, jnp.bool_), jnp.broadcast_to(~near[:, None, :], (number, heads, global_pair.shape[0]))], axis=2)
    return (jnp.clip(indices, 0, block_count - 1).astype(jnp.int32), valid)

def masked_softmax(raw, allow, axes):
    masked = jnp.where(allow, raw, NEG_FILL)
    peak = lax.optimization_barrier(jnp.max(masked, axis=axes, keepdims=True))
    weights = jnp.where(allow, jnp.exp(masked - peak), 0.0)
    return weights / lax.optimization_barrier(jnp.sum(weights, axis=axes, keepdims=True))

def attend(query, keys, values, seg_seq, random_seq, global_seq):
    block_ids = jnp.arange(NB, dtype=jnp.int32)
    indices, valid = key_lists(block_ids, random_seq, global_seq, NB)
    seg_blocks = seg_seq.reshape(NB, BLOCK)

    def one_head(items):
        query_head, keys_head, values_head, index_head, valid_head = items
        query_blocks = query_head.reshape(NB, BLOCK, HS)
        key_sel = keys_head.reshape(NB, BLOCK, HS)[index_head]
        value_sel = values_head.reshape(NB, BLOCK, HS)[index_head]
        raw = low_back(jnp.einsum('bpe,bjqe->bpjq', query_blocks, key_sel, precision=HIGH) * SCALE_QK)
        seg_sel = seg_blocks[index_head]
        allow = valid_head[:, None, :, None] & (seg_blocks[:, :, None, None] == seg_sel[:, None, :, :])
        shares = low(masked_softmax(raw, allow, (2, 3)))
        sparse = jnp.einsum('bpjq,bjqe->bpe', shares, value_sel, precision=HIGH)
        query_glob = query_blocks[global_seq]
        raw_glob = low_back(jnp.einsum('gpe,ke->gpk', query_glob, keys_head, precision=HIGH) * SCALE_QK)
        allow_glob = seg_blocks[global_seq][:, :, None] == seg_seq[None, None, :]
        shares_glob = low(masked_softmax(raw_glob, allow_glob, (2,)))
        glob_out = jnp.einsum('gpk,ke->gpe', shares_glob, values_head, precision=HIGH)
        return sparse.at[global_seq].set(glob_out).reshape(SEQ, HS)
    per_head = lax.map(jax.checkpoint(one_head), (query.reshape(SEQ, H, HS).transpose(1, 0, 2), keys.reshape(SEQ, H, HS).transpose(1, 0, 2), values.reshape(SEQ, H, HS).transpose(1, 0, 2), indices.transpose(1, 0, 2), valid.transpose(1, 0, 2)))
    return per_head.transpose(1, 0, 2).reshape(SEQ, H * HS)

def forward(params, residual_in, seg_seq, random_seq, global_seq):
    first_gain, first_bias, joint_weight, output_weight, second_gain, second_bias, up_weight, up_bias, down_weight, down_bias = params
    normed_one = low(normalize(residual_in, first_gain, first_bias))
    projected = jnp.dot(normed_one, joint_weight, precision=HIGH)
    query = low_back(low(projected[:, :D]))
    keys = low_back(low(projected[:, D:2 * D]))
    values = low_back(low(projected[:, 2 * D:]))
    attended = low_back(low(attend(query, keys, values, seg_seq, random_seq, global_seq)))
    middle = residual_in + low_back(jnp.dot(attended, output_weight, precision=HIGH))
    normed_two = low(normalize(middle, second_gain, second_bias))
    up_sum = low_back(jnp.dot(normed_two, up_weight, precision=HIGH) + up_bias)
    hidden = low(jax.nn.gelu(up_sum, approximate=False))
    return middle + jnp.dot(hidden, down_weight, precision=HIGH) + down_bias

def reference(tokens, segment_ids, random_blocks, global_blocks, first_gain, first_bias, joint_weight, output_weight, second_gain, second_bias, up_weight, up_bias, down_weight, down_bias, cotangent):
    params = tuple((item.astype(jnp.float32) for item in (first_gain, first_bias, joint_weight, output_weight, second_gain, second_bias, up_weight, up_bias, down_weight, down_bias)))

    def per_sequence(accum, items):
        token_seq, seg_seq, random_seq, global_seq, cot_seq = items

        def apply(weights, inputs):
            return forward(weights, inputs, seg_seq, random_seq, global_seq)
        result, pull = jax.vjp(apply, params, token_seq.astype(jnp.float32))
        param_grads, input_grad = pull(cot_seq.astype(jnp.float32))
        accum = jax.tree.map(lambda left, right: left + right, accum, param_grads)
        return (accum, (result.astype(jnp.bfloat16), input_grad))
    start = jax.tree.map(jnp.zeros_like, params)
    grads, (layer_out, tokens_grad) = lax.scan(per_sequence, start, (tokens, segment_ids, random_blocks, global_blocks, cotangent))
    return (layer_out, tokens_grad, grads[0], grads[1], grads[2], grads[3], grads[4], grads[5], grads[6], grads[7], grads[8], grads[9])
```

```python
import types

import jax
import jax.numpy as jnp
from jax import lax
from jax.experimental import pallas as pl
from jax.experimental.pallas import tpu as pltpu
from jax.sharding import PartitionSpec as P

BLOCK = 64
LANES = 128
CTX = 8
SEGMENTS = 4
EPS = 1e-05
BIG = 1e30
MESH = pl.DeviceIdType.MESH
BF16 = jnp.bfloat16
F32 = jnp.float32


def dot(a, b):
    return lax.dot_general(a, b, (((1,), (0,)), ((), ())), preferred_element_type=F32)


def dot_nt(a, b):
    return lax.dot_general(a, b, (((1,), (1,)), ((), ())), preferred_element_type=F32)


def dot_tn(a, b):
    return lax.dot_general(a, b, (((0,), (0,)), ((), ())), preferred_element_type=F32)


def loop(lower, upper, body):
    lax.fori_loop(lower, upper, lambda i, carry: (body(i), carry)[1], jnp.int32(0))


def rows_of(index, size):
    return pl.ds(pl.multiple_of(index * size, size), size)


def remote(src, dst, send, recv, device):
    return pltpu.make_async_remote_copy(
        src_ref=src,
        dst_ref=dst,
        send_sem=send,
        recv_sem=recv,
        device_id=device,
        device_id_type=MESH,
    )


class Place:
    def __init__(self, planes):
        self.c = lax.axis_index("ctx")
        self.f = lax.axis_index("fsdp")
        self.planes = planes
        self.parity = lax.rem(self.c, 2)
        self.chip = lax.div(self.c, 2)
        self.partner = 2 * self.chip + 1 - self.parity

    def chip_at(self, g):
        low = lax.rem(lax.rem(self.chip, 2) + lax.rem(g, 2), 2)
        high = lax.rem(lax.div(self.chip, 2) + lax.div(g, 2), 2)
        return low + 2 * high

    def same(self, g):
        return 2 * self.chip_at(g) + self.parity

    def other(self, g):
        return 2 * self.chip_at(g) + 1 - self.parity

    def ctx_at(self, d):
        return lax.rem(self.c + d, CTX)

    def plane_at(self, d):
        return lax.rem(self.f + d, self.planes)


class Gather:
    def __init__(self, at, src, slot, send, recv):
        self.at, self.src, self.slot, self.send, self.recv = at, src, slot, send, recv

    def direct(self, i):
        at = self.at
        to = at.partner if i == 0 else at.same(jnp.int32(i))
        return remote(self.src, self.slot(at.c), self.send.at[i], self.recv.at[at.c], (to, at.f))

    def passed(self, g):
        at = self.at
        block = self.slot(at.same(g))
        return remote(
            block, block, self.send.at[3 + g], self.recv.at[at.same(g)], (at.partner, at.f)
        )

    def start(self):
        for i in range(4):
            self.direct(i).start()

    def wait(self, c):
        at = self.at
        block = self.slot(c)
        remote(block, block, self.send.at[0], self.recv.at[c], (at.partner, at.f)).wait_recv()

    def relay(self, g):
        self.wait(self.at.same(g))
        self.passed(g).start()

    def relays(self):
        loop(1, 4, self.relay)

    def waits(self):
        loop(0, 4, lambda g: self.wait(self.at.other(g)))

    def finish(self):
        for i in range(4):
            self.direct(i).wait_send()
        loop(1, 4, lambda g: self.passed(g).wait_send())


class Exchange:
    def __init__(self, at, src, slot, send, recv):
        self.at, self.src, self.slot, self.send, self.recv = at, src, slot, send, recv

    def copy(self, d):
        at = self.at
        to = at.ctx_at(d)
        return remote(
            self.src(to), self.slot(at.c), self.send.at[d - 1], self.recv.at[at.c], (to, at.f)
        )

    def start(self):
        loop(1, CTX, lambda d: self.copy(d).start())

    def wait(self, d):
        at = self.at
        c = at.ctx_at(d)
        block = self.slot(c)
        remote(block, block, self.send.at[0], self.recv.at[c], (c, at.f)).wait_recv()

    def waits(self):
        loop(1, CTX, self.wait)

    def finish(self):
        loop(1, CTX, lambda d: self.copy(d).wait_send())


class Planes:
    def __init__(self, at, src, slot, send, recv):
        self.at, self.src, self.slot, self.send, self.recv = at, src, slot, send, recv

    def copy(self, d):
        at = self.at
        to = at.plane_at(d)
        return remote(
            self.src(to), self.slot(at.f), self.send.at[d - 1], self.recv.at[at.f], (at.c, to)
        )

    def start(self):
        loop(1, self.at.planes, lambda d: self.copy(d).start())

    def wait(self, d):
        at = self.at
        f = at.plane_at(d)
        block = self.slot(f)
        remote(block, block, self.send.at[0], self.recv.at[f], (at.c, f)).wait_recv()

    def waits(self):
        loop(1, self.at.planes, self.wait)

    def finish(self):
        loop(1, self.at.planes, lambda d: self.copy(d).wait_send())


class Scatter:
    def __init__(self, at, part, pair, far, pair_send, pair_recv, far_send, far_recv):
        self.at, self.part, self.pair, self.far = at, part, pair, far
        self.pair_send, self.pair_recv = pair_send, pair_recv
        self.far_send, self.far_recv = far_send, far_recv

    def to_partner(self, g):
        at = self.at
        return remote(
            self.part.at[at.other(g)],
            self.pair.at[g],
            self.pair_send.at[g],
            self.pair_recv.at[g],
            (at.partner, at.f),
        )

    def to_chip(self, g):
        at = self.at
        return remote(
            self.part.at[at.same(g)],
            self.far.at[g - 1],
            self.far_send.at[g - 1],
            self.far_recv.at[g - 1],
            (at.same(g), at.f),
        )

    def forward(self, g):
        self.to_partner(g).wait_recv()
        own = self.at.same(g)
        both = self.part[own].astype(F32) + self.pair[g].astype(F32)
        self.part[own] = both.astype(BF16)
        self.to_chip(g).start()

    def forwards(self):
        loop(1, 4, self.forward)

    def total(self):
        zero = jnp.int32(0)
        self.to_partner(zero).wait_recv()
        loop(1, 4, lambda g: self.to_chip(g).wait_recv())
        both = self.part[self.at.c].astype(F32) + self.pair[0].astype(F32)
        return (both + self.far[0].astype(F32)) + (
            self.far[1].astype(F32) + self.far[2].astype(F32)
        )

    def finish(self):
        loop(0, 4, lambda g: self.to_partner(g).wait_send())
        loop(1, 4, lambda g: self.to_chip(g).wait_send())


def standard(values):
    centre = jnp.mean(values, axis=-1, keepdims=True)
    offset = values - centre
    spread = jnp.mean(offset * offset, axis=-1, keepdims=True)
    rate = lax.rsqrt(spread + EPS)
    return offset * rate, rate


def standard_grad(e, normal, rate):
    return rate * (
        e - jnp.mean(e, axis=-1, keepdims=True) - normal * jnp.mean(e * normal, axis=-1, keepdims=True)
    )


def layer_kernel(r, planes):
    at = Place(planes)
    me, f = at.c, at.f
    tokens, cotangent, extras, small = r.tokens, r.cotangent, r.extras, r.small
    local, width = tokens.shape
    seq = local * CTX
    part_rows = width // planes
    columns = width // CTX
    ff = planes * r.down.shape[0]
    ff_blocks = ff // LANES // CTX
    shard_blocks = ff // LANES // planes
    k_own = lax.div(f * shard_blocks, CTX)
    has_down = lax.div(me, shard_blocks) == lax.rem(f, CTX // shard_blocks)
    down_place = lax.rem(me, shard_blocks)

    def down_owner(k):
        return lax.div(CTX * k + me, shard_blocks)

    my_rows = rows_of(f, part_rows)
    my_columns = rows_of(me, columns)
    my_tokens = rows_of(me, local)

    stage = []
    for j in range(3):
        stage.append(
            pltpu.make_async_copy(
                r.joint.at[:, pl.ds(pl.multiple_of(width * j + columns * me, LANES), columns)],
                r.wj.at[my_rows, pl.ds(columns * j, columns)],
                r.stage.at[j],
            )
        )
    stage.append(
        pltpu.make_async_copy(
            r.outw.at[:, my_columns], r.wo.at[my_rows, my_columns], r.stage.at[3]
        )
    )
    for k in range(ff_blocks):
        stage.append(
            pltpu.make_async_copy(
                r.up.at[:, pl.ds(pl.multiple_of(CTX * LANES * k + LANES * me, LANES), LANES)],
                r.wu.at[my_rows, pl.ds(LANES * k, LANES)],
                r.stage.at[4 + k],
            )
        )
    down_copy = pltpu.make_async_copy(
        r.down.at[rows_of(down_place, LANES), :],
        r.wd.at[rows_of(k_own, LANES), :],
        r.stage.at[4 + ff_blocks],
    )
    for copy in stage:
        copy.start()

    @pl.when(has_down)
    def _():
        down_copy.start()

    barrier = pltpu.get_barrier_semaphore()
    loop(
        1,
        CTX,
        lambda d: pl.semaphore_signal(
            barrier, inc=1, device_id=(at.ctx_at(d), f), device_id_type=MESH
        ),
    )
    loop(
        1,
        planes,
        lambda d: pl.semaphore_signal(
            barrier, inc=1, device_id=(me, at.plane_at(d)), device_id_type=MESH
        ),
    )
    pl.semaphore_wait(barrier, CTX - 1 + planes - 1)

    tok_gather = Gather(
        at, tokens, lambda c: r.tokg.at[rows_of(c, local)], *r.tok_sem
    )
    cot_gather = Gather(
        at, cotangent, lambda c: r.cotg.at[rows_of(c, local)], *r.cot_sem
    )
    ext_swap = Exchange(
        at,
        lambda c: extras.at[c],
        lambda c: r.extg.at[rows_of(c, local)],
        *r.ext_sem,
    )
    small_planes = Planes(
        at, lambda to: small, lambda p: r.smallg.at[p], *r.small_sem
    )

    def weight_planes(ref, sems, width_ds):
        view = lambda p: ref.at[rows_of(p, part_rows), width_ds]
        return Planes(at, lambda to: view(f), view, *sems)

    wj_planes = weight_planes(r.wj, r.wj_sem, slice(None))
    wo_planes = weight_planes(r.wo, r.wo_sem, my_columns)
    wu_planes = weight_planes(r.wu, r.wu_sem, slice(None))
    wo_block = r.wo.at[:, my_columns]
    wo_gather = Gather(
        at, wo_block, lambda c: r.wo.at[:, rows_of(c, columns)], *r.wog_sem
    )

    def wd_copy(d):
        to = at.plane_at(d)
        block = r.wd.at[rows_of(k_own, LANES), :]
        return remote(block, block, r.wd_sem[0].at[d - 1], r.wd_sem[1].at[k_own], (me, to))

    small_planes.start()
    tok_gather.start()
    ext_swap.start()
    for copy in stage[:3]:
        copy.wait()
    wj_planes.start()
    stage[3].wait()
    wo_planes.start()

    r.tokg[my_tokens, :] = tokens[...]
    r.cotg[my_tokens, :] = cotangent[...]
    r.extg[my_tokens, :] = extras[me]
    r.smallg[f] = small[...]
    small_planes.waits()
    params = r.params
    params[...] = jnp.zeros_like(params)

    def add_params(p):
        params[...] += r.smallg[p].astype(F32)

    loop(0, planes, add_params)
    for k in range(ff_blocks):
        r.ub[0:1, k * LANES : (k + 1) * LANES] = params[5 + k : 6 + k, my_columns]

    def norm_tokens(g):
        @pl.when(g > 0)
        def _():
            tok_gather.relay(g)

        tok_gather.wait(at.other(g))
        rows = rows_of(at.chip_at(g), 2 * local)
        normal, _ = standard(r.tokg[rows, :].astype(F32))
        r.x1[rows, :] = (normal * params[0:1, :] + params[1:2, :]).astype(BF16)

    loop(0, 4, norm_tokens)
    cot_gather.start()
    for copy in stage[4:]:
        copy.wait()
    wu_planes.start()

    @pl.when(has_down)
    def _():
        down_copy.wait()
        loop(1, planes, lambda d: wd_copy(d).start())

    ext_swap.waits()
    wj_planes.waits()

    tile = 2 * local
    lane = lax.broadcasted_iota(jnp.int32, (tile, columns), 1)
    low = lane < columns // 2
    zero_tile = jnp.zeros((tile, columns), BF16)

    def project(i):
        rows = rows_of(i, tile)
        projected = dot(r.x1[rows, :], r.wj[...]).astype(BF16)
        q = projected[:, :columns] * jnp.array(0.125, BF16)
        k = projected[:, columns : 2 * columns]
        v = projected[:, 2 * columns :]
        ext = r.extg[rows, :]
        half = lax.rem(lane, columns // 2)
        token = lax.broadcasted_iota(jnp.int32, (tile, columns), 0) + i * tile
        hot = jnp.where(half == lax.div(token, BLOCK), 1.0, 0.0)
        blocks = seq // BLOCK
        k_ext = jnp.where(
            half < blocks,
            hot,
            jnp.where(half < blocks + SEGMENTS, (1.0 - ext.astype(F32)) * -BIG, 0.0),
        ).astype(BF16)
        r.q[rows, :] = q
        r.qa[0, rows, :] = jnp.where(low, q, ext)
        r.qa[1, rows, :] = jnp.where(low, ext, q)
        r.ka[0, rows, :] = jnp.where(low, k, k_ext)
        r.ka[1, rows, :] = jnp.where(low, k_ext, k)
        r.km[0, rows, :] = jnp.where(low, k, zero_tile)
        r.km[1, rows, :] = jnp.where(low, zero_tile, k)
        r.vm[0, rows, :] = jnp.where(low, v, zero_tile)
        r.vm[1, rows, :] = jnp.where(low, zero_tile, v)

    loop(0, seq // tile, project)
    wo_planes.waits()
    wo_gather.start()

    def attend(i):
        rows = rows_of(i, tile)
        out = None
        for h in range(2):
            scores = dot_nt(r.qa[h, rows, :], r.ka[h])
            weights = jnp.exp(scores - jnp.max(scores, axis=1, keepdims=True))
            shares = (weights / jnp.sum(weights, axis=1, keepdims=True)).astype(BF16)
            r.probs[h, rows, :] = shares
            term = dot(shares, r.vm[h])
            out = term if out is None else out + term
        r.att[rows, :] = out.astype(BF16)

    loop(0, seq // tile, attend)

    att_swap = Exchange(
        at,
        lambda c: r.att.at[rows_of(c, local)],
        lambda c: r.attx.at[c],
        *r.att_sem,
    )
    att_swap.start()
    cot_gather.relays()
    wo_gather.relays()
    r.attx[me] = r.att[my_tokens, :]
    att_swap.waits()
    for c in range(CTX):
        r.attg[my_tokens, c * columns : (c + 1) * columns] = r.attx[c]
    wo_gather.waits()
    middle = tokens[...].astype(F32) + dot(r.attg[my_tokens, :], r.wo[...])
    normal, rate = standard(middle)
    r.middle[...] = middle
    r.n2[...] = normal
    r.rate2[...] = jnp.broadcast_to(rate, r.rate2.shape)
    r.x2[my_tokens, :] = (normal * params[2:3, :] + params[3:4, :]).astype(BF16)
    x2_view = lambda c: r.x2.at[rows_of(c, local)]
    x2_gather = Gather(at, x2_view(me), x2_view, *r.x2_sem)
    x2_gather.start()
    attg_view = lambda c: r.attg.at[rows_of(c, local)]
    att_gather = Gather(at, attg_view(me), attg_view, *r.attg_sem)
    wu_planes.waits()

    def wd_wait(k):
        @pl.when(down_owner(k) != f)
        def _():
            block = r.wd.at[rows_of(k, LANES), :]
            remote(block, block, r.wd_sem[0].at[0], r.wd_sem[1].at[k], (me, down_owner(k))).wait_recv()

    loop(0, ff_blocks, wd_wait)

    back = Scatter(at, *r.back)
    feed = Scatter(at, *r.feed)
    first = Scatter(at, *r.first)
    r.ubg[...] = jnp.zeros_like(r.ubg)

    def feed_forward(g):
        @pl.when(g > 0)
        def _():
            x2_gather.relay(g)

        x2_gather.wait(at.other(g))
        cot_gather.wait(at.other(g))
        chip = at.chip_at(g)
        rows = rows_of(chip, tile)
        up_sum = dot(r.x2[rows, :], r.wu[...]) + r.ub[...]
        share = 0.5 * (1.0 + lax.erf(up_sum * 0.7071067811865476))
        hidden = (up_sum * share).astype(BF16)
        slope = share + up_sum * jnp.exp(-0.5 * up_sum * up_sum) * 0.3989422804014327
        r.hidden[rows, :] = hidden
        up_grad = (dot_nt(r.cotg[rows, :], r.wd[...]) * slope).astype(BF16)
        r.upg[rows, :] = up_grad
        r.ubg[...] += jnp.sum(up_grad.astype(F32), axis=0, keepdims=True)
        back_part = dot_nt(up_grad, r.wu[...]).astype(BF16)
        r.back[0][2 * chip] = back_part[:local]
        r.back[0][2 * chip + 1] = back_part[local:]
        back.to_partner(g).start()
        feed_part = dot(hidden, r.wd[...]).astype(BF16)
        r.feed[0][2 * chip] = feed_part[:local]
        r.feed[0][2 * chip + 1] = feed_part[local:]

    loop(0, 4, feed_forward)
    back.forwards()
    att_gather.start()

    def down_grad(k):
        r.dwd[k] = dot_tn(r.hidden[:, rows_of(k, LANES)], r.cotg[...]).astype(BF16)

    def dwd_copy(k):
        return remote(
            r.dwd.at[k], r.rd.at[f], r.dwd_sem[0].at[k], r.dwd_sem[1].at[f], (me, down_owner(k))
        )

    def dwd_send(k):
        down_grad(k)

        @pl.when(down_owner(k) != f)
        def _():
            dwd_copy(k).start()

    loop(0, ff_blocks, dwd_send)
    rows_tile = min(tile, width)

    def weight_grad(out, left, right):
        def body(i):
            out[rows_of(i, rows_tile), :] = dot_tn(
                left[:, rows_of(i, rows_tile)], right[...]
            ).astype(BF16)

        loop(0, width // rows_tile, body)

    def grad_planes(grad, taken, sems):
        return Planes(
            at,
            lambda to: grad.at[rows_of(to, part_rows), :],
            lambda p: taken.at[p],
            *sems,
        )

    du_planes = grad_planes(r.du, r.ru, r.du_sem)
    do_planes = grad_planes(r.do, r.ro, r.do_sem)
    dj_planes = grad_planes(r.dj, r.rj, r.dj_sem)
    weight_grad(r.du, r.x2, r.upg)
    du_planes.start()

    normed_two_grad = back.total()
    normal = r.n2[...]
    cot_own = cotangent[...].astype(F32)
    sums = r.sums
    sums[...] = jnp.zeros_like(sums)
    sums[2:3, :] = jnp.sum(normed_two_grad * normal, axis=0, keepdims=True)
    sums[3:4, :] = jnp.sum(normed_two_grad, axis=0, keepdims=True)
    sums[4:5, :] = jnp.sum(cot_own, axis=0, keepdims=True)
    for k in range(ff_blocks):
        sums[5 + k : 6 + k, my_columns] = r.ubg[0:1, k * LANES : (k + 1) * LANES]
    middle_grad = cot_own + standard_grad(
        normed_two_grad * params[2:3, :], normal, r.rate2[:, 0:1]
    )
    r.tokens_grad[...] = middle_grad
    branch = middle_grad.astype(BF16)
    attended_grad = dot_nt(branch, r.wo[...]).astype(BF16)
    for c in range(CTX):
        r.dat[c] = attended_grad[:, c * columns : (c + 1) * columns]
        r.brs[c] = branch[:, c * columns : (c + 1) * columns]

    def token_swap(src, dst, sems):
        return Exchange(at, lambda c: src.at[c], lambda c: dst.at[rows_of(c, local)], *sems)

    dat_swap = token_swap(r.dat, r.datg, r.dat_sem)
    br_swap = token_swap(r.brs, r.brg, r.br_sem)
    dat_swap.start()
    br_swap.start()
    r.datg[my_tokens, :] = r.dat[me]
    r.brg[my_tokens, :] = r.brs[me]
    att_gather.relays()
    loop(0, 4, lambda g: feed.to_partner(g).start())
    r.dk[...] = jnp.zeros_like(r.dk)
    r.dv[...] = jnp.zeros_like(r.dv)
    dat_swap.waits()

    def attend_back(i):
        rows = rows_of(i, tile)
        grad = r.datg[rows, :]
        both = grad.astype(F32) * r.att[rows, :].astype(F32)
        q = r.q[rows, :]
        query_grad = None
        for h in range(2):
            keep = low if h == 0 else ~low
            delta = jnp.sum(jnp.where(keep, both, 0.0), axis=1, keepdims=True)
            probs = r.probs[h, rows, :]
            prob_grad = dot_nt(grad, r.vm[h])
            score_grad = (probs.astype(F32) * (prob_grad - delta)).astype(BF16)
            term = dot(score_grad, r.km[h])
            query_grad = term if query_grad is None else query_grad + term
            r.dk[...] += dot_tn(score_grad, jnp.where(keep, q, zero_tile))
            r.dv[...] += dot_tn(probs, jnp.where(keep, grad, zero_tile))
        r.pg[rows, :columns] = (query_grad * 0.125).astype(BF16)

    loop(0, seq // tile, attend_back)
    r.pg[:, columns : 2 * columns] = r.dk[...].astype(BF16)
    r.pg[:, 2 * columns :] = r.dv[...].astype(BF16)
    weight_grad(r.dj, r.x1, r.pg)
    dj_planes.start()

    def first_part(g):
        chip = at.chip_at(g)
        part = dot_nt(r.pg[rows_of(chip, tile), :], r.wj[...]).astype(BF16)
        r.first[0][2 * chip] = part[:local]
        r.first[0][2 * chip + 1] = part[local:]
        first.to_partner(g).start()

    loop(0, 4, first_part)
    feed.forwards()
    first.forwards()
    att_gather.waits()
    br_swap.waits()
    weight_grad(r.do, r.attg, r.brg)
    do_planes.start()

    class Owned:
        def __init__(self, number, copies, grad, taken, acc, total, out, sems):
            self.copies, self.grad, self.taken, self.acc, self.total = copies, grad, taken, acc, total
            self.gather = Gather(at, total, lambda c: out.at[c], *sems)
            self.own = pltpu.make_async_copy(total, out.at[me], r.own.at[number])

        def reduce(self):
            self.copies.waits()
            self.acc[...] = self.grad[my_rows, :].astype(F32)

            def add(d):
                self.acc[...] += self.taken[at.plane_at(d)].astype(F32)

            loop(1, planes, add)
            self.total[...] = self.acc[...].astype(BF16)
            self.gather.start()
            self.own.start()

    owned_u = Owned(0, du_planes, r.du, r.ru, r.au, r.tu, r.gu, r.gu_sem)
    owned_o = Owned(1, do_planes, r.do, r.ro, r.ao, r.to, r.go, r.go_sem)
    owned_j = Owned(2, dj_planes, r.dj, r.rj, r.aj, r.tj, r.gj, r.gj_sem)

    full_shard = shard_blocks == CTX
    gd_gather = Gather(
        at, r.td, lambda c: r.gd.at[c], *r.gd_sem
    )
    gd_own = pltpu.make_async_copy(r.td, r.gd.at[down_place], r.own.at[3])

    def gd_copy(d):
        return remote(
            r.td, r.gd.at[down_place], r.gd_sem[0].at[d - 1], r.gd_sem[1].at[down_place], (at.ctx_at(d), f)
        )

    @pl.when(has_down)
    def _():
        def take(d):
            p = at.plane_at(d)
            block = r.rd.at[p]
            remote(block, block, r.dwd_sem[0].at[0], r.dwd_sem[1].at[p], (me, p)).wait_recv()

        loop(1, planes, take)
        total = r.n2
        total[...] = r.dwd[k_own].astype(F32)

        def add(d):
            total[...] += r.rd[at.plane_at(d)].astype(F32)

        loop(1, planes, add)
        r.td[...] = total[...].astype(BF16)
        gd_own.start()
        if not full_shard:
            loop(1, CTX, lambda d: gd_copy(d).start())

    if full_shard:
        gd_gather.start()
    owned_u.reduce()

    feed_total = feed.total()
    r.layer_out[...] = (r.middle[...] + feed_total + params[4:5, :]).astype(BF16)
    owned_j.reduce()

    normed_one_grad = first.total()
    normal, rate = standard(tokens[...].astype(F32))
    sums[0:1, :] = jnp.sum(normed_one_grad * normal, axis=0, keepdims=True)
    sums[1:2, :] = jnp.sum(normed_one_grad, axis=0, keepdims=True)
    r.tokens_grad[...] += standard_grad(
        normed_one_grad * params[0:1, :], normal, rate
    )
    r.sum_s[...] = sums[...].astype(BF16)
    sum_swap = Exchange(
        at, lambda c: r.sum_s, lambda c: r.sum_c.at[c], *r.sumc_sem
    )
    sum_swap.start()
    owned_o.reduce()
    if full_shard:
        gd_gather.relays()
    owned_u.gather.relays()
    sum_swap.waits()

    def add_ctx(d):
        sums[...] += r.sum_c[at.ctx_at(d)].astype(F32)

    loop(1, CTX, add_ctx)
    r.sum_p[...] = sums[...].astype(BF16)
    sum_planes = Planes(
        at, lambda to: r.sum_p, lambda p: r.sum_z.at[p], *r.sumz_sem
    )
    sum_planes.start()
    owned_j.gather.relays()
    owned_o.gather.relays()
    sum_planes.waits()

    def add_planes(d):
        sums[...] += r.sum_z[at.plane_at(d)].astype(F32)

    loop(1, planes, add_planes)
    r.totals[...] = sums[...]

    for each in (owned_u, owned_o, owned_j):
        each.gather.waits()
        each.own.wait()
    if full_shard:
        gd_own.wait()
        gd_gather.waits()
        gd_gather.finish()
    else:

        @pl.when(has_down)
        def _():
            gd_own.wait()
            loop(1, CTX, lambda d: gd_copy(d).wait_send())

        def gd_take(b):
            @pl.when(me != lax.rem(f * shard_blocks + b, CTX))
            def _():
                block = r.gd.at[b]
                remote(
                    block, block, r.gd_sem[0].at[0], r.gd_sem[1].at[b], (at.ctx_at(jnp.int32(1)), f)
                ).wait_recv()

        loop(0, shard_blocks, gd_take)

    @pl.when(has_down)
    def _():
        loop(1, planes, lambda d: wd_copy(d).wait_send())

    def dwd_sent(k):
        @pl.when(down_owner(k) != f)
        def _():
            dwd_copy(k).wait_send()

    loop(0, ff_blocks, dwd_sent)
    for each in (
        tok_gather, cot_gather, wo_gather, x2_gather, att_gather, owned_u.gather, owned_o.gather,
        owned_j.gather, ext_swap, att_swap, dat_swap, br_swap, sum_swap, small_planes, wj_planes,
        wo_planes, wu_planes, du_planes, do_planes, dj_planes, sum_planes, back, feed, first,
    ):
        each.finish()


def shards(
    tokens,
    segment_ids,
    random_blocks,
    global_blocks,
    first_gain,
    first_bias,
    joint_weight,
    output_weight,
    second_gain,
    second_bias,
    up_weight,
    up_bias,
    down_weight,
    down_bias,
    cotangent,
):
    local, width = tokens.shape[1:]
    ctx, planes = lax.axis_size("ctx"), lax.axis_size("fsdp")
    plane = lax.axis_index("fsdp")
    heads = random_blocks.shape[2]
    seq = local * ctx
    blocks = seq // BLOCK
    part_rows = width // planes
    columns = width // ctx
    ff_shard = up_bias.shape[0]
    ff = ff_shard * planes
    ff_blocks = ff // LANES // ctx
    shard_blocks = ff_shard // LANES
    ff_part = ff // ctx
    assert ctx == CTX and columns == LANES and heads == 2 * ctx and blocks + SEGMENTS <= 64
    assert CTX % shard_blocks == 0 and ff // width == ff_blocks

    local_blocks = local // BLOCK
    block_ids = lax.axis_index("ctx") * local_blocks + jnp.arange(local_blocks, dtype=jnp.int32)
    key_ids = jnp.arange(blocks, dtype=jnp.int32)
    window = jnp.abs(key_ids[None, :] - block_ids[:, None]) <= 1
    chosen = jnp.any(key_ids[:, None] == global_blocks[0][None, :], axis=1)
    whole = jnp.any(block_ids[:, None] == global_blocks[0][None, :], axis=1)
    drawn = jnp.any(random_blocks[0][:, :, :, None] == key_ids, axis=2)
    counted = drawn | (window | chosen[None, :] | whole[:, None])[:, None, :]
    code = jnp.where(counted, 0.0, -BIG).astype(BF16)
    code = jnp.broadcast_to(
        code.transpose(1, 0, 2)[:, :, None, :], (heads, local_blocks, BLOCK, blocks)
    ).reshape(heads, local, blocks)
    segment = (
        segment_ids[0][:, None] == jnp.arange(SEGMENTS, dtype=jnp.int32)[None, :]
    ).astype(BF16)
    segment = jnp.broadcast_to(segment[None], (heads, local, SEGMENTS))
    rest = jnp.zeros((heads, local, 64 - blocks - SEGMENTS), BF16)
    extras = jnp.concatenate([code, segment, rest], axis=2).reshape(ctx, 2, local, 64)
    extras = jnp.concatenate([extras[:, 1], extras[:, 0]], axis=2)

    vectors = jnp.stack([first_gain, first_bias, second_gain, second_bias, down_bias])
    small = jnp.zeros((16, width), BF16)
    small = lax.dynamic_update_slice(small, vectors, (0, plane * part_rows))
    flat = lax.dynamic_update_slice(jnp.zeros((ff,), BF16), up_bias, (plane * ff_shard,))
    small = lax.dynamic_update_slice(small, flat.reshape(ff_blocks, width), (5, 0))

    vmem, hbm = pl.BlockSpec(memory_space=pltpu.VMEM), pl.BlockSpec(memory_space=pl.ANY)
    inputs = dict(
        tokens=(tokens[0], vmem),
        cotangent=(cotangent[0], vmem),
        extras=(extras, vmem),
        small=(small, vmem),
        joint=(joint_weight, hbm),
        outw=(output_weight, hbm),
        up=(up_weight, hbm),
        down=(down_weight, hbm),
    )
    outputs = dict(
        layer_out=((local, width), BF16, vmem),
        tokens_grad=((local, width), F32, vmem),
        totals=((16, width), F32, vmem),
        gj=((ctx, part_rows, 3 * columns), BF16, hbm),
        go=((ctx, part_rows, columns), BF16, hbm),
        gu=((ctx, part_rows, ff_part), BF16, hbm),
        gd=((shard_blocks, LANES, width), BF16, hbm),
    )
    dma = lambda n: pltpu.SemaphoreType.DMA((n,))
    v16 = lambda *shape: pltpu.VMEM(shape, BF16)
    v32 = lambda *shape: pltpu.VMEM(shape, F32)
    others = max(planes - 1, 1)
    scatter = (
        v16(ctx, local, width), v16(4, local, width), v16(3, local, width),
        dma(4), dma(4), dma(3), dma(3),
    )
    gather, swap, plane_sems = (dma(7), dma(ctx)), (dma(ctx - 1), dma(ctx)), (dma(others), dma(planes))
    scratch = dict(
        wj=v16(width, 3 * columns), wo=v16(width, width), wu=v16(width, ff_part),
        wd=v16(ff_part, width), tokg=v16(seq, width), cotg=v16(seq, width),
        x1=v16(seq, width), x2=v16(seq, width), attg=v16(seq, width),
        extg=v16(seq, columns), smallg=v16(planes, 16, width), params=v32(16, width),
        ub=v32(1, ff_part), ubg=v32(1, ff_part), q=v16(seq, columns),
        qa=v16(2, seq, columns), ka=v16(2, seq, columns), km=v16(2, seq, columns),
        vm=v16(2, seq, columns), probs=v16(2, seq, seq), att=v16(seq, columns),
        attx=v16(ctx, local, columns), middle=v32(local, width), n2=v32(local, width),
        rate2=v32(local, LANES), hidden=v16(seq, ff_part),
        upg=v16(seq, ff_part), dat=v16(ctx, local, columns), brs=v16(ctx, local, columns),
        datg=v16(seq, columns), brg=v16(seq, columns), dk=v32(seq, columns),
        dv=v32(seq, columns), pg=v16(seq, 3 * columns), sums=v32(16, width),
        sum_s=v16(16, width), sum_p=v16(16, width), sum_c=v16(ctx, 16, width),
        sum_z=v16(planes, 16, width),
        dj=v16(width, 3 * columns), do=v16(width, columns), du=v16(width, ff_part),
        dwd=v16(ff_blocks, LANES, width),
        rj=v16(planes, part_rows, 3 * columns), ro=v16(planes, part_rows, columns),
        ru=v16(planes, part_rows, ff_part), rd=v16(planes, LANES, width),
        aj=v32(part_rows, 3 * columns), ao=v32(part_rows, columns), au=v32(part_rows, ff_part),
        tj=v16(part_rows, 3 * columns), to=v16(part_rows, columns),
        tu=v16(part_rows, ff_part), td=v16(LANES, width),
        stage=dma(5 + ff_blocks), own=dma(4), wd_sem=(dma(others), dma(ff_blocks)),
        dwd_sem=(dma(ff_blocks), dma(planes)), back=scatter, feed=scatter, first=scatter,
        tok_sem=gather, cot_sem=gather, wog_sem=gather, x2_sem=gather, attg_sem=gather,
        gj_sem=gather, go_sem=gather, gu_sem=gather, gd_sem=gather,
        ext_sem=swap, att_sem=swap, dat_sem=swap, br_sem=swap, sumc_sem=swap,
        small_sem=plane_sems, wj_sem=plane_sems, wo_sem=plane_sems, wu_sem=plane_sems,
        dj_sem=plane_sems, do_sem=plane_sems, du_sem=plane_sems, sumz_sem=plane_sems,
    )
    shapes, scratch_tree = jax.tree.flatten(scratch)
    ins, outs = len(inputs), len(outputs)

    def kernel(*refs):
        held = dict(zip([*inputs, *outputs], refs, strict=False))
        held |= jax.tree.unflatten(scratch_tree, refs[ins + outs :])
        layer_kernel(types.SimpleNamespace(**held), planes)

    layer_out, tokens_grad, totals, gj, go, gu, gd = pl.pallas_call(
        kernel,
        out_shape=[jax.ShapeDtypeStruct(shape, dtype) for shape, dtype, _ in outputs.values()],
        in_specs=[spec for _, spec in inputs.values()],
        out_specs=[spec for *_, spec in outputs.values()],
        scratch_shapes=shapes,
        compiler_params=pltpu.CompilerParams(
            collective_id=0, has_side_effects=True, vmem_limit_bytes=60 * 1024 * 1024
        ),
    )(*(value for value, _ in inputs.values()))

    def spread(blocks_of, groups):
        parts = blocks_of.astype(F32).reshape(ctx, part_rows, groups, columns)
        return parts.transpose(1, 2, 0, 3).reshape(part_rows, groups * ctx * columns)

    mine = lax.dynamic_slice(totals[:5], (0, plane * part_rows), (5, part_rows))
    bias = lax.dynamic_slice(totals[5 : 5 + ff_blocks].reshape(ff), (plane * ff_shard,), (ff_shard,))
    return (
        layer_out[None],
        tokens_grad[None],
        mine[0],
        mine[1],
        spread(gj, 3),
        spread(go, 1),
        mine[2],
        mine[3],
        spread(gu, ff_blocks),
        bias,
        gd.astype(F32).reshape(ff_shard, width),
        mine[4],
    )


def solution(mesh):
    in_specs = (
        P("fsdp", "ctx", None),
        P("fsdp", "ctx"),
        P("fsdp", "ctx", None, None),
        P("fsdp", None),
        P("fsdp"),
        P("fsdp"),
        P("fsdp", None),
        P("fsdp", None),
        P("fsdp"),
        P("fsdp"),
        P("fsdp", None),
        P("fsdp"),
        P("fsdp", None),
        P("fsdp"),
        P("fsdp", "ctx", None),
    )
    out_specs = (
        P("fsdp", "ctx", None),
        P("fsdp", "ctx", None),
        P("fsdp"),
        P("fsdp"),
        P("fsdp", None),
        P("fsdp", None),
        P("fsdp"),
        P("fsdp"),
        P("fsdp", None),
        P("fsdp"),
        P("fsdp", None),
        P("fsdp"),
    )
    return jax.shard_map(shards, mesh=mesh, in_specs=in_specs, out_specs=out_specs, check_vma=False)
```

```python
import types

import jax
import jax.numpy as jnp
from jax import lax
from jax.experimental import pallas as pl
from jax.experimental.pallas import tpu as pltpu
from jax.sharding import PartitionSpec as P

BLOCK = 64
LANES = 128
CTX = 8
SEGMENTS = 4
EPS = 1e-05
BIG = 1e30
MESH = pl.DeviceIdType.MESH
BF16 = jnp.bfloat16
F32 = jnp.float32


def dot(a, b):
    return lax.dot_general(a, b, (((1,), (0,)), ((), ())), preferred_element_type=F32)


def dot_nt(a, b):
    return lax.dot_general(a, b, (((1,), (1,)), ((), ())), preferred_element_type=F32)


def dot_tn(a, b):
    return lax.dot_general(a, b, (((0,), (0,)), ((), ())), preferred_element_type=F32)


def loop(lower, upper, body):
    lax.fori_loop(lower, upper, lambda i, carry: (body(i), carry)[1], jnp.int32(0))


def rows_of(index, size):
    return pl.ds(pl.multiple_of(index * size, size), size)


def remote(src, dst, send, recv, device):
    return pltpu.make_async_remote_copy(
        src_ref=src,
        dst_ref=dst,
        send_sem=send,
        recv_sem=recv,
        device_id=device,
        device_id_type=MESH,
    )


class Place:
    def __init__(self, planes):
        self.c = lax.axis_index("ctx")
        self.f = lax.axis_index("fsdp")
        self.planes = planes
        self.parity = lax.rem(self.c, 2)
        self.chip = lax.div(self.c, 2)
        self.partner = 2 * self.chip + 1 - self.parity

    def chip_at(self, g):
        low = lax.rem(lax.rem(self.chip, 2) + lax.rem(g, 2), 2)
        high = lax.rem(lax.div(self.chip, 2) + lax.div(g, 2), 2)
        return low + 2 * high

    def same(self, g):
        return 2 * self.chip_at(g) + self.parity

    def other(self, g):
        return 2 * self.chip_at(g) + 1 - self.parity

    def ctx_at(self, d):
        return lax.rem(self.c + d, CTX)

    def plane_at(self, d):
        return lax.rem(self.f + d, self.planes)


class Gather:
    def __init__(self, at, src, slot, send, recv):
        self.at, self.src, self.slot, self.send, self.recv = at, src, slot, send, recv

    def direct(self, i):
        at = self.at
        to = at.partner if i == 0 else at.same(jnp.int32(i))
        return remote(self.src, self.slot(at.c), self.send.at[i], self.recv.at[at.c], (to, at.f))

    def passed(self, g):
        at = self.at
        block = self.slot(at.same(g))
        return remote(
            block, block, self.send.at[3 + g], self.recv.at[at.same(g)], (at.partner, at.f)
        )

    def start(self):
        for i in range(4):
            self.direct(i).start()

    def wait(self, c):
        at = self.at
        block = self.slot(c)
        remote(block, block, self.send.at[0], self.recv.at[c], (at.partner, at.f)).wait_recv()

    def relay(self, g):
        self.wait(self.at.same(g))
        self.passed(g).start()

    def relays(self):
        loop(1, 4, self.relay)

    def waits(self):
        loop(0, 4, lambda g: self.wait(self.at.other(g)))

    def finish(self):
        for i in range(4):
            self.direct(i).wait_send()
        loop(1, 4, lambda g: self.passed(g).wait_send())


class Exchange:
    def __init__(self, at, src, slot, send, recv):
        self.at, self.src, self.slot, self.send, self.recv = at, src, slot, send, recv

    def copy(self, d):
        at = self.at
        to = at.ctx_at(d)
        return remote(
            self.src(to), self.slot(at.c), self.send.at[d - 1], self.recv.at[at.c], (to, at.f)
        )

    def start(self):
        loop(1, CTX, lambda d: self.copy(d).start())

    def wait(self, d):
        at = self.at
        c = at.ctx_at(d)
        block = self.slot(c)
        remote(block, block, self.send.at[0], self.recv.at[c], (c, at.f)).wait_recv()

    def waits(self):
        loop(1, CTX, self.wait)

    def finish(self):
        loop(1, CTX, lambda d: self.copy(d).wait_send())


class Planes:
    def __init__(self, at, src, slot, send, recv):
        self.at, self.src, self.slot, self.send, self.recv = at, src, slot, send, recv

    def copy(self, d):
        at = self.at
        to = at.plane_at(d)
        return remote(
            self.src(to), self.slot(at.f), self.send.at[d - 1], self.recv.at[at.f], (at.c, to)
        )

    def start(self):
        loop(1, self.at.planes, lambda d: self.copy(d).start())

    def wait(self, d):
        at = self.at
        f = at.plane_at(d)
        block = self.slot(f)
        remote(block, block, self.send.at[0], self.recv.at[f], (at.c, f)).wait_recv()

    def waits(self):
        loop(1, self.at.planes, self.wait)

    def finish(self):
        loop(1, self.at.planes, lambda d: self.copy(d).wait_send())


class Scatter:
    def __init__(self, at, part, pair, far, pair_send, pair_recv, far_send, far_recv):
        self.at, self.part, self.pair, self.far = at, part, pair, far
        self.pair_send, self.pair_recv = pair_send, pair_recv
        self.far_send, self.far_recv = far_send, far_recv

    def to_partner(self, g):
        at = self.at
        return remote(
            self.part.at[at.other(g)],
            self.pair.at[g],
            self.pair_send.at[g],
            self.pair_recv.at[g],
            (at.partner, at.f),
        )

    def to_chip(self, g):
        at = self.at
        return remote(
            self.part.at[at.same(g)],
            self.far.at[g - 1],
            self.far_send.at[g - 1],
            self.far_recv.at[g - 1],
            (at.same(g), at.f),
        )

    def forward(self, g):
        self.to_partner(g).wait_recv()
        own = self.at.same(g)
        both = self.part[own].astype(F32) + self.pair[g].astype(F32)
        self.part[own] = both.astype(BF16)
        self.to_chip(g).start()

    def forwards(self):
        loop(1, 4, self.forward)

    def total(self):
        zero = jnp.int32(0)
        self.to_partner(zero).wait_recv()
        loop(1, 4, lambda g: self.to_chip(g).wait_recv())
        both = self.part[self.at.c].astype(F32) + self.pair[0].astype(F32)
        return (both + self.far[0].astype(F32)) + (
            self.far[1].astype(F32) + self.far[2].astype(F32)
        )

    def finish(self):
        loop(0, 4, lambda g: self.to_partner(g).wait_send())
        loop(1, 4, lambda g: self.to_chip(g).wait_send())


def standard(values):
    centre = jnp.mean(values, axis=-1, keepdims=True)
    offset = values - centre
    spread = jnp.mean(offset * offset, axis=-1, keepdims=True)
    rate = lax.rsqrt(spread + EPS)
    return offset * rate, rate


def standard_grad(e, normal, rate):
    return rate * (
        e - jnp.mean(e, axis=-1, keepdims=True) - normal * jnp.mean(e * normal, axis=-1, keepdims=True)
    )


def write_extras(r, at, seq):
    local = r.segments.shape[1]
    blocks, local_blocks = seq // BLOCK, local // BLOCK
    heads = r.random.shape[1]
    half = LANES // 2
    key = lax.rem(lax.broadcasted_iota(jnp.int32, (heads, LANES), 1), half)
    lower = lax.broadcasted_iota(jnp.int32, (1, LANES), 1) < half
    place = lax.rem(lax.broadcasted_iota(jnp.int32, (LANES, local), 0), half)
    hot = jnp.where(r.segments[...] == place - blocks, 1.0, 0.0).T
    hot = jnp.where(key[0:1] >= blocks + SEGMENTS, 0.0, hot)
    pair = r.globals[...]
    for b in range(local_blocks):
        block = at.c * local_blocks + b
        drawn = r.random[b]
        counted = jnp.abs(key - block) <= 1
        for j in range(drawn.shape[1]):
            counted = counted | (key == drawn[:, j : j + 1])
        for j in range(pair.shape[1]):
            chosen = pair[:, j : j + 1]
            counted = counted | (key == chosen) | (chosen == block)
        code = jnp.where(counted | (key >= blocks), 0.0, -BIG)
        rows = slice(b * BLOCK, (b + 1) * BLOCK)
        for d in range(heads // 2):
            both = jnp.where(lower, code[2 * d + 1 : 2 * d + 2], code[2 * d : 2 * d + 1])
            r.extras[d, rows, :] = (both + hot[rows]).astype(BF16)


def layer_kernel(r, planes):
    at = Place(planes)
    me, f = at.c, at.f
    tokens, cotangent = r.tokens, r.cotangent
    local, width = tokens.shape
    seq = local * CTX
    part_rows = width // planes
    columns = width // CTX
    ff = planes * r.down.shape[0]
    ff_blocks = ff // LANES // CTX
    shard_blocks = ff // LANES // planes
    k_own = lax.div(f * shard_blocks, CTX)
    has_down = lax.div(me, shard_blocks) == lax.rem(f, CTX // shard_blocks)
    down_place = lax.rem(me, shard_blocks)

    def down_owner(k):
        return lax.div(CTX * k + me, shard_blocks)

    my_rows = rows_of(f, part_rows)
    my_columns = rows_of(me, columns)
    my_tokens = rows_of(me, local)

    stage = []
    for j in range(3):
        stage.append(
            pltpu.make_async_copy(
                r.joint.at[:, pl.ds(pl.multiple_of(width * j + columns * me, LANES), columns)],
                r.wj.at[my_rows, pl.ds(columns * j, columns)],
                r.stage.at[j],
            )
        )
    stage.append(
        pltpu.make_async_copy(
            r.outw.at[:, my_columns], r.wo.at[my_rows, my_columns], r.stage.at[3]
        )
    )
    for k in range(ff_blocks):
        stage.append(
            pltpu.make_async_copy(
                r.up.at[:, pl.ds(pl.multiple_of(CTX * LANES * k + LANES * me, LANES), LANES)],
                r.wu.at[my_rows, pl.ds(LANES * k, LANES)],
                r.stage.at[4 + k],
            )
        )
    down_copy = pltpu.make_async_copy(
        r.down.at[rows_of(down_place, LANES), :],
        r.wd.at[rows_of(k_own, LANES), :],
        r.stage.at[4 + ff_blocks],
    )
    for copy in stage:
        copy.start()

    @pl.when(has_down)
    def _():
        down_copy.start()

    small, wide, shard = r.small, r.sums, ff // planes
    wide[...] = jnp.zeros_like(wide)
    for i, vector in enumerate((r.gain_one, r.bias_one, r.gain_two, r.bias_two, r.bias_down)):
        wide[i : i + 1, 0:part_rows] = vector[...].astype(F32).reshape(1, part_rows)
    wide[8:9, 0:shard] = r.bias_up[...].astype(F32).reshape(1, shard)
    vectors = pltpu.roll(wide[0:8, :], f * part_rows, axis=1)
    bias_row = lax.div(f * shard, width)
    bias = pltpu.roll(wide[8:16, :], lax.rem(f * shard, width), axis=1)[0:1]
    row = lax.broadcasted_iota(jnp.int32, (16, width), 0)
    small[...] = jnp.where(
        row == 5 + bias_row, bias, jnp.concatenate([vectors, jnp.zeros_like(vectors)], axis=0)
    ).astype(BF16)

    barrier = pltpu.get_barrier_semaphore()
    loop(
        1,
        CTX,
        lambda d: pl.semaphore_signal(
            barrier, inc=1, device_id=(at.ctx_at(d), f), device_id_type=MESH
        ),
    )
    loop(
        1,
        planes,
        lambda d: pl.semaphore_signal(
            barrier, inc=1, device_id=(me, at.plane_at(d)), device_id_type=MESH
        ),
    )
    pl.semaphore_wait(barrier, CTX - 1 + planes - 1)

    tok_gather = Gather(
        at, tokens, lambda c: r.tokg.at[rows_of(c, local)], *r.tok_sem
    )
    cot_gather = Gather(
        at, cotangent, lambda c: r.cotg.at[rows_of(c, local)], *r.cot_sem
    )
    ext_swap = Exchange(
        at,
        lambda c: r.extras.at[c],
        lambda c: r.extg.at[rows_of(c, local)],
        *r.ext_sem,
    )
    small_planes = Planes(
        at, lambda to: small, lambda p: r.smallg.at[p], *r.small_sem
    )

    def weight_planes(ref, sems, width_ds):
        view = lambda p: ref.at[rows_of(p, part_rows), width_ds]
        return Planes(at, lambda to: view(f), view, *sems)

    wj_planes = weight_planes(r.wj, r.wj_sem, slice(None))
    wo_planes = weight_planes(r.wo, r.wo_sem, my_columns)
    wu_planes = weight_planes(r.wu, r.wu_sem, slice(None))
    wo_block = r.wo.at[:, my_columns]
    wo_gather = Gather(
        at, wo_block, lambda c: r.wo.at[:, rows_of(c, columns)], *r.wog_sem
    )

    def wd_copy(d):
        to = at.plane_at(d)
        block = r.wd.at[rows_of(k_own, LANES), :]
        return remote(block, block, r.wd_sem[0].at[d - 1], r.wd_sem[1].at[k_own], (me, to))

    small_planes.start()
    tok_gather.start()
    write_extras(r, at, seq)
    ext_swap.start()
    for copy in stage[:3]:
        copy.wait()
    wj_planes.start()
    stage[3].wait()
    wo_planes.start()

    r.tokg[my_tokens, :] = tokens[...]
    r.cotg[my_tokens, :] = cotangent[...]
    r.extg[my_tokens, :] = r.extras[me]
    r.smallg[f] = small[...]
    small_planes.waits()
    params = r.params
    params[...] = jnp.zeros_like(params)

    def add_params(p):
        params[...] += r.smallg[p].astype(F32)

    loop(0, planes, add_params)
    for k in range(ff_blocks):
        r.ub[0:1, k * LANES : (k + 1) * LANES] = params[5 + k : 6 + k, my_columns]

    def norm_tokens(g):
        @pl.when(g > 0)
        def _():
            tok_gather.relay(g)

        tok_gather.wait(at.other(g))
        rows = rows_of(at.chip_at(g), 2 * local)
        normal, _ = standard(r.tokg[rows, :].astype(F32))
        r.x1[rows, :] = (normal * params[0:1, :] + params[1:2, :]).astype(BF16)

    loop(0, 4, norm_tokens)
    cot_gather.start()
    for copy in stage[4:]:
        copy.wait()
    wu_planes.start()

    @pl.when(has_down)
    def _():
        down_copy.wait()
        loop(1, planes, lambda d: wd_copy(d).start())

    ext_swap.waits()
    wj_planes.waits()

    tile = 2 * local
    lane = lax.broadcasted_iota(jnp.int32, (tile, columns), 1)
    low = lane < columns // 2
    zero_tile = jnp.zeros((tile, columns), BF16)

    def project(i):
        rows = rows_of(i, tile)
        projected = dot(r.x1[rows, :], r.wj[...]).astype(BF16)
        q = projected[:, :columns] * jnp.array(0.125, BF16)
        k = projected[:, columns : 2 * columns]
        v = projected[:, 2 * columns :]
        ext = r.extg[rows, :]
        half = lax.rem(lane, columns // 2)
        token = lax.broadcasted_iota(jnp.int32, (tile, columns), 0) + i * tile
        hot = jnp.where(half == lax.div(token, BLOCK), 1.0, 0.0)
        blocks = seq // BLOCK
        k_ext = jnp.where(
            half < blocks,
            hot,
            jnp.where(half < blocks + SEGMENTS, (1.0 - ext.astype(F32)) * -BIG, 0.0),
        ).astype(BF16)
        r.q[rows, :] = q
        r.qa[0, rows, :] = jnp.where(low, q, ext)
        r.qa[1, rows, :] = jnp.where(low, ext, q)
        r.ka[0, rows, :] = jnp.where(low, k, k_ext)
        r.ka[1, rows, :] = jnp.where(low, k_ext, k)
        r.km[0, rows, :] = jnp.where(low, k, zero_tile)
        r.km[1, rows, :] = jnp.where(low, zero_tile, k)
        r.vm[0, rows, :] = jnp.where(low, v, zero_tile)
        r.vm[1, rows, :] = jnp.where(low, zero_tile, v)

    loop(0, seq // tile, project)
    wo_planes.waits()
    wo_gather.start()

    def attend(i):
        rows = rows_of(i, tile)
        out = None
        for h in range(2):
            scores = dot_nt(r.qa[h, rows, :], r.ka[h])
            weights = jnp.exp(scores - jnp.max(scores, axis=1, keepdims=True))
            shares = (weights / jnp.sum(weights, axis=1, keepdims=True)).astype(BF16)
            r.probs[h, rows, :] = shares
            term = dot(shares, r.vm[h])
            out = term if out is None else out + term
        r.att[rows, :] = out.astype(BF16)

    loop(0, seq // tile, attend)

    att_swap = Exchange(
        at,
        lambda c: r.att.at[rows_of(c, local)],
        lambda c: r.attx.at[c],
        *r.att_sem,
    )
    att_swap.start()
    cot_gather.relays()
    wo_gather.relays()
    r.attx[me] = r.att[my_tokens, :]
    att_swap.waits()
    for c in range(CTX):
        r.attg[my_tokens, c * columns : (c + 1) * columns] = r.attx[c]
    wo_gather.waits()
    middle = tokens[...].astype(F32) + dot(r.attg[my_tokens, :], r.wo[...])
    normal, rate = standard(middle)
    r.middle[...] = middle
    r.n2[...] = normal
    r.rate2[...] = jnp.broadcast_to(rate, r.rate2.shape)
    r.x2[my_tokens, :] = (normal * params[2:3, :] + params[3:4, :]).astype(BF16)
    x2_view = lambda c: r.x2.at[rows_of(c, local)]
    x2_gather = Gather(at, x2_view(me), x2_view, *r.x2_sem)
    x2_gather.start()
    attg_view = lambda c: r.attg.at[rows_of(c, local)]
    att_gather = Gather(at, attg_view(me), attg_view, *r.attg_sem)
    wu_planes.waits()

    def wd_wait(k):
        @pl.when(down_owner(k) != f)
        def _():
            block = r.wd.at[rows_of(k, LANES), :]
            remote(block, block, r.wd_sem[0].at[0], r.wd_sem[1].at[k], (me, down_owner(k))).wait_recv()

    loop(0, ff_blocks, wd_wait)

    back = Scatter(at, *r.back)
    feed = Scatter(at, *r.feed)
    first = Scatter(at, *r.first)
    r.ubg[...] = jnp.zeros_like(r.ubg)

    def feed_forward(g):
        @pl.when(g > 0)
        def _():
            x2_gather.relay(g)

        x2_gather.wait(at.other(g))
        cot_gather.wait(at.other(g))
        chip = at.chip_at(g)
        rows = rows_of(chip, tile)
        up_sum = dot(r.x2[rows, :], r.wu[...]) + r.ub[...]
        share = 0.5 * (1.0 + lax.erf(up_sum * 0.7071067811865476))
        hidden = (up_sum * share).astype(BF16)
        slope = share + up_sum * jnp.exp(-0.5 * up_sum * up_sum) * 0.3989422804014327
        r.hidden[rows, :] = hidden
        up_grad = (dot_nt(r.cotg[rows, :], r.wd[...]) * slope).astype(BF16)
        r.upg[rows, :] = up_grad
        r.ubg[...] += jnp.sum(up_grad.astype(F32), axis=0, keepdims=True)
        back_part = dot_nt(up_grad, r.wu[...]).astype(BF16)
        r.back[0][2 * chip] = back_part[:local]
        r.back[0][2 * chip + 1] = back_part[local:]
        back.to_partner(g).start()
        feed_part = dot(hidden, r.wd[...]).astype(BF16)
        r.feed[0][2 * chip] = feed_part[:local]
        r.feed[0][2 * chip + 1] = feed_part[local:]

    loop(0, 4, feed_forward)
    back.forwards()
    att_gather.start()

    def down_grad(k):
        r.dwd[k] = dot_tn(r.hidden[:, rows_of(k, LANES)], r.cotg[...]).astype(BF16)

    def dwd_copy(k):
        return remote(
            r.dwd.at[k], r.rd.at[f], r.dwd_sem[0].at[k], r.dwd_sem[1].at[f], (me, down_owner(k))
        )

    def dwd_send(k):
        down_grad(k)

        @pl.when(down_owner(k) != f)
        def _():
            dwd_copy(k).start()

    loop(0, ff_blocks, dwd_send)
    rows_tile = min(tile, width)

    def weight_grad(out, left, right):
        def body(i):
            out[rows_of(i, rows_tile), :] = dot_tn(
                left[:, rows_of(i, rows_tile)], right[...]
            ).astype(BF16)

        loop(0, width // rows_tile, body)

    def grad_planes(grad, taken, sems):
        return Planes(
            at,
            lambda to: grad.at[rows_of(to, part_rows), :],
            lambda p: taken.at[p],
            *sems,
        )

    du_planes = grad_planes(r.du, r.ru, r.du_sem)
    do_planes = grad_planes(r.do, r.ro, r.do_sem)
    dj_planes = grad_planes(r.dj, r.rj, r.dj_sem)
    weight_grad(r.du, r.x2, r.upg)
    du_planes.start()

    normed_two_grad = back.total()
    normal = r.n2[...]
    cot_own = cotangent[...].astype(F32)
    sums = r.sums
    sums[...] = jnp.zeros_like(sums)
    sums[2:3, :] = jnp.sum(normed_two_grad * normal, axis=0, keepdims=True)
    sums[3:4, :] = jnp.sum(normed_two_grad, axis=0, keepdims=True)
    sums[4:5, :] = jnp.sum(cot_own, axis=0, keepdims=True)
    for k in range(ff_blocks):
        sums[5 + k : 6 + k, my_columns] = r.ubg[0:1, k * LANES : (k + 1) * LANES]
    middle_grad = cot_own + standard_grad(
        normed_two_grad * params[2:3, :], normal, r.rate2[:, 0:1]
    )
    r.tokens_grad[...] = middle_grad
    branch = middle_grad.astype(BF16)
    attended_grad = dot_nt(branch, r.wo[...]).astype(BF16)
    for c in range(CTX):
        r.dat[c] = attended_grad[:, c * columns : (c + 1) * columns]
        r.brs[c] = branch[:, c * columns : (c + 1) * columns]

    def token_swap(src, dst, sems):
        return Exchange(at, lambda c: src.at[c], lambda c: dst.at[rows_of(c, local)], *sems)

    dat_swap = token_swap(r.dat, r.datg, r.dat_sem)
    br_swap = token_swap(r.brs, r.brg, r.br_sem)
    dat_swap.start()
    br_swap.start()
    r.datg[my_tokens, :] = r.dat[me]
    r.brg[my_tokens, :] = r.brs[me]
    att_gather.relays()
    loop(0, 4, lambda g: feed.to_partner(g).start())
    r.dk[...] = jnp.zeros_like(r.dk)
    r.dv[...] = jnp.zeros_like(r.dv)
    dat_swap.waits()

    def attend_back(i):
        rows = rows_of(i, tile)
        grad = r.datg[rows, :]
        both = grad.astype(F32) * r.att[rows, :].astype(F32)
        q = r.q[rows, :]
        query_grad = None
        for h in range(2):
            keep = low if h == 0 else ~low
            delta = jnp.sum(jnp.where(keep, both, 0.0), axis=1, keepdims=True)
            probs = r.probs[h, rows, :]
            prob_grad = dot_nt(grad, r.vm[h])
            score_grad = (probs.astype(F32) * (prob_grad - delta)).astype(BF16)
            term = dot(score_grad, r.km[h])
            query_grad = term if query_grad is None else query_grad + term
            r.dk[...] += dot_tn(score_grad, jnp.where(keep, q, zero_tile))
            r.dv[...] += dot_tn(probs, jnp.where(keep, grad, zero_tile))
        r.pg[rows, :columns] = (query_grad * 0.125).astype(BF16)

    loop(0, seq // tile, attend_back)
    r.pg[:, columns : 2 * columns] = r.dk[...].astype(BF16)
    r.pg[:, 2 * columns :] = r.dv[...].astype(BF16)
    weight_grad(r.dj, r.x1, r.pg)
    dj_planes.start()

    def first_part(g):
        chip = at.chip_at(g)
        part = dot_nt(r.pg[rows_of(chip, tile), :], r.wj[...]).astype(BF16)
        r.first[0][2 * chip] = part[:local]
        r.first[0][2 * chip + 1] = part[local:]
        first.to_partner(g).start()

    loop(0, 4, first_part)
    feed.forwards()
    first.forwards()
    att_gather.waits()
    br_swap.waits()
    weight_grad(r.do, r.attg, r.brg)
    do_planes.start()

    class Owned:
        def __init__(self, number, copies, grad, taken, acc, total, out, sems):
            self.copies, self.grad, self.taken, self.acc, self.total = copies, grad, taken, acc, total
            self.gather = Gather(at, total, lambda c: out.at[c], *sems)
            self.own = pltpu.make_async_copy(total, out.at[me], r.own.at[number])

        def reduce(self):
            self.copies.waits()
            self.acc[...] = self.grad[my_rows, :].astype(F32)

            def add(d):
                self.acc[...] += self.taken[at.plane_at(d)].astype(F32)

            loop(1, planes, add)
            self.total[...] = self.acc[...].astype(BF16)
            self.gather.start()
            self.own.start()

    owned_u = Owned(0, du_planes, r.du, r.ru, r.au, r.tu, r.gu, r.gu_sem)
    owned_o = Owned(1, do_planes, r.do, r.ro, r.ao, r.to, r.go, r.go_sem)
    owned_j = Owned(2, dj_planes, r.dj, r.rj, r.aj, r.tj, r.gj, r.gj_sem)

    full_shard = shard_blocks == CTX
    gd_gather = Gather(
        at, r.td, lambda c: r.gd.at[c], *r.gd_sem
    )
    gd_own = pltpu.make_async_copy(r.td, r.gd.at[down_place], r.own.at[3])

    def gd_copy(d):
        return remote(
            r.td, r.gd.at[down_place], r.gd_sem[0].at[d - 1], r.gd_sem[1].at[down_place], (at.ctx_at(d), f)
        )

    @pl.when(has_down)
    def _():
        def take(d):
            p = at.plane_at(d)
            block = r.rd.at[p]
            remote(block, block, r.dwd_sem[0].at[0], r.dwd_sem[1].at[p], (me, p)).wait_recv()

        loop(1, planes, take)
        total = r.n2
        total[...] = r.dwd[k_own].astype(F32)

        def add(d):
            total[...] += r.rd[at.plane_at(d)].astype(F32)

        loop(1, planes, add)
        r.td[...] = total[...].astype(BF16)
        gd_own.start()
        if not full_shard:
            loop(1, CTX, lambda d: gd_copy(d).start())

    if full_shard:
        gd_gather.start()
    owned_u.reduce()

    feed_total = feed.total()
    r.layer_out[...] = (r.middle[...] + feed_total + params[4:5, :]).astype(BF16)
    owned_j.reduce()

    normed_one_grad = first.total()
    normal, rate = standard(tokens[...].astype(F32))
    sums[0:1, :] = jnp.sum(normed_one_grad * normal, axis=0, keepdims=True)
    sums[1:2, :] = jnp.sum(normed_one_grad, axis=0, keepdims=True)
    r.tokens_grad[...] += standard_grad(
        normed_one_grad * params[0:1, :], normal, rate
    )
    r.sum_s[...] = sums[...].astype(BF16)
    sum_swap = Exchange(
        at, lambda c: r.sum_s, lambda c: r.sum_c.at[c], *r.sumc_sem
    )
    sum_swap.start()
    owned_o.reduce()
    if full_shard:
        gd_gather.relays()
    owned_u.gather.relays()
    sum_swap.waits()

    def add_ctx(d):
        sums[...] += r.sum_c[at.ctx_at(d)].astype(F32)

    loop(1, CTX, add_ctx)
    r.sum_p[...] = sums[...].astype(BF16)
    sum_planes = Planes(
        at, lambda to: r.sum_p, lambda p: r.sum_z.at[p], *r.sumz_sem
    )
    sum_planes.start()
    owned_j.gather.relays()
    owned_o.gather.relays()
    sum_planes.waits()

    def add_planes(d):
        sums[...] += r.sum_z[at.plane_at(d)].astype(F32)

    loop(1, planes, add_planes)
    r.totals[0:8, :] = pltpu.roll(
        sums[0:8, :], lax.rem((planes - f) * part_rows, width), axis=1
    )
    bias_total = jnp.sum(
        jnp.where(row == 5 + bias_row, sums[...], 0.0), axis=0, keepdims=True
    )
    r.totals[8:16, :] = pltpu.roll(
        jnp.broadcast_to(bias_total, (8, width)), width - lax.rem(f * shard, width), axis=1
    )

    for each in (owned_u, owned_o, owned_j):
        each.gather.waits()
        each.own.wait()
    if full_shard:
        gd_own.wait()
        gd_gather.waits()
        gd_gather.finish()
    else:

        @pl.when(has_down)
        def _():
            gd_own.wait()
            loop(1, CTX, lambda d: gd_copy(d).wait_send())

        def gd_take(b):
            @pl.when(me != lax.rem(f * shard_blocks + b, CTX))
            def _():
                block = r.gd.at[b]
                remote(
                    block, block, r.gd_sem[0].at[0], r.gd_sem[1].at[b], (at.ctx_at(jnp.int32(1)), f)
                ).wait_recv()

        loop(0, shard_blocks, gd_take)

    @pl.when(has_down)
    def _():
        loop(1, planes, lambda d: wd_copy(d).wait_send())

    def dwd_sent(k):
        @pl.when(down_owner(k) != f)
        def _():
            dwd_copy(k).wait_send()

    loop(0, ff_blocks, dwd_sent)
    for each in (
        tok_gather, cot_gather, wo_gather, x2_gather, att_gather, owned_u.gather, owned_o.gather,
        owned_j.gather, ext_swap, att_swap, dat_swap, br_swap, sum_swap, small_planes, wj_planes,
        wo_planes, wu_planes, du_planes, do_planes, dj_planes, sum_planes, back, feed, first,
    ):
        each.finish()


def shards(
    tokens,
    segment_ids,
    random_blocks,
    global_blocks,
    first_gain,
    first_bias,
    joint_weight,
    output_weight,
    second_gain,
    second_bias,
    up_weight,
    up_bias,
    down_weight,
    down_bias,
    cotangent,
):
    local, width = tokens.shape[1:]
    ctx, planes = lax.axis_size("ctx"), lax.axis_size("fsdp")
    heads = random_blocks.shape[2]
    seq = local * ctx
    blocks = seq // BLOCK
    part_rows = width // planes
    columns = width // ctx
    ff_shard = up_bias.shape[0]
    ff = ff_shard * planes
    ff_blocks = ff // LANES // ctx
    shard_blocks = ff_shard // LANES
    ff_part = ff // ctx
    assert ctx == CTX and columns == LANES and heads == 2 * ctx and blocks + SEGMENTS <= 64
    assert CTX % shard_blocks == 0 and ff // width == ff_blocks

    vmem, hbm = pl.BlockSpec(memory_space=pltpu.VMEM), pl.BlockSpec(memory_space=pl.ANY)
    inputs = dict(
        tokens=(tokens[0], vmem),
        cotangent=(cotangent[0], vmem),
        segments=(segment_ids, vmem),
        random=(random_blocks[0], vmem),
        globals=(global_blocks, vmem),
        gain_one=(first_gain, vmem),
        bias_one=(first_bias, vmem),
        gain_two=(second_gain, vmem),
        bias_two=(second_bias, vmem),
        bias_up=(up_bias, vmem),
        bias_down=(down_bias, vmem),
        joint=(joint_weight, hbm),
        outw=(output_weight, hbm),
        up=(up_weight, hbm),
        down=(down_weight, hbm),
    )
    outputs = dict(
        layer_out=((local, width), BF16, vmem),
        tokens_grad=((local, width), F32, vmem),
        totals=((16, width), F32, vmem),
        gj=((ctx, part_rows, 3 * columns), BF16, hbm),
        go=((ctx, part_rows, columns), BF16, hbm),
        gu=((ctx, part_rows, ff_part), BF16, hbm),
        gd=((shard_blocks, LANES, width), BF16, hbm),
    )
    dma = lambda n: pltpu.SemaphoreType.DMA((n,))
    v16 = lambda *shape: pltpu.VMEM(shape, BF16)
    v32 = lambda *shape: pltpu.VMEM(shape, F32)
    others = max(planes - 1, 1)
    scatter = (
        v16(ctx, local, width), v16(4, local, width), v16(3, local, width),
        dma(4), dma(4), dma(3), dma(3),
    )
    gather, swap, plane_sems = (dma(7), dma(ctx)), (dma(ctx - 1), dma(ctx)), (dma(others), dma(planes))
    scratch = dict(
        wj=v16(width, 3 * columns), wo=v16(width, width), wu=v16(width, ff_part),
        wd=v16(ff_part, width), tokg=v16(seq, width), cotg=v16(seq, width),
        x1=v16(seq, width), x2=v16(seq, width), attg=v16(seq, width),
        extras=v16(ctx, local, columns), small=v16(16, width), extg=v16(seq, columns), smallg=v16(planes, 16, width), params=v32(16, width),
        ub=v32(1, ff_part), ubg=v32(1, ff_part), q=v16(seq, columns),
        qa=v16(2, seq, columns), ka=v16(2, seq, columns), km=v16(2, seq, columns),
        vm=v16(2, seq, columns), probs=v16(2, seq, seq), att=v16(seq, columns),
        attx=v16(ctx, local, columns), middle=v32(local, width), n2=v32(local, width),
        rate2=v32(local, LANES), hidden=v16(seq, ff_part),
        upg=v16(seq, ff_part), dat=v16(ctx, local, columns), brs=v16(ctx, local, columns),
        datg=v16(seq, columns), brg=v16(seq, columns), dk=v32(seq, columns),
        dv=v32(seq, columns), pg=v16(seq, 3 * columns), sums=v32(16, width),
        sum_s=v16(16, width), sum_p=v16(16, width), sum_c=v16(ctx, 16, width),
        sum_z=v16(planes, 16, width),
        dj=v16(width, 3 * columns), do=v16(width, columns), du=v16(width, ff_part),
        dwd=v16(ff_blocks, LANES, width),
        rj=v16(planes, part_rows, 3 * columns), ro=v16(planes, part_rows, columns),
        ru=v16(planes, part_rows, ff_part), rd=v16(planes, LANES, width),
        aj=v32(part_rows, 3 * columns), ao=v32(part_rows, columns), au=v32(part_rows, ff_part),
        tj=v16(part_rows, 3 * columns), to=v16(part_rows, columns),
        tu=v16(part_rows, ff_part), td=v16(LANES, width),
        stage=dma(5 + ff_blocks), own=dma(4), wd_sem=(dma(others), dma(ff_blocks)),
        dwd_sem=(dma(ff_blocks), dma(planes)), back=scatter, feed=scatter, first=scatter,
        tok_sem=gather, cot_sem=gather, wog_sem=gather, x2_sem=gather, attg_sem=gather,
        gj_sem=gather, go_sem=gather, gu_sem=gather, gd_sem=gather,
        ext_sem=swap, att_sem=swap, dat_sem=swap, br_sem=swap, sumc_sem=swap,
        small_sem=plane_sems, wj_sem=plane_sems, wo_sem=plane_sems, wu_sem=plane_sems,
        dj_sem=plane_sems, do_sem=plane_sems, du_sem=plane_sems, sumz_sem=plane_sems,
    )
    shapes, scratch_tree = jax.tree.flatten(scratch)
    ins, outs = len(inputs), len(outputs)

    def kernel(*refs):
        held = dict(zip([*inputs, *outputs], refs, strict=False))
        held |= jax.tree.unflatten(scratch_tree, refs[ins + outs :])
        layer_kernel(types.SimpleNamespace(**held), planes)

    layer_out, tokens_grad, totals, gj, go, gu, gd = pl.pallas_call(
        kernel,
        out_shape=[jax.ShapeDtypeStruct(shape, dtype) for shape, dtype, _ in outputs.values()],
        in_specs=[spec for _, spec in inputs.values()],
        out_specs=[spec for *_, spec in outputs.values()],
        scratch_shapes=shapes,
        compiler_params=pltpu.CompilerParams(
            collective_id=0, has_side_effects=True, vmem_limit_bytes=60 * 1024 * 1024
        ),
    )(*(value for value, _ in inputs.values()))

    group = 4

    def spread(ref, out):
        for q in range(group):
            out[:, q * columns : (q + 1) * columns] = ref[q].astype(F32)

    def finish(totals, gj, go, gu, gd, joint, outw, up, down, *vectors):
        for ref, out in ((gj, joint), (go, outw), (gu, up)):
            spread(ref, out)
        down[...] = gd[0].astype(F32)
        for i, out in enumerate(vectors[:5]):
            out[...] = totals[i : i + 1, 0:part_rows].reshape(part_rows)
        vectors[5][...] = totals[8:9, 0:ff_shard].reshape(ff_shard)

    quads = ctx // group
    steps = ff_blocks * quads

    def spec_pair(groups):
        last = groups * quads - 1
        place = lambda i: jnp.minimum(i, last)
        return (
            pl.BlockSpec(
                (group, part_rows, columns), lambda i: (place(i) % quads, 0, place(i) // quads)
            ),
            pl.BlockSpec((part_rows, group * columns), lambda i: (0, place(i))),
        )

    pairs = [spec_pair(3), spec_pair(1), spec_pair(ff_blocks)]
    down_place = lambda i: jnp.minimum(i, shard_blocks - 1)
    whole = pl.BlockSpec(memory_space=pltpu.VMEM)
    made = pl.pallas_call(
        finish,
        grid=(steps,),
        out_shape=[
            jax.ShapeDtypeStruct(shape, F32)
            for shape in (
                (part_rows, 3 * width), (part_rows, width), (part_rows, ff), (ff_shard, width),
                *([(part_rows,)] * 5), (ff_shard,),
            )
        ],
        in_specs=[
            whole,
            *(pair[0] for pair in pairs),
            pl.BlockSpec((1, LANES, width), lambda i: (down_place(i), 0, 0)),
        ],
        out_specs=[
            *(pair[1] for pair in pairs),
            pl.BlockSpec((LANES, width), lambda i: (down_place(i), 0)),
            *([whole] * 6),
        ],
    )(totals, gj, go, gu, gd)
    return (
        layer_out[None],
        tokens_grad[None],
        made[4],
        made[5],
        made[0],
        made[1],
        made[6],
        made[7],
        made[2],
        made[9],
        made[3],
        made[8],
    )


def solution(mesh):
    in_specs = (
        P("fsdp", "ctx", None),
        P("fsdp", "ctx"),
        P("fsdp", "ctx", None, None),
        P("fsdp", None),
        P("fsdp"),
        P("fsdp"),
        P("fsdp", None),
        P("fsdp", None),
        P("fsdp"),
        P("fsdp"),
        P("fsdp", None),
        P("fsdp"),
        P("fsdp", None),
        P("fsdp"),
        P("fsdp", "ctx", None),
    )
    out_specs = (
        P("fsdp", "ctx", None),
        P("fsdp", "ctx", None),
        P("fsdp"),
        P("fsdp"),
        P("fsdp", None),
        P("fsdp", None),
        P("fsdp"),
        P("fsdp"),
        P("fsdp", None),
        P("fsdp"),
        P("fsdp", None),
        P("fsdp"),
    )
    return jax.shard_map(shards, mesh=mesh, in_specs=in_specs, out_specs=out_specs, check_vma=False)
```

```python
import types

import jax
import jax.numpy as jnp
from jax import lax
from jax.experimental import pallas as pl
from jax.experimental.pallas import tpu as pltpu
from jax.sharding import PartitionSpec as P

BLOCK = 64
LANES = 128
CTX = 8
SEGMENTS = 4
EPS = 1e-05
BIG = 1e30
MESH = pl.DeviceIdType.MESH
BF16 = jnp.bfloat16
F32 = jnp.float32


def dot(a, b):
    return lax.dot_general(a, b, (((1,), (0,)), ((), ())), preferred_element_type=F32)


def dot_nt(a, b):
    return lax.dot_general(a, b, (((1,), (1,)), ((), ())), preferred_element_type=F32)


def dot_tn(a, b):
    return lax.dot_general(a, b, (((0,), (0,)), ((), ())), preferred_element_type=F32)


def loop(lower, upper, body):
    lax.fori_loop(lower, upper, lambda i, carry: (body(i), carry)[1], jnp.int32(0))


def rows_of(index, size):
    return pl.ds(pl.multiple_of(index * size, size), size)


def remote(src, dst, send, recv, device):
    return pltpu.make_async_remote_copy(
        src_ref=src,
        dst_ref=dst,
        send_sem=send,
        recv_sem=recv,
        device_id=device,
        device_id_type=MESH,
    )


class Place:
    def __init__(self, planes):
        self.c = lax.axis_index("ctx")
        self.f = lax.axis_index("fsdp")
        self.planes = planes
        self.parity = lax.rem(self.c, 2)
        self.chip = lax.div(self.c, 2)
        self.partner = 2 * self.chip + 1 - self.parity

    def chip_at(self, g):
        low = lax.rem(lax.rem(self.chip, 2) + lax.rem(g, 2), 2)
        high = lax.rem(lax.div(self.chip, 2) + lax.div(g, 2), 2)
        return low + 2 * high

    def same(self, g):
        return 2 * self.chip_at(g) + self.parity

    def other(self, g):
        return 2 * self.chip_at(g) + 1 - self.parity

    def ctx_at(self, d):
        return lax.rem(self.c + d, CTX)

    def plane_at(self, d):
        return lax.rem(self.f + d, self.planes)


class Gather:
    def __init__(self, at, src, slot, send, recv):
        self.at, self.src, self.slot, self.send, self.recv = at, src, slot, send, recv

    def half(self, c, i):
        block = self.slot(c)
        size = block.shape[0] // 2
        return block.at[pl.ds(i * size, size)]

    def direct(self, i):
        at = self.at
        to = at.partner if i == 0 else at.same(jnp.int32(i))
        return remote(self.src, self.slot(at.c), self.send.at[i], self.recv.at[at.c], (to, at.f))

    def across(self, i):
        at = self.at
        c, to = at.same(jnp.int32(1 + i)), at.same(jnp.int32(2 - i))
        block = self.half(c, i)
        recv = self.recv.at[c] if i == 0 else self.recv.at[CTX]
        return remote(block, block, self.send.at[3 + i], recv, (to, at.f))

    def passed(self, g):
        at = self.at
        c = at.same(jnp.int32(g))
        block = self.slot(c)
        return remote(block, block, self.send.at[4 + g], self.recv.at[c], (at.partner, at.f))

    def start(self):
        for i in (1, 2, 0):
            self.direct(i).start()

    def wait(self, c):
        at = self.at
        block = self.slot(c)
        remote(block, block, self.send.at[0], self.recv.at[c], (at.partner, at.f)).wait_recv()

    def near(self):
        for i in range(2):
            self.wait(self.at.same(jnp.int32(1 + i)))
            self.across(i).start()
        for g in (1, 2):
            self.passed(g).start()

    def far(self):
        at = self.at
        for i in range(2):
            c = at.same(jnp.int32(3))
            block = self.half(c, i)
            recv = self.recv.at[c] if i == 0 else self.recv.at[CTX]
            remote(block, block, self.send.at[0], recv, (at.partner, at.f)).wait_recv()
        self.passed(3).start()

    def waits(self):
        loop(0, 4, lambda g: self.wait(self.at.other(g)))

    def finish(self):
        for i in range(3):
            self.direct(i).wait_send()
        for i in range(2):
            self.across(i).wait_send()
        for g in (1, 2, 3):
            self.passed(g).wait_send()


class Exchange:
    def __init__(self, at, src, slot, send, recv):
        self.at, self.src, self.slot, self.send, self.recv = at, src, slot, send, recv

    def copy(self, d):
        at = self.at
        to = at.ctx_at(d)
        return remote(
            self.src(to), self.slot(at.c), self.send.at[d - 1], self.recv.at[at.c], (to, at.f)
        )

    def start(self):
        loop(1, CTX, lambda d: self.copy(d).start())

    def wait(self, d):
        at = self.at
        c = at.ctx_at(d)
        block = self.slot(c)
        remote(block, block, self.send.at[0], self.recv.at[c], (c, at.f)).wait_recv()

    def waits(self):
        loop(1, CTX, self.wait)

    def finish(self):
        loop(1, CTX, lambda d: self.copy(d).wait_send())


class Planes:
    def __init__(self, at, src, slot, send, recv):
        self.at, self.src, self.slot, self.send, self.recv = at, src, slot, send, recv

    def copy(self, d):
        at = self.at
        to = at.plane_at(d)
        return remote(
            self.src(to), self.slot(at.f), self.send.at[d - 1], self.recv.at[at.f], (at.c, to)
        )

    def start(self):
        loop(1, self.at.planes, lambda d: self.copy(d).start())

    def wait(self, d):
        at = self.at
        f = at.plane_at(d)
        block = self.slot(f)
        remote(block, block, self.send.at[0], self.recv.at[f], (at.c, f)).wait_recv()

    def waits(self):
        loop(1, self.at.planes, self.wait)

    def finish(self):
        loop(1, self.at.planes, lambda d: self.copy(d).wait_send())


class Line:
    def __init__(self, at, items, owner, view, send, recv):
        self.at, self.items, self.owner, self.view = at, items, owner, view
        self.send, self.recv = send, recv

    def hop(self, i, up):
        at, block = self.at, self.view(i)
        to = jnp.minimum(at.f + 1, at.planes - 1) if up else jnp.maximum(at.f - 1, 0)
        return remote(
            block, block, self.send.at[2 * i + (1 if up else 0)], self.recv.at[i], (at.c, to)
        )

    def outward(self, i, act):
        at, owner = self.at, self.owner(i)

        @pl.when((owner <= at.f) & (at.f < at.planes - 1))
        def _():
            act(self.hop(i, True))

        @pl.when((owner >= at.f) & (at.f > 0))
        def _():
            act(self.hop(i, False))

    def start(self):
        def each(i):
            @pl.when(self.owner(i) == self.at.f)
            def _():
                self.outward(i, lambda copy: copy.start())

        loop(0, self.items, each)

    def arrive(self, i):
        self.hop(i, True).wait_recv()
        self.outward(i, lambda copy: copy.start())

    def passes(self, d):
        def each(i):
            owner = self.owner(i)

            @pl.when((owner == self.at.f + d) | (owner == self.at.f - d))
            def _():
                self.arrive(i)

        loop(0, self.items, each)

    def passes_at(self, d):
        if d < self.at.planes:
            self.passes(d)

    def rest(self, d):
        loop(d, self.at.planes, self.passes)

    def finish(self):
        loop(0, self.items, lambda i: self.outward(i, lambda copy: copy.wait_send()))


class Toward:
    def __init__(self, at, items, owner, part, taken, send, recv):
        self.at, self.items, self.owner, self.part, self.taken = at, items, owner, part, taken
        self.send, self.recv = send, recv

    def hop(self, i, up):
        at = self.at
        to = jnp.minimum(at.f + 1, at.planes - 1) if up else jnp.maximum(at.f - 1, 0)
        slot = i + 1 if up else i
        return remote(
            self.part(i), self.taken.at[slot], self.send.at[i], self.recv.at[slot], (at.c, to)
        )

    def step(self, d):
        at = self.at

        def one(i, up, comes):
            @pl.when(comes)
            def _():
                self.hop(i, up).wait_recv()
                block = self.part(i)
                come = self.taken[i + 1 if up else i].astype(F32)
                block[...] = (block[...].astype(F32) + come).astype(BF16)

            self.hop(i, up).start()

        def each(i):
            @pl.when(self.owner(i) == at.f + d)
            def _():
                one(i, True, at.f > 0)

            @pl.when(self.owner(i) == at.f - d)
            def _():
                one(i, False, at.f < at.planes - 1)

        loop(0, self.items, each)

    def first(self, d):
        loop(d, self.at.planes, lambda j: self.step(self.at.planes - 1 + d - j))

    def total(self, i, acc):
        at = self.at
        acc[...] = self.part(i)[...].astype(F32)

        @pl.when(at.f > 0)
        def _():
            self.hop(i, True).wait_recv()
            acc[...] += self.taken[i + 1].astype(F32)

        @pl.when(at.f < at.planes - 1)
        def _():
            self.hop(i, False).wait_recv()
            acc[...] += self.taken[i].astype(F32)

    def finish(self):
        def each(i):
            @pl.when(self.owner(i) > self.at.f)
            def _():
                self.hop(i, True).wait_send()

            @pl.when(self.owner(i) < self.at.f)
            def _():
                self.hop(i, False).wait_send()

        loop(0, self.items, each)


class Scatter:
    def __init__(self, at, part, pair, halves, far, pair_send, pair_recv, send, recv):
        self.at, self.part, self.pair, self.halves, self.far = at, part, pair, halves, far
        self.pair_send, self.pair_recv, self.send, self.recv = pair_send, pair_recv, send, recv
        self.size = part.shape[1] // 2

    def to_partner(self, g):
        at = self.at
        return remote(
            self.part.at[at.other(g)],
            self.pair.at[g],
            self.pair_send.at[g],
            self.pair_recv.at[g],
            (at.partner, at.f),
        )

    def across(self, i):
        at = self.at
        return remote(
            self.part.at[at.same(jnp.int32(3)), pl.ds(i * self.size, self.size)],
            self.halves.at[i],
            self.send.at[i],
            self.recv.at[i],
            (at.same(jnp.int32(1 + i)), at.f),
        )

    def beside(self, i):
        at = self.at
        to = at.same(jnp.int32(1 + i))
        return remote(
            self.part.at[to], self.far.at[i], self.send.at[2 + i], self.recv.at[2 + i], (to, at.f)
        )

    def add_pair(self, g):
        self.to_partner(jnp.int32(g)).wait_recv()
        own = self.at.same(jnp.int32(g))
        both = self.part[own].astype(F32) + self.pair[g].astype(F32)
        self.part[own] = both.astype(BF16)

    def first(self):
        self.add_pair(3)
        for i in range(2):
            self.across(i).start()

    def second(self):
        for i in range(2):
            self.add_pair(1 + i)
        for i in range(2):
            self.across(i).wait_recv()
            to = self.at.same(jnp.int32(2 - i))
            rows = pl.ds(i * self.size, self.size)
            both = self.part[to, rows].astype(F32) + self.halves[i].astype(F32)
            self.part[to, rows] = both.astype(BF16)
            self.beside(1 - i).start()

    def total(self):
        self.to_partner(jnp.int32(0)).wait_recv()
        for i in range(2):
            self.beside(i).wait_recv()
        both = self.part[self.at.c].astype(F32) + self.pair[0].astype(F32)
        return both + (self.far[0].astype(F32) + self.far[1].astype(F32))

    def finish(self):
        loop(0, 4, lambda g: self.to_partner(g).wait_send())
        for i in range(2):
            self.across(i).wait_send()
            self.beside(i).wait_send()


def standard(values):
    centre = jnp.mean(values, axis=-1, keepdims=True)
    offset = values - centre
    spread = jnp.mean(offset * offset, axis=-1, keepdims=True)
    rate = lax.rsqrt(spread + EPS)
    return offset * rate, rate


def standard_grad(e, normal, rate):
    return rate * (
        e - jnp.mean(e, axis=-1, keepdims=True) - normal * jnp.mean(e * normal, axis=-1, keepdims=True)
    )


def write_extras(r, at, seq):
    local = r.segments.shape[1]
    blocks, local_blocks = seq // BLOCK, local // BLOCK
    heads = r.random.shape[1]
    half = LANES // 2
    key = lax.rem(lax.broadcasted_iota(jnp.int32, (heads, LANES), 1), half)
    lower = lax.broadcasted_iota(jnp.int32, (1, LANES), 1) < half
    place = lax.rem(lax.broadcasted_iota(jnp.int32, (LANES, local), 0), half)
    hot = jnp.where(r.segments[...] == place - blocks, 1.0, 0.0).T
    hot = jnp.where(key[0:1] >= blocks + SEGMENTS, 0.0, hot)
    pair = r.globals[...]
    for b in range(local_blocks):
        block = at.c * local_blocks + b
        drawn = r.random[b]
        counted = jnp.abs(key - block) <= 1
        for j in range(drawn.shape[1]):
            counted = counted | (key == drawn[:, j : j + 1])
        for j in range(pair.shape[1]):
            chosen = pair[:, j : j + 1]
            counted = counted | (key == chosen) | (chosen == block)
        code = jnp.where(counted | (key >= blocks), 0.0, -BIG)
        rows = slice(b * BLOCK, (b + 1) * BLOCK)
        for d in range(heads // 2):
            both = jnp.where(lower, code[2 * d + 1 : 2 * d + 2], code[2 * d : 2 * d + 1])
            r.extras[d, rows, :] = (both + hot[rows]).astype(BF16)


def layer_kernel(r, planes):
    at = Place(planes)
    me, f = at.c, at.f
    tokens, cotangent = r.tokens, r.cotangent
    local, width = tokens.shape
    seq = local * CTX
    part_rows = width // planes
    columns = width // CTX
    ff = planes * r.down.shape[0]
    ff_blocks = ff // LANES // CTX
    shard_blocks = ff // LANES // planes
    k_own = lax.div(f * shard_blocks, CTX)
    has_down = lax.div(me, shard_blocks) == lax.rem(f, CTX // shard_blocks)
    down_place = lax.rem(me, shard_blocks)

    def down_owner(k):
        return lax.div(CTX * k + me, shard_blocks)

    my_rows = rows_of(f, part_rows)
    my_columns = rows_of(me, columns)
    my_tokens = rows_of(me, local)

    stage = []
    for j in range(3):
        stage.append(
            pltpu.make_async_copy(
                r.joint.at[:, pl.ds(pl.multiple_of(width * j + columns * me, LANES), columns)],
                r.wj.at[my_rows, pl.ds(columns * j, columns)],
                r.stage.at[j],
            )
        )
    stage.append(
        pltpu.make_async_copy(
            r.outw.at[:, my_columns], r.wo.at[my_rows, my_columns], r.stage.at[3]
        )
    )
    for k in range(ff_blocks):
        stage.append(
            pltpu.make_async_copy(
                r.up.at[:, pl.ds(pl.multiple_of(CTX * LANES * k + LANES * me, LANES), LANES)],
                r.wu.at[my_rows, pl.ds(LANES * k, LANES)],
                r.stage.at[4 + k],
            )
        )
    down_copy = pltpu.make_async_copy(
        r.down.at[rows_of(down_place, LANES), :],
        r.wd.at[rows_of(k_own, LANES), :],
        r.stage.at[4 + ff_blocks],
    )
    for copy in stage:
        copy.start()

    @pl.when(has_down)
    def _():
        down_copy.start()

    small, wide, shard = r.small, r.sums, ff // planes
    wide[...] = jnp.zeros_like(wide)
    for i, vector in enumerate((r.gain_one, r.bias_one, r.gain_two, r.bias_two, r.bias_down)):
        wide[i : i + 1, 0:part_rows] = vector[...].astype(F32).reshape(1, part_rows)
    wide[8:9, 0:shard] = r.bias_up[...].astype(F32).reshape(1, shard)
    vectors = pltpu.roll(wide[0:8, :], f * part_rows, axis=1)
    bias_row = lax.div(f * shard, width)
    bias = pltpu.roll(wide[8:16, :], lax.rem(f * shard, width), axis=1)[0:1]
    row = lax.broadcasted_iota(jnp.int32, (16, width), 0)
    small[...] = jnp.where(
        row == 5 + bias_row, bias, jnp.concatenate([vectors, jnp.zeros_like(vectors)], axis=0)
    ).astype(BF16)

    barrier = pltpu.get_barrier_semaphore()
    loop(
        1,
        CTX,
        lambda d: pl.semaphore_signal(
            barrier, inc=1, device_id=(at.ctx_at(d), f), device_id_type=MESH
        ),
    )
    loop(
        1,
        planes,
        lambda d: pl.semaphore_signal(
            barrier, inc=1, device_id=(me, at.plane_at(d)), device_id_type=MESH
        ),
    )
    pl.semaphore_wait(barrier, CTX - 1 + planes - 1)

    tok_gather = Gather(
        at, tokens, lambda c: r.tokg.at[rows_of(c, local)], *r.tok_sem
    )
    cot_gather = Gather(
        at, cotangent, lambda c: r.cotg.at[rows_of(c, local)], *r.cot_sem
    )
    ext_swap = Exchange(
        at,
        lambda c: r.extras.at[c],
        lambda c: r.extg.at[rows_of(c, local)],
        *r.ext_sem,
    )
    small_planes = Planes(
        at, lambda to: small, lambda p: r.smallg.at[p], *r.small_sem
    )

    def weight_planes(ref, sems, width_ds):
        view = lambda p: ref.at[rows_of(p, part_rows), width_ds]
        return Line(at, planes, lambda i: i, view, *sems)

    wj_planes = weight_planes(r.wj, r.wj_sem, slice(None))
    wo_planes = weight_planes(r.wo, r.wo_sem, my_columns)
    wu_planes = weight_planes(r.wu, r.wu_sem, slice(None))
    wo_block = r.wo.at[:, my_columns]
    wo_gather = Gather(
        at, wo_block, lambda c: r.wo.at[:, rows_of(c, columns)], *r.wog_sem
    )

    wd_planes = Line(
        at, ff_blocks, down_owner, lambda k: r.wd.at[rows_of(k, LANES), :], *r.wd_sem
    )

    small_planes.start()
    tok_gather.start()
    for copy in stage[:3]:
        copy.wait()
    wj_planes.start()
    write_extras(r, at, seq)
    r.tokg[my_tokens, :] = tokens[...]
    r.cotg[my_tokens, :] = cotangent[...]
    r.extg[my_tokens, :] = r.extras[me]
    r.smallg[f] = small[...]
    small_planes.waits()
    params = r.params
    params[...] = jnp.zeros_like(params)

    def add_params(p):
        params[...] += r.smallg[p].astype(F32)

    loop(0, planes, add_params)
    for k in range(ff_blocks):
        r.ub[0:1, k * LANES : (k + 1) * LANES] = params[5 + k : 6 + k, my_columns]

    def norm_tokens(g):
        @pl.when(g == 1)
        def _():
            tok_gather.near()
            ext_swap.start()

        @pl.when(g == 2)
        def _():
            wj_planes.passes_at(1)

        @pl.when(g == 3)
        def _():
            tok_gather.far()

        tok_gather.wait(at.other(g))
        rows = rows_of(at.chip_at(g), 2 * local)
        normal, _ = standard(r.tokg[rows, :].astype(F32))
        r.x1[rows, :] = (normal * params[0:1, :] + params[1:2, :]).astype(BF16)

    loop(0, 4, norm_tokens)
    cot_gather.start()
    wj_planes.passes_at(2)
    stage[3].wait()
    wo_planes.start()
    wj_planes.rest(3)
    ext_swap.waits()
    for copy in stage[4:]:
        copy.wait()

    @pl.when(has_down)
    def _():
        down_copy.wait()

    tile = 2 * local
    lane = lax.broadcasted_iota(jnp.int32, (tile, columns), 1)
    low = lane < columns // 2
    zero_tile = jnp.zeros((tile, columns), BF16)

    def project(i):
        rows = rows_of(i, tile)
        projected = dot(r.x1[rows, :], r.wj[...]).astype(BF16)
        q = projected[:, :columns] * jnp.array(0.125, BF16)
        k = projected[:, columns : 2 * columns]
        v = projected[:, 2 * columns :]
        ext = r.extg[rows, :]
        half = lax.rem(lane, columns // 2)
        token = lax.broadcasted_iota(jnp.int32, (tile, columns), 0) + i * tile
        hot = jnp.where(half == lax.div(token, BLOCK), 1.0, 0.0)
        blocks = seq // BLOCK
        k_ext = jnp.where(
            half < blocks,
            hot,
            jnp.where(half < blocks + SEGMENTS, (1.0 - ext.astype(F32)) * -BIG, 0.0),
        ).astype(BF16)
        r.q[rows, :] = q
        r.qa[0, rows, :] = jnp.where(low, q, ext)
        r.qa[1, rows, :] = jnp.where(low, ext, q)
        r.ka[0, rows, :] = jnp.where(low, k, k_ext)
        r.ka[1, rows, :] = jnp.where(low, k_ext, k)
        r.km[0, rows, :] = jnp.where(low, k, zero_tile)
        r.km[1, rows, :] = jnp.where(low, zero_tile, k)
        r.vm[0, rows, :] = jnp.where(low, v, zero_tile)
        r.vm[1, rows, :] = jnp.where(low, zero_tile, v)

    loop(0, seq // tile, project)
    wo_planes.passes_at(1)

    def attend(i):
        @pl.when(i == 1)
        def _():
            wo_planes.passes_at(2)
            wu_planes.start()

        @pl.when(i == 2)
        def _():
            wo_planes.rest(3)
            cot_gather.near()

        @pl.when(i == 3)
        def _():
            wo_gather.start()
            cot_gather.far()

        rows = rows_of(i, tile)
        out = None
        for h in range(2):
            scores = dot_nt(r.qa[h, rows, :], r.ka[h])
            weights = jnp.exp(scores - jnp.max(scores, axis=1, keepdims=True))
            shares = (weights / jnp.sum(weights, axis=1, keepdims=True)).astype(BF16)
            r.probs[h, rows, :] = shares
            term = dot(shares, r.vm[h])
            out = term if out is None else out + term
        r.att[rows, :] = out.astype(BF16)

    loop(0, seq // tile, attend)

    att_swap = Exchange(
        at,
        lambda c: r.att.at[rows_of(c, local)],
        lambda c: r.attx.at[c],
        *r.att_sem,
    )
    att_swap.start()
    wu_planes.passes_at(1)
    r.attx[me] = r.att[my_tokens, :]
    wo_gather.near()
    wu_planes.passes_at(2)
    wd_planes.start()
    wo_gather.far()
    att_swap.waits()
    for c in range(CTX):
        r.attg[my_tokens, c * columns : (c + 1) * columns] = r.attx[c]
    wo_gather.waits()
    middle = tokens[...].astype(F32) + dot(r.attg[my_tokens, :], r.wo[...])
    normal, rate = standard(middle)
    r.middle[...] = middle
    r.n2[...] = normal
    r.rate2[...] = jnp.broadcast_to(rate, r.rate2.shape)
    r.x2[my_tokens, :] = (normal * params[2:3, :] + params[3:4, :]).astype(BF16)
    x2_view = lambda c: r.x2.at[rows_of(c, local)]
    x2_gather = Gather(at, x2_view(me), x2_view, *r.x2_sem)
    x2_gather.start()
    attg_view = lambda c: r.attg.at[rows_of(c, local)]
    att_gather = Gather(at, attg_view(me), attg_view, *r.attg_sem)
    wu_planes.rest(3)

    back = Scatter(at, *r.back)
    feed = Scatter(at, *r.feed)
    first = Scatter(at, *r.first)
    r.ubg[...] = jnp.zeros_like(r.ubg)

    def hidden_units(g):
        @pl.when(g == 1)
        def _():
            x2_gather.near()

        @pl.when(g == 3)
        def _():
            x2_gather.far()

        x2_gather.wait(at.other(g))
        cot_gather.wait(at.other(g))
        rows = rows_of(at.chip_at(g), tile)
        up_sum = dot(r.x2[rows, :], r.wu[...]) + r.ub[...]
        share = 0.5 * (1.0 + lax.erf(up_sum * 0.7071067811865476))
        r.hidden[rows, :] = (up_sum * share).astype(BF16)
        r.slope[rows, :] = share + up_sum * jnp.exp(-0.5 * up_sum * up_sum) * 0.3989422804014327

    loop(0, 4, hidden_units)
    att_gather.start()

    def down_grad(k):
        r.dwd[k] = dot_tn(r.hidden[:, rows_of(k, LANES)], r.cotg[...]).astype(BF16)

    loop(0, ff_blocks, down_grad)
    dd_planes = Toward(at, ff_blocks, down_owner, lambda k: r.dwd.at[k], r.rd, *r.dwd_sem)
    wd_planes.passes_at(1)
    dd_planes.first(3)
    wd_planes.passes_at(2)
    if planes > 2:
        dd_planes.step(2)
    att_gather.near()
    wd_planes.rest(3)

    def feed_back(j):
        g = jnp.where(j == 0, 3, jnp.where(j == 3, 0, j))

        @pl.when(j == 2)
        def _():
            back.first()

        chip = at.chip_at(g)
        rows = rows_of(chip, tile)
        up_grad = (dot_nt(r.cotg[rows, :], r.wd[...]) * r.slope[rows, :]).astype(BF16)
        r.upg[rows, :] = up_grad
        r.ubg[...] += jnp.sum(up_grad.astype(F32), axis=0, keepdims=True)
        part = dot_nt(up_grad, r.wu[...]).astype(BF16)
        r.back[0][2 * chip] = part[:local]
        r.back[0][2 * chip + 1] = part[local:]
        back.to_partner(g).start()

    loop(0, 4, feed_back)
    back.second()
    if planes > 1:
        dd_planes.step(1)
    rows_tile = min(tile, width)

    def weight_grad(out, left, right):
        def body(i):
            out[rows_of(i, rows_tile), :] = dot_tn(
                left[:, rows_of(i, rows_tile)], right[...]
            ).astype(BF16)

        loop(0, width // rows_tile, body)

    def grad_planes(grad, taken, sems):
        return Toward(
            at,
            planes,
            lambda i: i,
            lambda i: grad.at[rows_of(i, part_rows), :],
            taken,
            *sems,
        )

    du_planes = grad_planes(r.du, r.ru, r.du_sem)
    do_planes = grad_planes(r.do, r.ro, r.do_sem)
    dj_planes = grad_planes(r.dj, r.rj, r.dj_sem)
    weight_grad(r.du, r.x2, r.upg)
    du_planes.first(3)

    def feed_part(g):
        chip = at.chip_at(g)
        part = dot(r.hidden[rows_of(chip, tile), :], r.wd[...]).astype(BF16)
        r.feed[0][2 * chip] = part[:local]
        r.feed[0][2 * chip + 1] = part[local:]
        feed.to_partner(g).start()

    loop(0, 4, feed_part)
    att_gather.far()

    normed_two_grad = back.total()
    normal = r.n2[...]
    cot_own = cotangent[...].astype(F32)
    sums = r.sums
    sums[...] = jnp.zeros_like(sums)
    sums[2:3, :] = jnp.sum(normed_two_grad * normal, axis=0, keepdims=True)
    sums[3:4, :] = jnp.sum(normed_two_grad, axis=0, keepdims=True)
    sums[4:5, :] = jnp.sum(cot_own, axis=0, keepdims=True)
    for k in range(ff_blocks):
        sums[5 + k : 6 + k, my_columns] = r.ubg[0:1, k * LANES : (k + 1) * LANES]
    middle_grad = cot_own + standard_grad(
        normed_two_grad * params[2:3, :], normal, r.rate2[:, 0:1]
    )
    r.tokens_grad[...] = middle_grad
    branch = middle_grad.astype(BF16)
    attended_grad = dot_nt(branch, r.wo[...]).astype(BF16)
    for c in range(CTX):
        r.dat[c] = attended_grad[:, c * columns : (c + 1) * columns]
        r.brs[c] = branch[:, c * columns : (c + 1) * columns]

    def token_swap(src, dst, sems):
        return Exchange(at, lambda c: src.at[c], lambda c: dst.at[rows_of(c, local)], *sems)

    dat_swap = token_swap(r.dat, r.datg, r.dat_sem)
    br_swap = token_swap(r.brs, r.brg, r.br_sem)
    dat_swap.start()
    br_swap.start()
    r.datg[my_tokens, :] = r.dat[me]
    r.brg[my_tokens, :] = r.brs[me]
    if planes > 2:
        du_planes.step(2)
    feed.first()
    r.dk[...] = jnp.zeros_like(r.dk)
    r.dv[...] = jnp.zeros_like(r.dv)

    class Owned:
        def __init__(self, number, copies, acc, total, out, sems):
            self.copies, self.acc, self.total = copies, acc, total
            self.gather = Gather(at, total, lambda c: out.at[c], *sems)
            self.own = pltpu.make_async_copy(total, out.at[me], r.own.at[number])

        def reduce(self):
            self.copies.total(f, self.acc)
            self.total[...] = self.acc[...].astype(BF16)
            self.gather.start()
            self.own.start()

    owned_u = Owned(0, du_planes, r.au, r.tu, r.gu, r.gu_sem)
    owned_o = Owned(1, do_planes, r.ao, r.to, r.go, r.go_sem)
    owned_j = Owned(2, dj_planes, r.aj, r.tj, r.gj, r.gj_sem)

    full_shard = shard_blocks == CTX
    gd_gather = Gather(
        at, r.td, lambda c: r.gd.at[c], *r.gd_sem
    )
    gd_own = pltpu.make_async_copy(r.td, r.gd.at[down_place], r.own.at[3])

    def gd_copy(d):
        return remote(
            r.td, r.gd.at[down_place], r.gd_sem[0].at[d - 1], r.gd_sem[1].at[down_place], (at.ctx_at(d), f)
        )

    def reduce_down():
        @pl.when(has_down)
        def _():
            dd_planes.total(k_own, r.ad)
            r.td[...] = r.ad[...].astype(BF16)
            gd_own.start()
            if not full_shard:
                loop(1, CTX, lambda d: gd_copy(d).start())

        if full_shard:
            gd_gather.start()

    reduce_down()
    dat_swap.waits()

    def attend_back(i):
        @pl.when(i == 1)
        def _():
            feed.second()

        @pl.when(i == 2)
        def _():
            if planes > 1:
                du_planes.step(1)
            if full_shard:
                gd_gather.near()

        @pl.when(i == 3)
        def _():
            if full_shard:
                gd_gather.far()

        rows = rows_of(i, tile)
        grad = r.datg[rows, :]
        both = grad.astype(F32) * r.att[rows, :].astype(F32)
        q = r.q[rows, :]
        query_grad = None
        for h in range(2):
            keep = low if h == 0 else ~low
            delta = jnp.sum(jnp.where(keep, both, 0.0), axis=1, keepdims=True)
            probs = r.probs[h, rows, :]
            prob_grad = dot_nt(grad, r.vm[h])
            score_grad = (probs.astype(F32) * (prob_grad - delta)).astype(BF16)
            term = dot(score_grad, r.km[h])
            query_grad = term if query_grad is None else query_grad + term
            r.dk[...] += dot_tn(score_grad, jnp.where(keep, q, zero_tile))
            r.dv[...] += dot_tn(probs, jnp.where(keep, grad, zero_tile))
        r.pg[rows, :columns] = (query_grad * 0.125).astype(BF16)

    loop(0, seq // tile, attend_back)
    r.pg[:, columns : 2 * columns] = r.dk[...].astype(BF16)
    r.pg[:, 2 * columns :] = r.dv[...].astype(BF16)
    owned_u.reduce()
    weight_grad(r.dj, r.x1, r.pg)
    dj_planes.first(3)

    def first_part(j):
        g = jnp.where(j == 0, 3, jnp.where(j == 3, 0, j))
        chip = at.chip_at(g)
        part = dot_nt(r.pg[rows_of(chip, tile), :], r.wj[...]).astype(BF16)
        r.first[0][2 * chip] = part[:local]
        r.first[0][2 * chip + 1] = part[local:]
        first.to_partner(g).start()

    loop(0, 4, first_part)
    first.first()
    if planes > 2:
        dj_planes.step(2)
    first.second()
    att_gather.waits()
    br_swap.waits()
    weight_grad(r.do, r.attg, r.brg)
    if planes > 1:
        dj_planes.step(1)
    do_planes.first(1)
    owned_u.gather.near()
    feed_total = feed.total()
    r.layer_out[...] = (r.middle[...] + feed_total + params[4:5, :]).astype(BF16)
    owned_j.reduce()
    normed_one_grad = first.total()
    normal, rate = standard(tokens[...].astype(F32))
    sums[0:1, :] = jnp.sum(normed_one_grad * normal, axis=0, keepdims=True)
    sums[1:2, :] = jnp.sum(normed_one_grad, axis=0, keepdims=True)
    r.tokens_grad[...] += standard_grad(normed_one_grad * params[0:1, :], normal, rate)
    r.sum_s[...] = sums[...].astype(BF16)
    sum_swap = Exchange(
        at, lambda c: r.sum_s, lambda c: r.sum_c.at[c], *r.sumc_sem
    )
    sum_swap.start()
    owned_o.reduce()
    owned_u.gather.far()
    owned_j.gather.near()
    sum_swap.waits()

    def add_ctx(d):
        sums[...] += r.sum_c[at.ctx_at(d)].astype(F32)

    loop(1, CTX, add_ctx)
    r.sum_p[...] = sums[...].astype(BF16)
    sum_planes = Planes(
        at, lambda to: r.sum_p, lambda p: r.sum_z.at[p], *r.sumz_sem
    )
    sum_planes.start()
    owned_o.gather.near()
    owned_j.gather.far()
    owned_o.gather.far()
    sum_planes.waits()

    def add_planes(d):
        sums[...] += r.sum_z[at.plane_at(d)].astype(F32)

    loop(1, planes, add_planes)
    r.totals[0:8, :] = pltpu.roll(
        sums[0:8, :], lax.rem((planes - f) * part_rows, width), axis=1
    )
    bias_total = jnp.sum(
        jnp.where(row == 5 + bias_row, sums[...], 0.0), axis=0, keepdims=True
    )
    r.totals[8:16, :] = pltpu.roll(
        jnp.broadcast_to(bias_total, (8, width)), width - lax.rem(f * shard, width), axis=1
    )

    for each in (owned_u, owned_o, owned_j):
        each.gather.waits()
        each.own.wait()
    if full_shard:
        gd_own.wait()
        gd_gather.waits()
        gd_gather.finish()
    else:

        @pl.when(has_down)
        def _():
            gd_own.wait()
            loop(1, CTX, lambda d: gd_copy(d).wait_send())

        def gd_take(b):
            @pl.when(me != lax.rem(f * shard_blocks + b, CTX))
            def _():
                block = r.gd.at[b]
                remote(
                    block, block, r.gd_sem[0].at[0], r.gd_sem[1].at[b], (at.ctx_at(jnp.int32(1)), f)
                ).wait_recv()

        loop(0, shard_blocks, gd_take)

    for each in (
        tok_gather, cot_gather, wo_gather, x2_gather, att_gather, owned_u.gather, owned_o.gather,
        owned_j.gather, ext_swap, att_swap, dat_swap, br_swap, sum_swap, small_planes, wj_planes,
        wo_planes, wu_planes, wd_planes, dd_planes, du_planes, do_planes, dj_planes, sum_planes, back, feed,
        first,
    ):
        each.finish()


def shards(
    tokens,
    segment_ids,
    random_blocks,
    global_blocks,
    first_gain,
    first_bias,
    joint_weight,
    output_weight,
    second_gain,
    second_bias,
    up_weight,
    up_bias,
    down_weight,
    down_bias,
    cotangent,
):
    local, width = tokens.shape[1:]
    ctx, planes = lax.axis_size("ctx"), lax.axis_size("fsdp")
    heads = random_blocks.shape[2]
    seq = local * ctx
    blocks = seq // BLOCK
    part_rows = width // planes
    columns = width // ctx
    ff_shard = up_bias.shape[0]
    ff = ff_shard * planes
    ff_blocks = ff // LANES // ctx
    shard_blocks = ff_shard // LANES
    ff_part = ff // ctx
    assert ctx == CTX and columns == LANES and heads == 2 * ctx and blocks + SEGMENTS <= 64
    assert CTX % shard_blocks == 0 and ff // width == ff_blocks

    vmem, hbm = pl.BlockSpec(memory_space=pltpu.VMEM), pl.BlockSpec(memory_space=pl.ANY)
    inputs = dict(
        tokens=(tokens[0], vmem),
        cotangent=(cotangent[0], vmem),
        segments=(segment_ids, vmem),
        random=(random_blocks[0], vmem),
        globals=(global_blocks, vmem),
        gain_one=(first_gain, vmem),
        bias_one=(first_bias, vmem),
        gain_two=(second_gain, vmem),
        bias_two=(second_bias, vmem),
        bias_up=(up_bias, vmem),
        bias_down=(down_bias, vmem),
        joint=(joint_weight, hbm),
        outw=(output_weight, hbm),
        up=(up_weight, hbm),
        down=(down_weight, hbm),
    )
    outputs = dict(
        layer_out=((local, width), BF16, vmem),
        tokens_grad=((local, width), F32, vmem),
        totals=((16, width), F32, vmem),
        gj=((ctx, part_rows, 3 * columns), BF16, hbm),
        go=((ctx, part_rows, columns), BF16, hbm),
        gu=((ctx, part_rows, ff_part), BF16, hbm),
        gd=((shard_blocks, LANES, width), BF16, hbm),
    )
    dma = lambda n: pltpu.SemaphoreType.DMA((n,))
    v16 = lambda *shape: pltpu.VMEM(shape, BF16)
    v32 = lambda *shape: pltpu.VMEM(shape, F32)
    others = max(planes - 1, 1)
    scatter = (
        v16(ctx, local, width), v16(4, local, width), v16(2, local // 2, width), v16(2, local, width),
        dma(4), dma(4), dma(4), dma(4),
    )
    gather, swap, plane_sems = (dma(8), dma(ctx + 1)), (dma(ctx - 1), dma(ctx)), (dma(others), dma(planes))
    line, toward = (dma(2 * planes), dma(planes)), (dma(planes), dma(planes + 1))
    scratch = dict(
        wj=v16(width, 3 * columns), wo=v16(width, width), wu=v16(width, ff_part),
        wd=v16(ff_part, width), tokg=v16(seq, width), cotg=v16(seq, width),
        x1=v16(seq, width), x2=v16(seq, width), attg=v16(seq, width),
        extras=v16(ctx, local, columns), small=v16(16, width), extg=v16(seq, columns), smallg=v16(planes, 16, width), params=v32(16, width),
        ub=v32(1, ff_part), ubg=v32(1, ff_part), q=v16(seq, columns),
        qa=v16(2, seq, columns), ka=v16(2, seq, columns), km=v16(2, seq, columns),
        vm=v16(2, seq, columns), probs=v16(2, seq, seq), att=v16(seq, columns),
        attx=v16(ctx, local, columns), middle=v32(local, width), n2=v32(local, width),
        rate2=v32(local, LANES), hidden=v16(seq, ff_part),
        upg=v16(seq, ff_part), dat=v16(ctx, local, columns), brs=v16(ctx, local, columns),
        datg=v16(seq, columns), brg=v16(seq, columns), dk=v32(seq, columns),
        dv=v32(seq, columns), pg=v16(seq, 3 * columns), sums=v32(16, width),
        sum_s=v16(16, width), sum_p=v16(16, width), sum_c=v16(ctx, 16, width),
        sum_z=v16(planes, 16, width),
        dj=v16(width, 3 * columns), do=v16(width, columns), du=v16(width, ff_part),
        dwd=v16(ff_blocks, LANES, width),
        rj=v16(planes + 1, part_rows, 3 * columns), ro=v16(planes + 1, part_rows, columns),
        ru=v16(planes + 1, part_rows, ff_part), rd=v16(ff_blocks + 1, LANES, width),
        aj=v32(part_rows, 3 * columns), ao=v32(part_rows, columns), au=v32(part_rows, ff_part), ad=v32(LANES, width), slope=v32(seq, ff_part),
        tj=v16(part_rows, 3 * columns), to=v16(part_rows, columns),
        tu=v16(part_rows, ff_part), td=v16(LANES, width),
        stage=dma(5 + ff_blocks), own=dma(4), wd_sem=(dma(2 * ff_blocks), dma(ff_blocks)),
        dwd_sem=(dma(ff_blocks), dma(ff_blocks + 1)), back=scatter, feed=scatter, first=scatter,
        tok_sem=gather, cot_sem=gather, wog_sem=gather, x2_sem=gather, attg_sem=gather,
        gj_sem=gather, go_sem=gather, gu_sem=gather, gd_sem=gather,
        ext_sem=swap, att_sem=swap, dat_sem=swap, br_sem=swap, sumc_sem=swap,
        small_sem=plane_sems, wj_sem=line, wo_sem=line, wu_sem=line,
        dj_sem=toward, do_sem=toward, du_sem=toward, sumz_sem=plane_sems,
    )
    shapes, scratch_tree = jax.tree.flatten(scratch)
    ins, outs = len(inputs), len(outputs)

    def kernel(*refs):
        held = dict(zip([*inputs, *outputs], refs, strict=False))
        held |= jax.tree.unflatten(scratch_tree, refs[ins + outs :])
        layer_kernel(types.SimpleNamespace(**held), planes)

    layer_out, tokens_grad, totals, gj, go, gu, gd = pl.pallas_call(
        kernel,
        out_shape=[jax.ShapeDtypeStruct(shape, dtype) for shape, dtype, _ in outputs.values()],
        in_specs=[spec for _, spec in inputs.values()],
        out_specs=[spec for *_, spec in outputs.values()],
        scratch_shapes=shapes,
        compiler_params=pltpu.CompilerParams(
            collective_id=0, has_side_effects=True, vmem_limit_bytes=60 * 1024 * 1024
        ),
    )(*(value for value, _ in inputs.values()))

    group = 4

    def spread(ref, out):
        for q in range(group):
            out[:, q * columns : (q + 1) * columns] = ref[q].astype(F32)

    def finish(totals, gj, go, gu, gd, joint, outw, up, down, *vectors):
        for ref, out in ((gj, joint), (go, outw), (gu, up)):
            spread(ref, out)
        down[...] = gd[0].astype(F32)
        for i, out in enumerate(vectors[:5]):
            out[...] = totals[i : i + 1, 0:part_rows].reshape(part_rows)
        vectors[5][...] = totals[8:9, 0:ff_shard].reshape(ff_shard)

    quads = ctx // group
    steps = ff_blocks * quads

    def spec_pair(groups):
        last = groups * quads - 1
        place = lambda i: jnp.minimum(i, last)
        return (
            pl.BlockSpec(
                (group, part_rows, columns), lambda i: (place(i) % quads, 0, place(i) // quads)
            ),
            pl.BlockSpec((part_rows, group * columns), lambda i: (0, place(i))),
        )

    pairs = [spec_pair(3), spec_pair(1), spec_pair(ff_blocks)]
    down_place = lambda i: jnp.minimum(i, shard_blocks - 1)
    whole = pl.BlockSpec(memory_space=pltpu.VMEM)
    made = pl.pallas_call(
        finish,
        grid=(steps,),
        out_shape=[
            jax.ShapeDtypeStruct(shape, F32)
            for shape in (
                (part_rows, 3 * width), (part_rows, width), (part_rows, ff), (ff_shard, width),
                *([(part_rows,)] * 5), (ff_shard,),
            )
        ],
        in_specs=[
            whole,
            *(pair[0] for pair in pairs),
            pl.BlockSpec((1, LANES, width), lambda i: (down_place(i), 0, 0)),
        ],
        out_specs=[
            *(pair[1] for pair in pairs),
            pl.BlockSpec((LANES, width), lambda i: (down_place(i), 0)),
            *([whole] * 6),
        ],
    )(totals, gj, go, gu, gd)
    return (
        layer_out[None],
        tokens_grad[None],
        made[4],
        made[5],
        made[0],
        made[1],
        made[6],
        made[7],
        made[2],
        made[9],
        made[3],
        made[8],
    )


def solution(mesh):
    in_specs = (
        P("fsdp", "ctx", None),
        P("fsdp", "ctx"),
        P("fsdp", "ctx", None, None),
        P("fsdp", None),
        P("fsdp"),
        P("fsdp"),
        P("fsdp", None),
        P("fsdp", None),
        P("fsdp"),
        P("fsdp"),
        P("fsdp", None),
        P("fsdp"),
        P("fsdp", None),
        P("fsdp"),
        P("fsdp", "ctx", None),
    )
    out_specs = (
        P("fsdp", "ctx", None),
        P("fsdp", "ctx", None),
        P("fsdp"),
        P("fsdp"),
        P("fsdp", None),
        P("fsdp", None),
        P("fsdp"),
        P("fsdp"),
        P("fsdp", None),
        P("fsdp"),
        P("fsdp", None),
        P("fsdp"),
    )
    return jax.shard_map(shards, mesh=mesh, in_specs=in_specs, out_specs=out_specs, check_vma=False)
```

```python
import types

import jax
import jax.numpy as jnp
from jax import lax
from jax.experimental import pallas as pl
from jax.experimental.pallas import tpu as pltpu
from jax.sharding import PartitionSpec as P

BLOCK = 64
LANES = 128
CTX = 8
SEGMENTS = 4
EPS = 1e-05
BIG = 1e30
MESH = pl.DeviceIdType.MESH
BF16 = jnp.bfloat16
F32 = jnp.float32


def dot(a, b):
    return lax.dot_general(a, b, (((1,), (0,)), ((), ())), preferred_element_type=F32)


def dot_nt(a, b):
    return lax.dot_general(a, b, (((1,), (1,)), ((), ())), preferred_element_type=F32)


def dot_tn(a, b):
    return lax.dot_general(a, b, (((0,), (0,)), ((), ())), preferred_element_type=F32)


def loop(lower, upper, body):
    lax.fori_loop(lower, upper, lambda i, carry: (body(i), carry)[1], jnp.int32(0))


def rows_of(index, size):
    return pl.ds(pl.multiple_of(index * size, size), size)


def remote(src, dst, send, recv, device):
    return pltpu.make_async_remote_copy(
        src_ref=src,
        dst_ref=dst,
        send_sem=send,
        recv_sem=recv,
        device_id=device,
        device_id_type=MESH,
    )


class Place:
    def __init__(self, planes):
        self.c = lax.axis_index("ctx")
        self.f = lax.axis_index("fsdp")
        self.planes = planes
        self.parity = lax.rem(self.c, 2)
        self.chip = lax.div(self.c, 2)
        self.partner = 2 * self.chip + 1 - self.parity

    def chip_at(self, g):
        low = lax.rem(lax.rem(self.chip, 2) + lax.rem(g, 2), 2)
        high = lax.rem(lax.div(self.chip, 2) + lax.div(g, 2), 2)
        return low + 2 * high

    def same(self, g):
        return 2 * self.chip_at(g) + self.parity

    def other(self, g):
        return 2 * self.chip_at(g) + 1 - self.parity

    def ctx_at(self, d):
        return lax.rem(self.c + d, CTX)

    def plane_at(self, d):
        return lax.rem(self.f + d, self.planes)


class Gather:
    def __init__(self, at, src, slot, send, recv):
        self.at, self.src, self.slot, self.send, self.recv = at, src, slot, send, recv

    def half(self, c, i):
        block = self.slot(c)
        size = block.shape[0] // 2
        return block.at[pl.ds(i * size, size)]

    def direct(self, i):
        at = self.at
        to = at.partner if i == 0 else at.same(jnp.int32(i))
        return remote(self.src, self.slot(at.c), self.send.at[i], self.recv.at[at.c], (to, at.f))

    def across(self, i):
        at = self.at
        c, to = at.same(jnp.int32(1 + i)), at.same(jnp.int32(2 - i))
        block = self.half(c, i)
        recv = self.recv.at[c] if i == 0 else self.recv.at[CTX]
        return remote(block, block, self.send.at[3 + i], recv, (to, at.f))

    def passed(self, g):
        at = self.at
        c = at.same(jnp.int32(g))
        block = self.slot(c)
        return remote(block, block, self.send.at[4 + g], self.recv.at[c], (at.partner, at.f))

    def start(self):
        for i in (1, 2, 0):
            self.direct(i).start()

    def wait(self, c):
        at = self.at
        block = self.slot(c)
        remote(block, block, self.send.at[0], self.recv.at[c], (at.partner, at.f)).wait_recv()

    def near(self, i):
        self.wait(self.at.same(jnp.int32(1 + i)))
        self.across(i).start()
        self.passed(1 + i).start()

    def far(self):
        at = self.at
        for i in range(2):
            c = at.same(jnp.int32(3))
            block = self.half(c, i)
            recv = self.recv.at[c] if i == 0 else self.recv.at[CTX]
            remote(block, block, self.send.at[0], recv, (at.partner, at.f)).wait_recv()
        self.passed(3).start()

    def waits(self):
        loop(0, 4, lambda g: self.wait(self.at.other(g)))

    def finish(self):
        for i in range(3):
            self.direct(i).wait_send()
        for i in range(2):
            self.across(i).wait_send()
        for g in (1, 2, 3):
            self.passed(g).wait_send()


class Exchange:
    def __init__(self, at, src, slot, send, recv):
        self.at, self.src, self.slot, self.send, self.recv = at, src, slot, send, recv

    def copy(self, d):
        at = self.at
        to = at.ctx_at(d)
        return remote(
            self.src(to), self.slot(at.c), self.send.at[d - 1], self.recv.at[at.c], (to, at.f)
        )

    def start(self):
        loop(1, CTX, lambda d: self.copy(d).start())

    def wait(self, d):
        at = self.at
        c = at.ctx_at(d)
        block = self.slot(c)
        remote(block, block, self.send.at[0], self.recv.at[c], (c, at.f)).wait_recv()

    def waits(self):
        loop(1, CTX, self.wait)

    def finish(self):
        loop(1, CTX, lambda d: self.copy(d).wait_send())


class Planes:
    def __init__(self, at, src, slot, send, recv):
        self.at, self.src, self.slot, self.send, self.recv = at, src, slot, send, recv

    def copy(self, d):
        at = self.at
        to = at.plane_at(d)
        return remote(
            self.src(to), self.slot(at.f), self.send.at[d - 1], self.recv.at[at.f], (at.c, to)
        )

    def start(self):
        loop(1, self.at.planes, lambda d: self.copy(d).start())

    def wait(self, d):
        at = self.at
        f = at.plane_at(d)
        block = self.slot(f)
        remote(block, block, self.send.at[0], self.recv.at[f], (at.c, f)).wait_recv()

    def waits(self):
        loop(1, self.at.planes, self.wait)

    def finish(self):
        loop(1, self.at.planes, lambda d: self.copy(d).wait_send())


class Line:
    def __init__(self, at, items, owner, view, send, recv):
        self.at, self.items, self.owner, self.view = at, items, owner, view
        self.send, self.recv = send, recv

    def hop(self, i, up):
        at, block = self.at, self.view(i)
        to = jnp.minimum(at.f + 1, at.planes - 1) if up else jnp.maximum(at.f - 1, 0)
        return remote(
            block, block, self.send.at[2 * i + (1 if up else 0)], self.recv.at[i], (at.c, to)
        )

    def outward(self, i, act):
        at, owner = self.at, self.owner(i)

        @pl.when((owner <= at.f) & (at.f < at.planes - 1))
        def _():
            act(self.hop(i, True))

        @pl.when((owner >= at.f) & (at.f > 0))
        def _():
            act(self.hop(i, False))

    def start(self):
        def each(i):
            @pl.when(self.owner(i) == self.at.f)
            def _():
                self.outward(i, lambda copy: copy.start())

        loop(0, self.items, each)

    def arrive(self, i):
        self.hop(i, True).wait_recv()
        self.outward(i, lambda copy: copy.start())

    def passes(self, d):
        if d == 3:
            loop(3, self.at.planes, self.passes_from)
        elif d < self.at.planes:
            self.passes_from(d)

    def passes_from(self, d):
        def each(i):
            owner = self.owner(i)

            @pl.when((owner == self.at.f + d) | (owner == self.at.f - d))
            def _():
                self.arrive(i)

        loop(0, self.items, each)

    def finish(self):
        loop(0, self.items, lambda i: self.outward(i, lambda copy: copy.wait_send()))


class Toward:
    def __init__(self, at, items, owner, part, taken, send, recv):
        self.at, self.items, self.owner, self.part, self.taken = at, items, owner, part, taken
        self.send, self.recv = send, recv

    def hop(self, i, up):
        at = self.at
        to = jnp.minimum(at.f + 1, at.planes - 1) if up else jnp.maximum(at.f - 1, 0)
        slot = i + 1 if up else i
        return remote(
            self.part(i), self.taken.at[slot], self.send.at[i], self.recv.at[slot], (at.c, to)
        )

    def step(self, d):
        at = self.at
        if d == 3:
            loop(3, at.planes, lambda j: self.step_to(at.planes + 2 - j))
        elif d < at.planes:
            self.step_to(d)

    def step_to(self, d):
        at = self.at

        def one(i, up, comes):
            @pl.when(comes)
            def _():
                self.hop(i, up).wait_recv()
                block = self.part(i)
                come = self.taken[i + 1 if up else i].astype(F32)
                block[...] = (block[...].astype(F32) + come).astype(BF16)

            self.hop(i, up).start()

        def each(i):
            @pl.when(self.owner(i) == at.f + d)
            def _():
                one(i, True, at.f > 0)

            @pl.when(self.owner(i) == at.f - d)
            def _():
                one(i, False, at.f < at.planes - 1)

        loop(0, self.items, each)

    def total(self, i, acc):
        at = self.at
        acc[...] = self.part(i)[...].astype(F32)

        @pl.when(at.f > 0)
        def _():
            self.hop(i, True).wait_recv()
            acc[...] += self.taken[i + 1].astype(F32)

        @pl.when(at.f < at.planes - 1)
        def _():
            self.hop(i, False).wait_recv()
            acc[...] += self.taken[i].astype(F32)

    def finish(self):
        def each(i):
            @pl.when(self.owner(i) > self.at.f)
            def _():
                self.hop(i, True).wait_send()

            @pl.when(self.owner(i) < self.at.f)
            def _():
                self.hop(i, False).wait_send()

        loop(0, self.items, each)


class Scatter:
    def __init__(self, at, part, pair, halves, far, pair_send, pair_recv, send, recv):
        self.at, self.part, self.pair, self.halves, self.far = at, part, pair, halves, far
        self.pair_send, self.pair_recv, self.send, self.recv = pair_send, pair_recv, send, recv
        self.size = part.shape[1] // 2

    def to_partner(self, g):
        at = self.at
        return remote(
            self.part.at[at.other(g)],
            self.pair.at[g],
            self.pair_send.at[g],
            self.pair_recv.at[g],
            (at.partner, at.f),
        )

    def across(self, i):
        at = self.at
        return remote(
            self.part.at[at.same(jnp.int32(3)), pl.ds(i * self.size, self.size)],
            self.halves.at[i],
            self.send.at[i],
            self.recv.at[i],
            (at.same(jnp.int32(1 + i)), at.f),
        )

    def beside(self, i):
        at = self.at
        to = at.same(jnp.int32(1 + i))
        return remote(
            self.part.at[to], self.far.at[i], self.send.at[2 + i], self.recv.at[2 + i], (to, at.f)
        )

    def add_pair(self, g):
        self.to_partner(jnp.int32(g)).wait_recv()
        own = self.at.same(jnp.int32(g))
        both = self.part[own].astype(F32) + self.pair[g].astype(F32)
        self.part[own] = both.astype(BF16)

    def first(self):
        self.add_pair(3)
        for i in range(2):
            self.across(i).start()

    def second(self):
        for i in range(2):
            self.add_pair(1 + i)
        for i in range(2):
            self.across(i).wait_recv()
            to = self.at.same(jnp.int32(2 - i))
            rows = pl.ds(i * self.size, self.size)
            both = self.part[to, rows].astype(F32) + self.halves[i].astype(F32)
            self.part[to, rows] = both.astype(BF16)
            self.beside(1 - i).start()

    def total(self):
        self.to_partner(jnp.int32(0)).wait_recv()
        for i in range(2):
            self.beside(i).wait_recv()
        both = self.part[self.at.c].astype(F32) + self.pair[0].astype(F32)
        return both + (self.far[0].astype(F32) + self.far[1].astype(F32))

    def finish(self):
        loop(0, 4, lambda g: self.to_partner(g).wait_send())
        for i in range(2):
            self.across(i).wait_send()
            self.beside(i).wait_send()


def standard(values):
    centre = jnp.mean(values, axis=-1, keepdims=True)
    offset = values - centre
    spread = jnp.mean(offset * offset, axis=-1, keepdims=True)
    rate = lax.rsqrt(spread + EPS)
    return offset * rate, rate


def standard_grad(e, normal, rate):
    return rate * (
        e - jnp.mean(e, axis=-1, keepdims=True) - normal * jnp.mean(e * normal, axis=-1, keepdims=True)
    )


def write_codes(r, at, seq):
    local = r.segments.shape[1]
    blocks, local_blocks = seq // BLOCK, local // BLOCK
    draws, _, heads = r.random.shape
    half = LANES // 2
    key = lax.rem(lax.broadcasted_iota(jnp.int32, (heads, LANES), 1), half)
    lower = lax.broadcasted_iota(jnp.int32, (1, LANES), 1) < half
    diagonal = lax.broadcasted_iota(jnp.int32, (heads, heads), 0) == lax.broadcasted_iota(
        jnp.int32, (heads, heads), 1
    )
    pair = r.globals[...]
    for b in range(local_blocks):
        block = at.c * local_blocks + b
        counted = jnp.abs(key - block) <= 1
        for j in range(draws):
            row = jnp.broadcast_to(r.random[j, b : b + 1, :].astype(F32), (heads, heads))
            drawn = jnp.sum(jnp.where(diagonal, row, 0.0), axis=1, keepdims=True)
            counted = counted | (key.astype(F32) == drawn)
        for j in range(pair.shape[1]):
            chosen = pair[:, j : j + 1]
            counted = counted | (key == chosen) | (chosen == block)
        code = jnp.where(counted | (key >= blocks), 0.0, -BIG)
        for d in range(heads // 2):
            both = jnp.where(lower, code[2 * d + 1 : 2 * d + 2], code[2 * d : 2 * d + 1])
            r.codes[d, b : b + 1, :] = both
    segments = r.segments[...].astype(F32)
    for d in range(heads // 2):
        r.codes[d, local_blocks : local_blocks + 1, :] = segments


def layer_kernel(r, planes):
    at = Place(planes)
    me, f = at.c, at.f
    tokens, cotangent = r.tokens, r.cotangent
    local, width = tokens.shape
    seq = local * CTX
    blocks, local_blocks = seq // BLOCK, local // BLOCK
    part_rows = width // planes
    columns = width // CTX
    shard = r.down.shape[0]
    ff = planes * shard
    ff_blocks = ff // LANES // CTX
    shard_blocks = shard // LANES
    full_shard = shard_blocks == CTX
    tile = 2 * local
    k_own = lax.div(f * shard_blocks, CTX)
    has_down = lax.div(me, shard_blocks) == lax.rem(f, CTX // shard_blocks)
    down_place = lax.rem(me, shard_blocks)

    def down_owner(k):
        return lax.div(CTX * k + me, shard_blocks)

    my_rows = rows_of(f, part_rows)
    my_columns = rows_of(me, columns)
    my_tokens = rows_of(me, local)

    barrier = pltpu.get_barrier_semaphore()
    loop(
        1,
        CTX,
        lambda d: pl.semaphore_signal(
            barrier, inc=1, device_id=(at.ctx_at(d), f), device_id_type=MESH
        ),
    )
    loop(
        1,
        planes,
        lambda d: pl.semaphore_signal(
            barrier, inc=1, device_id=(me, at.plane_at(d)), device_id_type=MESH
        ),
    )

    stage_j = [
        pltpu.make_async_copy(
            r.joint.at[:, pl.ds(pl.multiple_of(width * j + columns * me, LANES), columns)],
            r.wj.at[my_rows, pl.ds(columns * j, columns)],
            r.stage.at[j],
        )
        for j in range(3)
    ]
    stage_o = pltpu.make_async_copy(
        r.outw.at[:, my_columns], r.wo.at[my_rows, my_columns], r.stage.at[3]
    )
    stage_u = [
        pltpu.make_async_copy(
            r.up.at[:, pl.ds(pl.multiple_of(CTX * LANES * k + LANES * me, LANES), LANES)],
            r.wu.at[my_rows, pl.ds(LANES * k, LANES)],
            r.stage.at[4 + k],
        )
        for k in range(ff_blocks)
    ]
    stage_d = pltpu.make_async_copy(
        r.down.at[rows_of(down_place, LANES), :],
        r.wd.at[rows_of(k_own, LANES), :],
        r.stage.at[4 + ff_blocks],
    )
    for copy in [*stage_j, stage_o, *stage_u]:
        copy.start()

    @pl.when(has_down)
    def _():
        stage_d.start()

    small, short = r.small, r.small.shape[1]
    small[...] = jnp.zeros_like(small)
    for i, vector in enumerate((r.gain_one, r.bias_one, r.gain_two, r.bias_two, r.bias_down)):
        small[i : i + 1, 0:part_rows] = vector[...].astype(F32).reshape(1, part_rows)
    for i in range(shard // short):
        piece = r.bias_up[i * short : (i + 1) * short]
        small[5 + i : 6 + i, :] = piece.astype(F32).reshape(1, short)

    def token_gather(src, dst, sems):
        return Gather(at, src, lambda c: dst.at[rows_of(c, local)], *sems)

    tok = token_gather(tokens, r.tokg, r.tok_sem)
    cot = token_gather(cotangent, r.cotg, r.cot_sem)
    x2 = token_gather(r.x2.at[my_tokens], r.x2, r.x2_sem)
    attg = token_gather(r.attg.at[my_tokens], r.attg, r.attg_sem)
    wog = Gather(
        at, r.wo.at[:, my_columns], lambda c: r.wo.at[:, rows_of(c, columns)], *r.wog_sem
    )
    codes = Exchange(at, lambda c: r.codes.at[c], lambda c: r.codeg.at[c], *r.code_sem)
    att_swap = Exchange(
        at, lambda c: r.att.at[rows_of(c, local)], lambda c: r.attx.at[c], *r.att_sem
    )

    def token_swap(src, dst, sems):
        return Exchange(at, lambda c: src.at[c], lambda c: dst.at[rows_of(c, local)], *sems)

    dat_swap = token_swap(r.dat, r.datg, r.dat_sem)
    br_swap = token_swap(r.brs, r.brg, r.br_sem)
    small_planes = Planes(at, lambda to: small, lambda p: r.smallg.at[p], *r.small_sem)

    def weight_line(ref, sems, width_ds):
        return Line(
            at, planes, lambda i: i, lambda i: ref.at[rows_of(i, part_rows), width_ds], *sems
        )

    wj = weight_line(r.wj, r.wj_sem, slice(None))
    wo = weight_line(r.wo, r.wo_sem, my_columns)
    wu = weight_line(r.wu, r.wu_sem, slice(None))
    wd = Line(at, ff_blocks, down_owner, lambda k: r.wd.at[rows_of(k, LANES), :], *r.wd_sem)
    back, feed, first = (Scatter(at, *group) for group in (r.back, r.feed, r.first))

    def grad_line(grad, taken, sems):
        return Toward(
            at, planes, lambda i: i, lambda i: grad.at[rows_of(i, part_rows), :], taken, *sems
        )

    dd = Toward(at, ff_blocks, down_owner, lambda k: r.dwd.at[k], r.rd, *r.dwd_sem)
    du = grad_line(r.du, r.ru, r.du_sem)
    do = grad_line(r.do, r.ro, r.do_sem)
    dk = grad_line(r.dk, r.rk, r.dk_sem)
    dq = grad_line(r.dq, r.rq, r.dq_sem)

    class Owned:
        def __init__(self, number, line, acc, total, out, sems):
            self.line, self.acc, self.sum = line, acc, total
            self.gather = Gather(at, total, lambda c: out.at[c], *sems)
            self.own = pltpu.make_async_copy(total, out.at[me], r.own.at[number])

        def total(self):
            self.line.total(f, self.acc)
            self.sum[...] = self.acc[...].astype(BF16)
            self.gather.start()
            self.own.start()

        def near(self, i):
            self.gather.near(i)

        def far(self):
            self.gather.far()

        def waits(self):
            self.gather.waits()
            self.own.wait()

        def finish(self):
            self.gather.finish()

    gu = Owned(0, du, r.au, r.tu, r.gu, r.gu_sem)
    go = Owned(1, do, r.ao, r.to, r.go, r.go_sem)
    gk = Owned(2, dk, r.ak, r.tk, r.gk, r.gk_sem)
    gq = Owned(3, dq, r.aq, r.tq, r.gq, r.gq_sem)

    class OwnedDown:
        def __init__(self):
            self.gather = Gather(at, r.td, lambda c: r.gd.at[c], *r.gd_sem)
            self.own = pltpu.make_async_copy(r.td, r.gd.at[down_place], r.own.at[4])

        def copy(self, d):
            send, recv = r.gd_sem
            block = r.gd.at[down_place]
            return remote(r.td, block, send.at[d - 1], recv.at[down_place], (at.ctx_at(d), f))

        def total(self):
            @pl.when(has_down)
            def _():
                dd.total(k_own, r.ad)
                r.td[...] = r.ad[...].astype(BF16)
                self.own.start()
                if not full_shard:
                    loop(1, CTX, lambda d: self.copy(d).start())

            if full_shard:
                self.gather.start()

        def near(self, i):
            if full_shard:
                self.gather.near(i)

        def far(self):
            if full_shard:
                self.gather.far()

        def waits(self):
            @pl.when(has_down)
            def _():
                self.own.wait()

            if full_shard:
                self.gather.waits()
                return

            def take(b):
                @pl.when(me != lax.rem(f * shard_blocks + b, CTX))
                def _():
                    block, (send, recv) = r.gd.at[b], r.gd_sem
                    to = (at.ctx_at(jnp.int32(1)), f)
                    remote(block, block, send.at[0], recv.at[b], to).wait_recv()

            loop(0, shard_blocks, take)

        def finish(self):
            if full_shard:
                self.gather.finish()
                return

            @pl.when(has_down)
            def _():
                loop(1, CTX, lambda d: self.copy(d).wait_send())

    gd = OwnedDown()

    class Sums:
        def __init__(self, own, acc, sent, ctx_in, plane_in, ctx_sems, plane_sems):
            self.own, self.acc, self.sent, self.ctx_in, self.plane_in = own, acc, sent, ctx_in, plane_in
            self.swap = Exchange(at, lambda c: own, lambda c: ctx_in.at[c], *ctx_sems)
            self.planes = Planes(at, lambda to: sent, lambda p: plane_in.at[p], *plane_sems)

        def put(self, row, vector):
            for k in range(width // LANES):
                self.acc[row + k : row + k + 1, :] = vector[:, k * LANES : (k + 1) * LANES]

        def start(self):
            self.own[...] = self.acc[...].astype(BF16)
            self.swap.start()

        def middle(self):
            self.swap.waits()

            def add(d):
                self.acc[...] += self.ctx_in[at.ctx_at(d)].astype(F32)

            loop(1, CTX, add)
            self.sent[...] = self.acc[...].astype(BF16)
            self.planes.start()

        def end(self):
            self.planes.waits()

            def add(d):
                self.acc[...] += self.plane_in[at.plane_at(d)].astype(F32)

            loop(1, planes, add)

        def row(self, row):
            for k in range(width // LANES):
                r.wide[0:1, k * LANES : (k + 1) * LANES] = self.acc[row + k : row + k + 1, :]
            return r.wide[0:1, :]

        def finish(self):
            self.swap.finish()
            self.planes.finish()

    early, late = Sums(*r.early), Sums(*r.late)
    params = r.params

    def open_devices():
        pl.semaphore_wait(barrier, CTX - 1 + planes - 1)
        r.tokg[my_tokens, :] = tokens[...]
        r.cotg[my_tokens, :] = cotangent[...]

    def wj_start():
        for copy in stage_j:
            copy.wait()
        wj.start()

    def wo_start():
        stage_o.wait()
        wo.start()

    def wu_start():
        for copy in stage_u:
            copy.wait()
        wu.start()

    def wd_start():
        @pl.when(has_down)
        def _():
            stage_d.wait()

        wd.start()

    def make_codes():
        write_codes(r, at, seq)
        r.codeg[me] = r.codes[me]

    def take_params():
        r.smallg[f] = small[...]
        small_planes.waits()
        params[...] = jnp.zeros_like(params)
        r.wide[...] = jnp.zeros_like(r.wide)

        def add(p):
            r.wide[:, 0:short] = r.smallg[p, 0:8, :]
            params[...] += pltpu.roll(r.wide[...], p * part_rows, axis=1)

        loop(0, planes, add)
        for k in range(ff_blocks):
            block = CTX * k + me
            place = lax.rem(block, shard_blocks) * LANES
            lanes = pl.ds(pl.multiple_of(lax.rem(place, short), LANES), LANES)
            rows = r.smallg[down_owner(k), :, lanes]
            number = lax.broadcasted_iota(jnp.int32, rows.shape, 0)
            r.ub[0:1, k * LANES : (k + 1) * LANES] = jnp.sum(
                jnp.where(number == 5 + lax.div(place, short), rows, 0.0), axis=0, keepdims=True
            )

    def norm_tokens(g):
        tok.wait(at.other(g))
        rows = rows_of(at.chip_at(g), tile)
        normal, _ = standard(r.tokg[rows, :].astype(F32))
        r.x1[rows, :] = (normal * params[0:1, :] + params[1:2, :]).astype(BF16)

    lane = lax.broadcasted_iota(jnp.int32, (tile, columns), 1)
    low = lane < columns // 2
    zero_tile = jnp.zeros((tile, columns), BF16)

    def project(i):
        rows = rows_of(i, tile)
        projected = dot(r.x1[rows, :], r.wj[...]).astype(BF16)
        q = projected[:, :columns] * jnp.array(0.125, BF16)
        k = projected[:, columns : 2 * columns]
        v = projected[:, 2 * columns :]
        half = lax.rem(lane, columns // 2)
        segment_place = lax.rem(lax.broadcasted_iota(jnp.int32, (LANES, local), 0), LANES // 2) - blocks
        parts = []
        for e in range(2):
            code = r.codeg[2 * i + e]
            hot = jnp.where(
                code[local_blocks : local_blocks + 1] == segment_place.astype(F32), 1.0, 0.0
            ).T
            for b in range(local_blocks):
                parts.append(hot[b * BLOCK : (b + 1) * BLOCK] + code[b : b + 1])
        ext = jnp.concatenate(parts, axis=0)
        token = lax.broadcasted_iota(jnp.int32, (tile, columns), 0) + i * tile
        hot = jnp.where(half == lax.div(token, BLOCK), 1.0, 0.0)
        k_ext = jnp.where(
            half < blocks, hot, jnp.where(half < blocks + SEGMENTS, (1.0 - ext) * -BIG, 0.0)
        ).astype(BF16)
        ext = ext.astype(BF16)
        r.q[rows, :] = q
        r.qa[0, rows, :] = jnp.where(low, q, ext)
        r.qa[1, rows, :] = jnp.where(low, ext, q)
        r.ka[0, rows, :] = jnp.where(low, k, k_ext)
        r.ka[1, rows, :] = jnp.where(low, k_ext, k)
        r.km[0, rows, :] = jnp.where(low, k, zero_tile)
        r.km[1, rows, :] = jnp.where(low, zero_tile, k)
        r.vm[0, rows, :] = jnp.where(low, v, zero_tile)
        r.vm[1, rows, :] = jnp.where(low, zero_tile, v)

    def attend(i):
        rows = rows_of(i, tile)
        out = None
        for h in range(2):
            scores = dot_nt(r.qa[h, rows, :], r.ka[h])
            weights = jnp.exp(scores - jnp.max(scores, axis=1, keepdims=True))
            shares = (weights / jnp.sum(weights, axis=1, keepdims=True)).astype(BF16)
            r.probs[h, rows, :] = shares
            term = dot(shares, r.vm[h])
            out = term if out is None else out + term
        r.att[rows, :] = out.astype(BF16)

    def att_swap_start():
        att_swap.start()
        r.attx[me] = r.att[my_tokens, :]

    def project_out():
        att_swap.waits()
        for c in range(CTX):
            r.attg[my_tokens, c * columns : (c + 1) * columns] = r.attx[c]
        wog.waits()
        middle = tokens[...].astype(F32) + dot(r.attg[my_tokens, :], r.wo[...])
        normal, rate = standard(middle)
        r.middle[...] = middle
        r.n2[...] = normal
        r.rate2[...] = jnp.broadcast_to(rate, r.rate2.shape)
        r.x2[my_tokens, :] = (normal * params[2:3, :] + params[3:4, :]).astype(BF16)

    r.ubg[...] = jnp.zeros_like(r.ubg)

    def hidden_units(g):
        x2.wait(at.other(g))
        rows = rows_of(at.chip_at(g), tile)
        up_sum = dot(r.x2[rows, :], r.wu[...]) + r.ub[...]
        share = 0.5 * (1.0 + lax.erf(up_sum * 0.7071067811865476))
        r.hidden[rows, :] = (up_sum * share).astype(BF16)
        r.slope[rows, :] = share + up_sum * jnp.exp(-0.5 * up_sum * up_sum) * 0.3989422804014327

    def down_grad():
        def one(k):
            r.dwd[k] = dot_tn(r.hidden[:, rows_of(k, LANES)], r.cotg[...]).astype(BF16)

        loop(0, ff_blocks, one)

    def far_first(j):
        return jnp.where(j == 0, 3, jnp.where(j == 3, 0, j))

    def put_part(scatter, g, part):
        chip = at.chip_at(g)
        part = part.astype(BF16)
        scatter.part[2 * chip] = part[:local]
        scatter.part[2 * chip + 1] = part[local:]
        scatter.to_partner(g).start()

    def feed_back(j):
        g = far_first(j)
        rows = rows_of(at.chip_at(g), tile)
        up_grad = (dot_nt(r.cotg[rows, :], r.wd[...]) * r.slope[rows, :]).astype(BF16)
        r.upg[rows, :] = up_grad
        r.ubg[...] += jnp.sum(up_grad.astype(F32), axis=0, keepdims=True)
        put_part(back, g, dot_nt(up_grad, r.wu[...]))

    def feed_part(j):
        g = far_first(j)
        put_part(feed, g, dot(r.hidden[rows_of(at.chip_at(g), tile), :], r.wd[...]))

    def first_part(j):
        g = far_first(j)
        put_part(first, g, dot_nt(r.pg[rows_of(at.chip_at(g), tile), :], r.wj[...]))

    rows_tile = min(tile, width)

    def weight_grad(out, left, right, lanes=slice(None)):
        def body(i):
            out[rows_of(i, rows_tile), :] = dot_tn(
                left[:, rows_of(i, rows_tile)], right[:, lanes]
            ).astype(BF16)

        loop(0, width // rows_tile, body)

    def up_weight_grad():
        weight_grad(r.du, r.x2, r.upg)

    def middle_back():
        normed_two_grad = back.total()
        normal = r.n2[...]
        cot_own = cotangent[...].astype(F32)
        early.acc[...] = jnp.zeros_like(early.acc)
        early.put(0, jnp.sum(normed_two_grad * normal, axis=0, keepdims=True))
        early.put(8, jnp.sum(normed_two_grad, axis=0, keepdims=True))
        early.put(16, jnp.sum(cot_own, axis=0, keepdims=True))
        for k in range(ff_blocks):
            early.acc[pl.ds(24 + CTX * k + me, 1), :] = r.ubg[0:1, k * LANES : (k + 1) * LANES]
        middle_grad = cot_own + standard_grad(
            normed_two_grad * params[2:3, :], normal, r.rate2[:, 0:1]
        )
        r.tokens_grad[...] = middle_grad
        branch = middle_grad.astype(BF16)
        attended_grad = dot_nt(branch, r.wo[...]).astype(BF16)
        for c in range(CTX):
            r.dat[c] = attended_grad[:, c * columns : (c + 1) * columns]
            r.brs[c] = branch[:, c * columns : (c + 1) * columns]
        r.acc_k[...] = jnp.zeros_like(r.acc_k)
        r.acc_v[...] = jnp.zeros_like(r.acc_v)

    def dat_start():
        dat_swap.start()
        r.datg[my_tokens, :] = r.dat[me]

    def br_start():
        br_swap.start()
        r.brg[my_tokens, :] = r.brs[me]

    def attend_back(i):
        rows = rows_of(i, tile)
        grad = r.datg[rows, :]
        both = grad.astype(F32) * r.att[rows, :].astype(F32)
        q = r.q[rows, :]
        query_grad = None
        for h in range(2):
            keep = low if h == 0 else ~low
            delta = jnp.sum(jnp.where(keep, both, 0.0), axis=1, keepdims=True)
            probs = r.probs[h, rows, :]
            prob_grad = dot_nt(grad, r.vm[h])
            score_grad = (probs.astype(F32) * (prob_grad - delta)).astype(BF16)
            term = dot(score_grad, r.km[h])
            query_grad = term if query_grad is None else query_grad + term
            r.acc_k[...] += dot_tn(score_grad, jnp.where(keep, q, zero_tile))
            r.acc_v[...] += dot_tn(probs, jnp.where(keep, grad, zero_tile))
        r.pg[rows, :columns] = (query_grad * 0.125).astype(BF16)

    def keys_back():
        r.pg[:, columns : 2 * columns] = r.acc_k[...].astype(BF16)
        r.pg[:, 2 * columns :] = r.acc_v[...].astype(BF16)

    def key_weight_grad():
        weight_grad(r.dk, r.x1, r.pg, slice(columns, None))

    def query_weight_grad():
        weight_grad(r.dq, r.x1, r.pg, slice(0, columns))

    def out_weight_grad():
        attg.waits()
        br_swap.waits()
        weight_grad(r.do, r.attg, r.brg)

    def layer_end():
        r.layer_out[...] = (r.middle[...] + feed.total() + params[4:5, :]).astype(BF16)

    def tokens_back():
        normed_one_grad = first.total()
        normal, rate = standard(tokens[...].astype(F32))
        late.put(0, jnp.sum(normed_one_grad * normal, axis=0, keepdims=True))
        late.put(8, jnp.sum(normed_one_grad, axis=0, keepdims=True))
        r.tokens_grad[...] += standard_grad(normed_one_grad * params[0:1, :], normal, rate)

    def write_totals():
        for i, (sums, row) in enumerate(((late, 0), (late, 8), (early, 0), (early, 8), (early, 16))):
            vector = jnp.broadcast_to(sums.row(row), (8, width))
            turned = pltpu.roll(vector, lax.rem((planes - f) * part_rows, width), axis=1)
            r.totals[i : i + 1, :] = turned[0:1]
        for k in range(shard_blocks):
            r.totals[5:6, k * LANES : (k + 1) * LANES] = early.acc[
                pl.ds(24 + f * shard_blocks + k, 1), :
            ]

    open_devices()
    tok.start()
    wj_start()
    wo_start()
    wo.passes(1)
    small_planes.start()
    cot.start()
    take_params()
    wj.passes(1)
    tok.near(0)
    wo.passes(2)
    tok.near(1)
    make_codes()
    codes.start()
    wj.passes(2)

    def step_1(i):

        @pl.when(i == 2)
        def _():
            wu_start()
            tok.far()
            cot.near(0)

        @pl.when(i == 3)
        def _():
            wo.passes(3)
            wog.start()

        norm_tokens(i)

    loop(0, 4, step_1)

    codes.waits()
    wj.passes(3)

    def step_2(i):

        @pl.when(i == 1)
        def _():
            cot.near(1)

        project(i)

    loop(0, 4, step_2)


    def step_3(i):

        @pl.when(i == 2)
        def _():
            wu.passes(1)
            wog.near(1)
            cot.far()
            wog.near(0)

        attend(i)

    loop(0, 4, step_3)

    att_swap_start()
    wd_start()
    wog.far()
    wu.passes(2)
    project_out()
    x2.start()
    wd.passes(1)
    x2.near(0)
    x2.near(1)
    wu.passes(3)

    def step_4(i):

        @pl.when(i == 2)
        def _():
            attg.start()
            wd.passes(2)
            x2.far()

        hidden_units(i)

    loop(0, 4, step_4)

    cot.waits()
    down_grad()
    wd.passes(3)
    attg.near(0)
    attg.near(1)
    dd.step(3)
    feed_back(jnp.int32(0))
    feed_part(jnp.int32(0))
    back.first()

    def step_5(i):

        @pl.when(i == 3)
        def _():
            back.second()
            dd.step(2)

        feed_back(i)

    loop(1, 4, step_5)

    up_weight_grad()
    du.step(3)
    middle_back()
    dat_start()
    dd.step(1)
    loop(1, 3, feed_part)
    feed.first()
    br_start()
    dat_swap.waits()

    def step_6(i):

        @pl.when(i == 1)
        def _():
            du.step(2)
            gd.total()

        @pl.when(i == 2)
        def _():
            feed.second()

        @pl.when(i == 3)
        def _():
            du.step(1)
            early.start()

        attend_back(i)

    loop(0, 4, step_6)

    keys_back()

    def step_7(i):

        @pl.when(i == 1)
        def _():
            query_weight_grad()

        @pl.when(i == 2)
        def _():
            key_weight_grad()
            dk.step(3)
            attg.far()
            first.first()
            early.middle()
            out_weight_grad()
            dk.step(2)
            dq.step(3)
            gd.near(0)
            gd.near(1)

        first_part(i)

    loop(0, 3, step_7)

    first.second()
    dq.step(2)
    gu.total()
    dk.step(1)
    do.step(3)
    dq.step(1)
    do.step(2)
    feed_part(jnp.int32(3))
    gk.total()
    gq.total()
    first_part(jnp.int32(3))
    early.end()
    do.step(1)
    gu.near(1)
    go.total()
    gu.near(0)
    gq.near(1)
    tokens_back()
    gk.near(0)
    gk.near(1)
    late.start()
    go.near(0)
    gd.far()
    gq.near(0)
    late.middle()
    go.near(1)
    gu.far()
    gk.far()
    go.far()
    layer_end()
    gq.far()
    late.end()
    for each in (gd, gu, go, gk, gq):
        each.waits()
    write_totals()
    for each in (
        tok, cot, wog, x2, attg, gu, go, gk, gq, gd, codes, att_swap, dat_swap, br_swap, early, late,
        small_planes, wj, wo, wu, wd, dd, du, do, dk, dq, back, feed, first,
    ):
        each.finish()


def shards(
    tokens,
    segment_ids,
    random_blocks,
    global_blocks,
    first_gain,
    first_bias,
    joint_weight,
    output_weight,
    second_gain,
    second_bias,
    up_weight,
    up_bias,
    down_weight,
    down_bias,
    cotangent,
):
    local, width = tokens.shape[1:]
    ctx, planes = lax.axis_size("ctx"), lax.axis_size("fsdp")
    heads = random_blocks.shape[2]
    seq = local * ctx
    blocks = seq // BLOCK
    part_rows = width // planes
    columns = width // ctx
    ff_shard = up_bias.shape[0]
    ff = ff_shard * planes
    ff_blocks = ff // LANES // ctx
    shard_blocks = ff_shard // LANES
    ff_part = ff // ctx
    assert ctx == CTX and columns == LANES and heads == 2 * ctx and blocks + SEGMENTS <= 64
    assert CTX % shard_blocks == 0 and ff // width == ff_blocks

    vmem, hbm = pl.BlockSpec(memory_space=pltpu.VMEM), pl.BlockSpec(memory_space=pl.ANY)
    inputs = dict(
        tokens=(tokens[0], vmem),
        cotangent=(cotangent[0], vmem),
        segments=(segment_ids, vmem),
        random=(random_blocks[0].transpose(2, 0, 1), vmem),
        globals=(global_blocks, vmem),
        gain_one=(first_gain, vmem),
        bias_one=(first_bias, vmem),
        gain_two=(second_gain, vmem),
        bias_two=(second_bias, vmem),
        bias_up=(up_bias, vmem),
        bias_down=(down_bias, vmem),
        joint=(joint_weight, hbm),
        outw=(output_weight, hbm),
        up=(up_weight, hbm),
        down=(down_weight, hbm),
    )
    outputs = dict(
        layer_out=((local, width), BF16, vmem),
        tokens_grad=((local, width), F32, vmem),
        totals=((8, width), F32, vmem),
        gk=((ctx, part_rows, 2 * columns), BF16, hbm),
        gq=((ctx, part_rows, columns), BF16, hbm),
        go=((ctx, part_rows, columns), BF16, hbm),
        gu=((ctx, part_rows, ff_part), BF16, hbm),
        gd=((shard_blocks, LANES, width), BF16, hbm),
    )
    dma = lambda n: pltpu.SemaphoreType.DMA((n,))
    v16 = lambda *shape: pltpu.VMEM(shape, BF16)
    v32 = lambda *shape: pltpu.VMEM(shape, F32)
    others = max(planes - 1, 1)
    scatter = (
        v16(ctx, local, width), v16(4, local, width), v16(2, local // 2, width), v16(2, local, width),
        dma(4), dma(4), dma(4), dma(4),
    )
    gather, swap, plane_sems = (dma(8), dma(ctx + 1)), (dma(ctx - 1), dma(ctx)), (dma(others), dma(planes))
    line, toward = (dma(2 * planes), dma(planes)), (dma(planes), dma(planes + 1))
    short = max(part_rows, LANES)
    vectors = lambda rows: (
        v16(rows, LANES), v32(rows, LANES), v16(rows, LANES), v16(ctx, rows, LANES),
        v16(planes, rows, LANES), swap, plane_sems,
    )
    scratch = dict(
        wj=v16(width, 3 * columns), wo=v16(width, width), wu=v16(width, ff_part),
        wd=v16(ff_part, width), tokg=v16(seq, width), cotg=v16(seq, width),
        x1=v16(seq, width), x2=v16(seq, width), attg=v16(seq, width),
        codes=v32(ctx, 8, LANES), codeg=v32(ctx, 8, LANES), small=v32(16, short),
        smallg=v32(planes, 16, short), params=v32(8, width), wide=v32(8, width),
        ub=v32(1, ff_part), ubg=v32(1, ff_part), q=v16(seq, columns),
        qa=v16(2, seq, columns), ka=v16(2, seq, columns), km=v16(2, seq, columns),
        vm=v16(2, seq, columns), probs=v16(2, seq, seq), att=v16(seq, columns),
        attx=v16(ctx, local, columns), middle=v32(local, width), n2=v32(local, width),
        rate2=v32(local, LANES), hidden=v16(seq, ff_part), slope=v32(seq, ff_part),
        upg=v16(seq, ff_part), dat=v16(ctx, local, columns), brs=v16(ctx, local, columns),
        datg=v16(seq, columns), brg=v16(seq, columns), acc_k=v32(seq, columns),
        acc_v=v32(seq, columns), pg=v16(seq, 3 * columns), early=vectors(64), late=vectors(16),
        dk=v16(width, 2 * columns), dq=v16(width, columns), do=v16(width, columns),
        du=v16(width, ff_part), dwd=v16(ff_blocks, LANES, width),
        rk=v16(planes + 1, part_rows, 2 * columns), rq=v16(planes + 1, part_rows, columns),
        ro=v16(planes + 1, part_rows, columns), ru=v16(planes + 1, part_rows, ff_part),
        rd=v16(ff_blocks + 1, LANES, width),
        ak=v32(part_rows, 2 * columns), aq=v32(part_rows, columns), ao=v32(part_rows, columns),
        au=v32(part_rows, ff_part), ad=v32(LANES, width),
        tk=v16(part_rows, 2 * columns), tq=v16(part_rows, columns), to=v16(part_rows, columns),
        tu=v16(part_rows, ff_part), td=v16(LANES, width),
        stage=dma(5 + ff_blocks), own=dma(5), wd_sem=(dma(2 * ff_blocks), dma(ff_blocks)),
        dwd_sem=(dma(ff_blocks), dma(ff_blocks + 1)), back=scatter, feed=scatter, first=scatter,
        tok_sem=gather, cot_sem=gather, wog_sem=gather, x2_sem=gather, attg_sem=gather,
        gk_sem=gather, gq_sem=gather, go_sem=gather, gu_sem=gather, gd_sem=gather,
        code_sem=swap, att_sem=swap, dat_sem=swap, br_sem=swap,
        small_sem=plane_sems, wj_sem=line, wo_sem=line, wu_sem=line,
        dk_sem=toward, dq_sem=toward, do_sem=toward, du_sem=toward,
    )
    shapes, scratch_tree = jax.tree.flatten(scratch)
    ins, outs = len(inputs), len(outputs)

    def kernel(*refs):
        held = dict(zip([*inputs, *outputs], refs, strict=False))
        held |= jax.tree.unflatten(scratch_tree, refs[ins + outs :])
        layer_kernel(types.SimpleNamespace(**held), planes)

    layer_out, tokens_grad, totals, gk, gq, go, gu, gd = pl.pallas_call(
        kernel,
        out_shape=[jax.ShapeDtypeStruct(shape, dtype) for shape, dtype, _ in outputs.values()],
        in_specs=[spec for _, spec in inputs.values()],
        out_specs=[spec for *_, spec in outputs.values()],
        scratch_shapes=shapes,
        compiler_params=pltpu.CompilerParams(
            collective_id=0, has_side_effects=True, vmem_limit_bytes=60 * 1024 * 1024
        ),
    )(*(value for value, _ in inputs.values()))

    group = 4
    quads = ctx // group
    steps = ff_blocks * quads

    def spread(ref, out):
        for q in range(group):
            out[:, q * columns : (q + 1) * columns] = ref[q].astype(F32)

    def finish(out_in, grad_in, totals, gk, gq, go, gu, gd, joint, outw, up, down, out, grad, *vectors):
        step = pl.program_id(0)

        @pl.when(step < quads)
        def _():
            spread(gq, joint)
            spread(go, outw)

        @pl.when((step >= quads) & (step < 3 * quads))
        def _():
            spread(gk, joint)

        spread(gu, up)
        down[...] = gd[0].astype(F32)
        out[...] = out_in[...]
        grad[...] = grad_in[...]
        for i, vector in enumerate(vectors[:5]):
            vector[...] = totals[i : i + 1, 0:part_rows].reshape(part_rows)
        vectors[5][...] = totals[5:6, 0:ff_shard].reshape(ff_shard)

    def from_places(start, count):
        place = lambda i: jnp.clip(i - start, 0, count - 1)
        return pl.BlockSpec(
            (group, part_rows, columns), lambda i: (place(i) % quads, 0, place(i) // quads)
        )

    def to_columns(count):
        return pl.BlockSpec((part_rows, group * columns), lambda i: (0, jnp.minimum(i, count - 1)))

    down_place = lambda i: jnp.minimum(i, shard_blocks - 1)
    whole = pl.BlockSpec(memory_space=pltpu.VMEM)
    tokens_spec = pl.BlockSpec((local // steps, width), lambda i: (i, 0))
    made = pl.pallas_call(
        finish,
        grid=(steps,),
        out_shape=[
            jax.ShapeDtypeStruct(shape, dtype)
            for shape, dtype in (
                ((part_rows, 3 * width), F32), ((part_rows, width), F32), ((part_rows, ff), F32),
                ((ff_shard, width), F32), ((local, width), BF16), ((local, width), F32),
                *([((part_rows,), F32)] * 5), ((ff_shard,), F32),
            )
        ],
        in_specs=[
            tokens_spec,
            tokens_spec,
            whole,
            from_places(quads, 2 * quads),
            from_places(0, quads),
            from_places(0, quads),
            from_places(0, steps),
            pl.BlockSpec((1, LANES, width), lambda i: (down_place(i), 0, 0)),
        ],
        out_specs=[
            to_columns(3 * quads),
            to_columns(quads),
            to_columns(steps),
            pl.BlockSpec((LANES, width), lambda i: (down_place(i), 0)),
            tokens_spec,
            tokens_spec,
            *([whole] * 6),
        ],
    )(layer_out, tokens_grad, totals, gk, gq, go, gu, gd)
    return (
        made[4][None],
        made[5][None],
        made[6],
        made[7],
        made[0],
        made[1],
        made[8],
        made[9],
        made[2],
        made[11],
        made[3],
        made[10],
    )


def solution(mesh):
    in_specs = (
        P("fsdp", "ctx", None),
        P("fsdp", "ctx"),
        P("fsdp", "ctx", None, None),
        P("fsdp", None),
        P("fsdp"),
        P("fsdp"),
        P("fsdp", None),
        P("fsdp", None),
        P("fsdp"),
        P("fsdp"),
        P("fsdp", None),
        P("fsdp"),
        P("fsdp", None),
        P("fsdp"),
        P("fsdp", "ctx", None),
    )
    out_specs = (
        P("fsdp", "ctx", None),
        P("fsdp", "ctx", None),
        P("fsdp"),
        P("fsdp"),
        P("fsdp", None),
        P("fsdp", None),
        P("fsdp"),
        P("fsdp"),
        P("fsdp", None),
        P("fsdp"),
        P("fsdp", None),
        P("fsdp"),
    )
    return jax.shard_map(shards, mesh=mesh, in_specs=in_specs, out_specs=out_specs, check_vma=False)
```

```python
import types

import jax
import jax.numpy as jnp
from jax import lax
from jax.experimental import pallas as pl
from jax.experimental.pallas import tpu as pltpu
from jax.sharding import PartitionSpec as P

BLOCK = 64
LANES = 128
CTX = 8
SEGMENTS = 4
EPS = 1e-05
BIG = 1e30
MESH = pl.DeviceIdType.MESH
BF16 = jnp.bfloat16
F32 = jnp.float32


def dot(a, b):
    return lax.dot_general(a, b, (((1,), (0,)), ((), ())), preferred_element_type=F32)


def dot_nt(a, b):
    return lax.dot_general(a, b, (((1,), (1,)), ((), ())), preferred_element_type=F32)


def dot_tn(a, b):
    return lax.dot_general(a, b, (((0,), (0,)), ((), ())), preferred_element_type=F32)


def loop(lower, upper, body):
    lax.fori_loop(lower, upper, lambda i, carry: (body(i), carry)[1], jnp.int32(0))


def rows_of(index, size):
    return pl.ds(pl.multiple_of(index * size, size), size)


def remote(src, dst, send, recv, device):
    return pltpu.make_async_remote_copy(
        src_ref=src,
        dst_ref=dst,
        send_sem=send,
        recv_sem=recv,
        device_id=device,
        device_id_type=MESH,
    )


class Place:
    def __init__(self, planes):
        self.c = lax.axis_index("ctx")
        self.f = lax.axis_index("fsdp")
        self.planes = planes
        self.parity = lax.rem(self.c, 2)
        self.chip = lax.div(self.c, 2)
        self.partner = 2 * self.chip + 1 - self.parity

    def chip_at(self, g):
        low = lax.rem(lax.rem(self.chip, 2) + lax.rem(g, 2), 2)
        high = lax.rem(lax.div(self.chip, 2) + lax.div(g, 2), 2)
        return low + 2 * high

    def same(self, g):
        return 2 * self.chip_at(g) + self.parity

    def other(self, g):
        return 2 * self.chip_at(g) + 1 - self.parity

    def ctx_at(self, d):
        return lax.rem(self.c + d, CTX)

    def plane_at(self, d):
        return lax.rem(self.f + d, self.planes)


class Gather:
    def __init__(self, at, src, slot, bulk, send, recv):
        self.at, self.src, self.slot, self.bulk = at, src, slot, bulk
        self.send, self.recv = send.at[0], recv

    def half(self, c, i):
        block = self.slot(c)
        size = block.shape[0] // 2
        return block.at[pl.ds(i * size, size)]

    def direct(self, i):
        at = self.at
        to = at.partner if i == 0 else at.same(jnp.int32(i))
        return remote(self.src, self.slot(at.c), self.send, self.recv.at[at.c], (to, at.f))

    def across(self, i):
        at = self.at
        c, to = at.same(jnp.int32(1 + i)), at.same(jnp.int32(2 - i))
        block = self.half(c, i)
        recv = self.recv.at[c] if i == 0 else self.recv.at[CTX]
        return remote(block, block, self.send, recv, (to, at.f))

    def passed(self, g):
        at = self.at
        c = at.same(jnp.int32(g))
        block = self.slot(c)
        return remote(block, block, self.send, self.recv.at[c], (at.partner, at.f))

    def start(self):
        for i in (1, 2, 0):
            self.direct(i).start()

    def wait(self, c):
        at = self.at
        block = self.slot(c)
        remote(block, block, self.send, self.recv.at[c], (at.partner, at.f)).wait_recv()

    def near(self, i):
        self.wait(self.at.same(jnp.int32(1 + i)))
        self.across(i).start()
        self.passed(1 + i).start()

    def far(self):
        at = self.at
        for i in range(2):
            c = at.same(jnp.int32(3))
            block = self.half(c, i)
            recv = self.recv.at[c] if i == 0 else self.recv.at[CTX]
            remote(block, block, self.send, recv, (at.partner, at.f)).wait_recv()
        self.passed(3).start()

    def waits(self):
        loop(0, 4, lambda g: self.wait(self.at.other(g)))

    def finish(self):
        remote(self.bulk, self.bulk, self.send, self.recv.at[0], (self.at.partner, self.at.f)).wait_send()


class Exchange:
    def __init__(self, at, src, slot, bulk, send, recv):
        self.at, self.src, self.slot, self.bulk = at, src, slot, bulk
        self.send, self.recv = send.at[0], recv.at[0]

    def copy(self, d):
        at = self.at
        to = at.ctx_at(d)
        return remote(self.src(to), self.slot(at.c), self.send, self.recv, (to, at.f))

    def start(self):
        loop(1, CTX, lambda d: self.copy(d).start())

    def whole(self):
        return remote(self.bulk, self.bulk, self.send, self.recv, (self.at.partner, self.at.f))

    def waits(self):
        self.whole().wait_recv()

    def finish(self):
        self.whole().wait_send()


class Planes:
    def __init__(self, at, src, slot, bulk, send, recv):
        self.at, self.src, self.slot, self.bulk = at, src, slot, bulk
        self.send, self.recv = send.at[0], recv.at[0]

    def copy(self, d):
        at = self.at
        to = at.plane_at(d)
        return remote(self.src(to), self.slot(at.f), self.send, self.recv, (at.c, to))

    def start(self):
        loop(1, self.at.planes, lambda d: self.copy(d).start())

    def whole(self):
        at = self.at
        to = at.plane_at(jnp.int32(1))
        return remote(self.bulk, self.bulk, self.send, self.recv, (at.c, to))

    def waits(self):
        self.whole().wait_recv()

    def finish(self):
        self.whole().wait_send()


class Line:
    def __init__(self, at, items, owner, view, send, recv):
        self.at, self.items, self.owner, self.view = at, items, owner, view
        self.send, self.recv = send, recv

    def hop(self, i, up):
        at, block = self.at, self.view(i)
        to = jnp.minimum(at.f + 1, at.planes - 1) if up else jnp.maximum(at.f - 1, 0)
        return remote(
            block, block, self.send.at[2 * i + (1 if up else 0)], self.recv.at[i], (at.c, to)
        )

    def outward(self, i, act):
        at, owner = self.at, self.owner(i)

        @pl.when((owner <= at.f) & (at.f < at.planes - 1))
        def _():
            act(self.hop(i, True))

        @pl.when((owner >= at.f) & (at.f > 0))
        def _():
            act(self.hop(i, False))

    def start(self):
        def each(i):
            @pl.when(self.owner(i) == self.at.f)
            def _():
                self.outward(i, lambda copy: copy.start())

        loop(0, self.items, each)

    def arrive(self, i):
        self.hop(i, True).wait_recv()
        self.outward(i, lambda copy: copy.start())

    def passes(self, d):
        if d == 3:
            loop(3, self.at.planes, self.passes_from)
        elif d < self.at.planes:
            self.passes_from(d)

    def passes_from(self, d):
        def each(i):
            owner = self.owner(i)

            @pl.when((owner == self.at.f + d) | (owner == self.at.f - d))
            def _():
                self.arrive(i)

        loop(0, self.items, each)

    def finish(self):
        loop(0, self.items, lambda i: self.outward(i, lambda copy: copy.wait_send()))


class Toward:
    def __init__(self, at, items, owner, part, taken, send, recv):
        self.at, self.items, self.owner, self.part, self.taken = at, items, owner, part, taken
        self.send, self.recv = send, recv

    def hop(self, i, up):
        at = self.at
        to = jnp.minimum(at.f + 1, at.planes - 1) if up else jnp.maximum(at.f - 1, 0)
        slot = i + 1 if up else i
        return remote(
            self.part(i), self.taken.at[slot], self.send.at[i], self.recv.at[slot], (at.c, to)
        )

    def step(self, d):
        at = self.at
        if d == 3:
            loop(3, at.planes, lambda j: self.step_to(at.planes + 2 - j))
        elif d < at.planes:
            self.step_to(d)

    def step_to(self, d):
        at = self.at

        def one(i, up, comes):
            @pl.when(comes)
            def _():
                self.hop(i, up).wait_recv()
                block = self.part(i)
                come = self.taken[i + 1 if up else i].astype(F32)
                block[...] = (block[...].astype(F32) + come).astype(BF16)

            self.hop(i, up).start()

        def each(i):
            @pl.when(self.owner(i) == at.f + d)
            def _():
                one(i, True, at.f > 0)

            @pl.when(self.owner(i) == at.f - d)
            def _():
                one(i, False, at.f < at.planes - 1)

        loop(0, self.items, each)

    def total(self, i, acc):
        at = self.at
        acc[...] = self.part(i)[...].astype(F32)

        @pl.when(at.f > 0)
        def _():
            self.hop(i, True).wait_recv()
            acc[...] += self.taken[i + 1].astype(F32)

        @pl.when(at.f < at.planes - 1)
        def _():
            self.hop(i, False).wait_recv()
            acc[...] += self.taken[i].astype(F32)

    def finish(self):
        def each(i):
            @pl.when(self.owner(i) > self.at.f)
            def _():
                self.hop(i, True).wait_send()

            @pl.when(self.owner(i) < self.at.f)
            def _():
                self.hop(i, False).wait_send()

        loop(0, self.items, each)


class Scatter:
    def __init__(self, at, part, pair, halves, far, send, pair_recv, recv):
        self.at, self.part, self.pair, self.halves, self.far = at, part, pair, halves, far
        self.send, self.pair_recv, self.recv = send.at[0], pair_recv, recv
        self.size = part.shape[1] // 2

    def to_partner(self, g):
        at = self.at
        return remote(
            self.part.at[at.other(g)],
            self.pair.at[g],
            self.send,
            self.pair_recv.at[g],
            (at.partner, at.f),
        )

    def across(self, i):
        at = self.at
        return remote(
            self.part.at[at.same(jnp.int32(3)), pl.ds(i * self.size, self.size)],
            self.halves.at[i],
            self.send,
            self.recv.at[i],
            (at.same(jnp.int32(1 + i)), at.f),
        )

    def beside(self, i):
        at = self.at
        to = at.same(jnp.int32(1 + i))
        return remote(
            self.part.at[to], self.far.at[i], self.send, self.recv.at[2 + i], (to, at.f)
        )

    def add_pair(self, g):
        self.to_partner(jnp.int32(g)).wait_recv()
        own = self.at.same(jnp.int32(g))
        both = self.part[own].astype(F32) + self.pair[g].astype(F32)
        self.part[own] = both.astype(BF16)

    def first(self):
        self.add_pair(3)
        for i in range(2):
            self.across(i).start()

    def second(self):
        for i in range(2):
            self.add_pair(1 + i)
        for i in range(2):
            self.across(i).wait_recv()
            to = self.at.same(jnp.int32(2 - i))
            rows = pl.ds(i * self.size, self.size)
            both = self.part[to, rows].astype(F32) + self.halves[i].astype(F32)
            self.part[to, rows] = both.astype(BF16)
            self.beside(1 - i).start()

    def total(self):
        self.to_partner(jnp.int32(0)).wait_recv()
        for i in range(2):
            self.beside(i).wait_recv()
        both = self.part[self.at.c].astype(F32) + self.pair[0].astype(F32)
        return both + (self.far[0].astype(F32) + self.far[1].astype(F32))

    def finish(self):
        at, blocks = self.at, self.part.at[pl.ds(0, CTX - 1)]
        remote(blocks, blocks, self.send, self.recv.at[0], (at.partner, at.f)).wait_send()


def standard(values):
    centre = jnp.mean(values, axis=-1, keepdims=True)
    offset = values - centre
    spread = jnp.mean(offset * offset, axis=-1, keepdims=True)
    rate = lax.rsqrt(spread + EPS)
    return offset * rate, rate


def standard_grad(e, normal, rate):
    return rate * (
        e - jnp.mean(e, axis=-1, keepdims=True) - normal * jnp.mean(e * normal, axis=-1, keepdims=True)
    )


def write_codes(r, at, seq):
    local = r.segments.shape[1]
    blocks, local_blocks = seq // BLOCK, local // BLOCK
    draws, _, heads = r.random.shape
    half = LANES // 2
    key = lax.rem(lax.broadcasted_iota(jnp.int32, (heads, LANES), 1), half)
    lower = lax.broadcasted_iota(jnp.int32, (1, LANES), 1) < half
    diagonal = lax.broadcasted_iota(jnp.int32, (heads, heads), 0) == lax.broadcasted_iota(
        jnp.int32, (heads, heads), 1
    )
    pair = r.globals[...]
    for b in range(local_blocks):
        block = at.c * local_blocks + b
        counted = jnp.abs(key - block) <= 1
        for j in range(draws):
            row = jnp.broadcast_to(r.random[j, b : b + 1, :].astype(F32), (heads, heads))
            drawn = jnp.sum(jnp.where(diagonal, row, 0.0), axis=1, keepdims=True)
            counted = counted | (key.astype(F32) == drawn)
        for j in range(pair.shape[1]):
            chosen = pair[:, j : j + 1]
            counted = counted | (key == chosen) | (chosen == block)
        code = jnp.where(counted | (key >= blocks), 0.0, -BIG)
        for d in range(heads // 2):
            both = jnp.where(lower, code[2 * d + 1 : 2 * d + 2], code[2 * d : 2 * d + 1])
            r.codes[d, b : b + 1, :] = both
    segments = r.segments[...].astype(F32)
    for d in range(heads // 2):
        r.codes[d, local_blocks : local_blocks + 1, :] = segments


def layer_kernel(r, planes):
    at = Place(planes)
    me, f = at.c, at.f
    local, width = r.tokens_in.shape
    seq = local * CTX
    blocks, local_blocks = seq // BLOCK, local // BLOCK
    part_rows = width // planes
    columns = width // CTX
    shard = r.down.shape[0]
    ff = planes * shard
    ff_blocks = ff // LANES // CTX
    shard_blocks = shard // LANES
    full_shard = shard_blocks == CTX
    tile = 2 * local
    k_own = lax.div(f * shard_blocks, CTX)
    has_down = lax.div(me, shard_blocks) == lax.rem(f, CTX // shard_blocks)
    down_place = lax.rem(me, shard_blocks)

    def down_owner(k):
        return lax.div(CTX * k + me, shard_blocks)

    my_rows = rows_of(f, part_rows)
    my_columns = rows_of(me, columns)
    my_tokens = rows_of(me, local)
    tokens, cotangent = r.tokg.at[my_tokens], r.cotg.at[my_tokens]

    barrier = pltpu.get_barrier_semaphore()
    loop(
        1,
        CTX,
        lambda d: pl.semaphore_signal(
            barrier, inc=1, device_id=(at.ctx_at(d), f), device_id_type=MESH
        ),
    )
    loop(
        1,
        planes,
        lambda d: pl.semaphore_signal(
            barrier, inc=1, device_id=(me, at.plane_at(d)), device_id_type=MESH
        ),
    )

    fetched = (
        (r.tokens_in, tokens), (r.gain_one_in, r.gain_one), (r.bias_one_in, r.bias_one),
        (r.gain_two_in, r.gain_two), (r.bias_two_in, r.bias_two), (r.bias_down_in, r.bias_down),
        (r.bias_up_in, r.bias_up), (r.segments_in, r.segments), (r.random_in, r.random),
        (r.globals_in, r.globals), (r.cotangent_in, cotangent),
    )
    fetch = [
        pltpu.make_async_copy(src, dst, r.fetch.at[i]) for i, (src, dst) in enumerate(fetched)
    ]
    for copy in fetch:
        copy.start()
    layer_copy = pltpu.make_async_copy(r.layer, r.layer_out, r.fetch.at[len(fetch)])
    grad_copy = pltpu.make_async_copy(r.grad, r.tokens_grad, r.fetch.at[len(fetch) + 1])
    totals_copy = pltpu.make_async_copy(r.sums, r.totals, r.fetch.at[len(fetch) + 2])
    stage_j = [
        pltpu.make_async_copy(
            r.joint.at[:, pl.ds(pl.multiple_of(width * j + columns * me, LANES), columns)],
            r.wj.at[my_rows, pl.ds(columns * j, columns)],
            r.stage.at[j],
        )
        for j in range(3)
    ]
    stage_o = pltpu.make_async_copy(
        r.outw.at[:, my_columns], r.wo.at[my_rows, my_columns], r.stage.at[3]
    )
    stage_u = [
        pltpu.make_async_copy(
            r.up.at[:, pl.ds(pl.multiple_of(CTX * LANES * k + LANES * me, LANES), LANES)],
            r.wu.at[my_rows, pl.ds(LANES * k, LANES)],
            r.stage.at[4 + k],
        )
        for k in range(ff_blocks)
    ]
    stage_d = pltpu.make_async_copy(
        r.down.at[rows_of(down_place, LANES), :],
        r.wd.at[rows_of(k_own, LANES), :],
        r.stage.at[4 + ff_blocks],
    )
    for copy in [*stage_j, stage_o, *stage_u]:
        copy.start()

    @pl.when(has_down)
    def _():
        stage_d.start()

    for copy in fetch[1:10]:
        copy.wait()
    small, short = r.small, r.small.shape[1]
    small[...] = jnp.zeros_like(small)
    for i, vector in enumerate((r.gain_one, r.bias_one, r.gain_two, r.bias_two, r.bias_down)):
        small[i : i + 1, 0:part_rows] = vector[...].astype(F32).reshape(1, part_rows)
    for i in range(shard // short):
        piece = r.bias_up[i * short : (i + 1) * short]
        small[5 + i : 6 + i, :] = piece.astype(F32).reshape(1, short)

    def token_gather(src, dst, sems):
        bulk = dst.at[pl.ds(0, (CTX - 1) * local)]
        return Gather(at, src, lambda c: dst.at[rows_of(c, local)], bulk, *sems)

    tok = token_gather(tokens, r.tokg, r.tok_sem)
    cot = token_gather(cotangent, r.cotg, r.cot_sem)
    x2 = token_gather(r.x2.at[my_tokens], r.x2, r.x2_sem)
    attg = token_gather(r.attg.at[my_tokens], r.attg, r.attg_sem)
    wog = Gather(
        at, r.wo.at[:, my_columns], lambda c: r.wo.at[:, rows_of(c, columns)],
        r.wo.at[:, pl.ds(0, (CTX - 1) * columns)], *r.wog_sem
    )
    seven = pl.ds(0, CTX - 1)
    codes = Exchange(
        at, lambda c: r.codes.at[c], lambda c: r.codeg.at[c], r.codeg.at[seven], *r.code_sem
    )
    att_swap = Exchange(
        at, lambda c: r.att.at[rows_of(c, local)], lambda c: r.attx.at[c], r.attx.at[seven], *r.att_sem
    )

    def token_swap(src, dst, sems):
        return Exchange(
            at, lambda c: src.at[c], lambda c: dst.at[rows_of(c, local)], src.at[seven], *sems
        )

    dat_swap = token_swap(r.dat, r.datg, r.dat_sem)
    br_swap = token_swap(r.brs, r.brg, r.br_sem)
    rest = pl.ds(0, planes - 1)
    small_planes = Planes(
        at, lambda to: small, lambda p: r.smallg.at[p], r.smallg.at[rest], *r.small_sem
    )

    def weight_line(ref, sems, width_ds):
        return Line(
            at, planes, lambda i: i, lambda i: ref.at[rows_of(i, part_rows), width_ds], *sems
        )

    wj = weight_line(r.wj, r.wj_sem, slice(None))
    wo = weight_line(r.wo, r.wo_sem, my_columns)
    wu = weight_line(r.wu, r.wu_sem, slice(None))
    wd = Line(at, ff_blocks, down_owner, lambda k: r.wd.at[rows_of(k, LANES), :], *r.wd_sem)
    back, feed, first = (Scatter(at, *group) for group in (r.back, r.feed, r.first))

    def grad_line(grad, taken, sems):
        return Toward(
            at, planes, lambda i: i, lambda i: grad.at[rows_of(i, part_rows), :], taken, *sems
        )

    dd = Toward(at, ff_blocks, down_owner, lambda k: r.dwd.at[k], r.rd, *r.dwd_sem)
    du = grad_line(r.du, r.ru, r.du_sem)
    do = grad_line(r.do, r.ro, r.do_sem)
    dk = grad_line(r.dk, r.rk, r.dk_sem)
    dq = grad_line(r.dq, r.rq, r.dq_sem)

    class Owned:
        def __init__(self, number, line, acc, total, out, sems):
            self.line, self.acc, self.sum = line, acc, total
            self.gather = Gather(at, total, lambda c: out.at[c], out.at[seven], *sems)
            self.own = pltpu.make_async_copy(total, out.at[me], r.own.at[number])

        def total(self):
            self.line.total(f, self.acc)
            self.sum[...] = self.acc[...].astype(BF16)
            self.gather.start()
            self.own.start()

        def near(self, i):
            self.gather.near(i)

        def far(self):
            self.gather.far()

        def waits(self):
            self.gather.waits()
            self.own.wait()

        def finish(self):
            self.gather.finish()

    gu = Owned(0, du, r.au, r.tu, r.gu, r.gu_sem)
    go = Owned(1, do, r.ao, r.to, r.go, r.go_sem)
    gk = Owned(2, dk, r.ak, r.tk, r.gk, r.gk_sem)
    gq = Owned(3, dq, r.aq, r.tq, r.gq, r.gq_sem)

    class OwnedDown:
        def __init__(self):
            if full_shard:
                self.gather = Gather(at, r.td, lambda c: r.gd.at[c], r.gd.at[seven], *r.gd_sem)
            self.own = pltpu.make_async_copy(r.td, r.gd.at[down_place], r.own.at[4])

        def copy(self, d):
            send, recv = r.gd_sem
            block = r.gd.at[down_place]
            return remote(r.td, block, send.at[d - 1], recv.at[down_place], (at.ctx_at(d), f))

        def total(self):
            @pl.when(has_down)
            def _():
                dd.total(k_own, r.ad)
                r.td[...] = r.ad[...].astype(BF16)
                self.own.start()
                if not full_shard:
                    loop(1, CTX, lambda d: self.copy(d).start())

            if full_shard:
                self.gather.start()

        def near(self, i):
            if full_shard:
                self.gather.near(i)

        def far(self):
            if full_shard:
                self.gather.far()

        def waits(self):
            @pl.when(has_down)
            def _():
                self.own.wait()

            if full_shard:
                self.gather.waits()
                return

            def take(b):
                @pl.when(me != lax.rem(f * shard_blocks + b, CTX))
                def _():
                    block, (send, recv) = r.gd.at[b], r.gd_sem
                    to = (at.ctx_at(jnp.int32(1)), f)
                    remote(block, block, send.at[0], recv.at[b], to).wait_recv()

            loop(0, shard_blocks, take)

        def finish(self):
            if full_shard:
                self.gather.finish()
                return

            @pl.when(has_down)
            def _():
                loop(1, CTX, lambda d: self.copy(d).wait_send())

    gd = OwnedDown()

    class Sums:
        def __init__(self, own, acc, sent, ctx_in, plane_in, ctx_sems, plane_sems):
            self.own, self.acc, self.sent, self.ctx_in, self.plane_in = own, acc, sent, ctx_in, plane_in
            self.swap = Exchange(
                at, lambda c: own, lambda c: ctx_in.at[c], ctx_in.at[seven], *ctx_sems
            )
            self.planes = Planes(
                at, lambda to: sent, lambda p: plane_in.at[p], plane_in.at[rest], *plane_sems
            )

        def put(self, row, vector):
            for k in range(width // LANES):
                self.acc[row + k : row + k + 1, :] = vector[:, k * LANES : (k + 1) * LANES]

        def start(self):
            self.own[...] = self.acc[...].astype(BF16)
            self.swap.start()

        def middle(self):
            self.swap.waits()

            def add(d):
                self.acc[...] += self.ctx_in[at.ctx_at(d)].astype(F32)

            loop(1, CTX, add)
            self.sent[...] = self.acc[...].astype(BF16)
            self.planes.start()

        def end(self):
            self.planes.waits()

            def add(d):
                self.acc[...] += self.plane_in[at.plane_at(d)].astype(F32)

            loop(1, planes, add)

        def row(self, row):
            for k in range(width // LANES):
                r.wide[0:1, k * LANES : (k + 1) * LANES] = self.acc[row + k : row + k + 1, :]
            return r.wide[0:1, :]

        def finish(self):
            self.swap.finish()
            self.planes.finish()

    early, late = Sums(*r.early), Sums(*r.late)
    params = r.params

    def open_devices():
        pl.semaphore_wait(barrier, CTX - 1 + planes - 1)
        fetch[0].wait()
        fetch[10].wait()

    def wj_start():
        for copy in stage_j:
            copy.wait()
        wj.start()

    def wo_start():
        stage_o.wait()
        wo.start()

    def wu_start():
        for copy in stage_u:
            copy.wait()
        wu.start()

    def wd_start():
        @pl.when(has_down)
        def _():
            stage_d.wait()

        wd.start()

    def make_codes():
        write_codes(r, at, seq)
        r.codeg[me] = r.codes[me]

    def take_params():
        r.smallg[f] = small[...]
        small_planes.waits()
        params[...] = jnp.zeros_like(params)
        r.wide[...] = jnp.zeros_like(r.wide)

        def add(p):
            r.wide[:, 0:short] = r.smallg[p, 0:8, :]
            params[...] += pltpu.roll(r.wide[...], p * part_rows, axis=1)

        loop(0, planes, add)
        for k in range(ff_blocks):
            block = CTX * k + me
            place = lax.rem(block, shard_blocks) * LANES
            lanes = pl.ds(pl.multiple_of(lax.rem(place, short), LANES), LANES)
            rows = r.smallg[down_owner(k), :, lanes]
            number = lax.broadcasted_iota(jnp.int32, rows.shape, 0)
            r.ub[0:1, k * LANES : (k + 1) * LANES] = jnp.sum(
                jnp.where(number == 5 + lax.div(place, short), rows, 0.0), axis=0, keepdims=True
            )

    def norm_tokens(g):
        tok.wait(at.other(g))
        rows = rows_of(at.chip_at(g), tile)
        normal, _ = standard(r.tokg[rows, :].astype(F32))
        r.x1[rows, :] = (normal * params[0:1, :] + params[1:2, :]).astype(BF16)

    lane = lax.broadcasted_iota(jnp.int32, (tile, columns), 1)
    low = lane < columns // 2
    zero_tile = jnp.zeros((tile, columns), BF16)

    def project(i):
        rows = rows_of(i, tile)
        projected = dot(r.x1[rows, :], r.wj[...]).astype(BF16)
        q = projected[:, :columns] * jnp.array(0.125, BF16)
        k = projected[:, columns : 2 * columns]
        v = projected[:, 2 * columns :]
        half = lax.rem(lane, columns // 2)
        segment_place = lax.rem(lax.broadcasted_iota(jnp.int32, (LANES, local), 0), LANES // 2) - blocks
        parts = []
        for e in range(2):
            code = r.codeg[2 * i + e]
            hot = jnp.where(
                code[local_blocks : local_blocks + 1] == segment_place.astype(F32), 1.0, 0.0
            ).T
            for b in range(local_blocks):
                parts.append(hot[b * BLOCK : (b + 1) * BLOCK] + code[b : b + 1])
        ext = jnp.concatenate(parts, axis=0)
        token = lax.broadcasted_iota(jnp.int32, (tile, columns), 0) + i * tile
        hot = jnp.where(half == lax.div(token, BLOCK), 1.0, 0.0)
        k_ext = jnp.where(
            half < blocks, hot, jnp.where(half < blocks + SEGMENTS, (1.0 - ext) * -BIG, 0.0)
        ).astype(BF16)
        ext = ext.astype(BF16)
        r.q[rows, :] = q
        r.qa[0, rows, :] = jnp.where(low, q, ext)
        r.qa[1, rows, :] = jnp.where(low, ext, q)
        r.ka[0, rows, :] = jnp.where(low, k, k_ext)
        r.ka[1, rows, :] = jnp.where(low, k_ext, k)
        r.km[0, rows, :] = jnp.where(low, k, zero_tile)
        r.km[1, rows, :] = jnp.where(low, zero_tile, k)
        r.vm[0, rows, :] = jnp.where(low, v, zero_tile)
        r.vm[1, rows, :] = jnp.where(low, zero_tile, v)

    def attend(i):
        rows = rows_of(i, tile)
        out = None
        for h in range(2):
            scores = dot_nt(r.qa[h, rows, :], r.ka[h])
            weights = jnp.exp(scores - jnp.max(scores, axis=1, keepdims=True))
            shares = (weights / jnp.sum(weights, axis=1, keepdims=True)).astype(BF16)
            r.probs[h, rows, :] = shares
            term = dot(shares, r.vm[h])
            out = term if out is None else out + term
        r.att[rows, :] = out.astype(BF16)

    def att_swap_start():
        att_swap.start()
        r.attx[me] = r.att[my_tokens, :]

    def project_out():
        att_swap.waits()
        for c in range(CTX):
            r.attg[my_tokens, c * columns : (c + 1) * columns] = r.attx[c]
        wog.waits()
        middle = tokens[...].astype(F32) + dot(r.attg[my_tokens, :], r.wo[...])
        normal, rate = standard(middle)
        r.middle[...] = middle
        r.n2[...] = normal
        r.rate2[...] = jnp.broadcast_to(rate, r.rate2.shape)
        r.x2[my_tokens, :] = (normal * params[2:3, :] + params[3:4, :]).astype(BF16)

    r.ubg[...] = jnp.zeros_like(r.ubg)

    def hidden_units(g):
        x2.wait(at.other(g))
        rows = rows_of(at.chip_at(g), tile)
        up_sum = dot(r.x2[rows, :], r.wu[...]) + r.ub[...]
        share = 0.5 * (1.0 + lax.erf(up_sum * 0.7071067811865476))
        r.hidden[rows, :] = (up_sum * share).astype(BF16)
        r.slope[rows, :] = share + up_sum * jnp.exp(-0.5 * up_sum * up_sum) * 0.3989422804014327

    def down_grad():
        def one(k):
            r.dwd[k] = dot_tn(r.hidden[:, rows_of(k, LANES)], r.cotg[...]).astype(BF16)

        loop(0, ff_blocks, one)

    def far_first(j):
        return jnp.where(j == 0, 3, jnp.where(j == 3, 0, j))

    def put_part(scatter, g, part):
        chip = at.chip_at(g)
        part = part.astype(BF16)
        scatter.part[2 * chip] = part[:local]
        scatter.part[2 * chip + 1] = part[local:]
        scatter.to_partner(g).start()

    def feed_back(j):
        g = far_first(j)
        rows = rows_of(at.chip_at(g), tile)
        up_grad = (dot_nt(r.cotg[rows, :], r.wd[...]) * r.slope[rows, :]).astype(BF16)
        r.upg[rows, :] = up_grad
        r.ubg[...] += jnp.sum(up_grad.astype(F32), axis=0, keepdims=True)
        put_part(back, g, dot_nt(up_grad, r.wu[...]))

    def feed_part(j):
        g = far_first(j)
        put_part(feed, g, dot(r.hidden[rows_of(at.chip_at(g), tile), :], r.wd[...]))

    def first_part(j):
        g = far_first(j)
        put_part(first, g, dot_nt(r.pg[rows_of(at.chip_at(g), tile), :], r.wj[...]))

    rows_tile = min(tile, width)

    def weight_grad(out, left, right, lanes=slice(None)):
        def body(i):
            out[rows_of(i, rows_tile), :] = dot_tn(
                left[:, rows_of(i, rows_tile)], right[:, lanes]
            ).astype(BF16)

        loop(0, width // rows_tile, body)

    def up_weight_grad():
        weight_grad(r.du, r.x2, r.upg)

    def middle_back():
        normed_two_grad = back.total()
        normal = r.n2[...]
        cot_own = cotangent[...].astype(F32)
        early.acc[...] = jnp.zeros_like(early.acc)
        early.put(0, jnp.sum(normed_two_grad * normal, axis=0, keepdims=True))
        early.put(8, jnp.sum(normed_two_grad, axis=0, keepdims=True))
        early.put(16, jnp.sum(cot_own, axis=0, keepdims=True))
        for k in range(ff_blocks):
            early.acc[pl.ds(24 + CTX * k + me, 1), :] = r.ubg[0:1, k * LANES : (k + 1) * LANES]
        middle_grad = cot_own + standard_grad(
            normed_two_grad * params[2:3, :], normal, r.rate2[:, 0:1]
        )
        r.grad[...] = middle_grad
        branch = middle_grad.astype(BF16)
        attended_grad = dot_nt(branch, r.wo[...]).astype(BF16)
        for c in range(CTX):
            r.dat[c] = attended_grad[:, c * columns : (c + 1) * columns]
            r.brs[c] = branch[:, c * columns : (c + 1) * columns]
        r.acc_k[...] = jnp.zeros_like(r.acc_k)
        r.acc_v[...] = jnp.zeros_like(r.acc_v)

    def dat_start():
        dat_swap.start()
        r.datg[my_tokens, :] = r.dat[me]

    def br_start():
        br_swap.start()
        r.brg[my_tokens, :] = r.brs[me]

    def attend_back(i):
        rows = rows_of(i, tile)
        grad = r.datg[rows, :]
        both = grad.astype(F32) * r.att[rows, :].astype(F32)
        q = r.q[rows, :]
        query_grad = None
        for h in range(2):
            keep = low if h == 0 else ~low
            delta = jnp.sum(jnp.where(keep, both, 0.0), axis=1, keepdims=True)
            probs = r.probs[h, rows, :]
            prob_grad = dot_nt(grad, r.vm[h])
            score_grad = (probs.astype(F32) * (prob_grad - delta)).astype(BF16)
            term = dot(score_grad, r.km[h])
            query_grad = term if query_grad is None else query_grad + term
            r.acc_k[...] += dot_tn(score_grad, jnp.where(keep, q, zero_tile))
            r.acc_v[...] += dot_tn(probs, jnp.where(keep, grad, zero_tile))
        r.pg[rows, :columns] = (query_grad * 0.125).astype(BF16)

    def keys_back():
        r.pg[:, columns : 2 * columns] = r.acc_k[...].astype(BF16)
        r.pg[:, 2 * columns :] = r.acc_v[...].astype(BF16)

    def key_weight_grad():
        weight_grad(r.dk, r.x1, r.pg, slice(columns, None))

    def query_weight_grad():
        weight_grad(r.dq, r.x1, r.pg, slice(0, columns))

    def out_weight_grad():
        attg.waits()
        br_swap.waits()
        weight_grad(r.do, r.attg, r.brg)

    def layer_end():
        r.layer[...] = (r.middle[...] + feed.total() + params[4:5, :]).astype(BF16)
        layer_copy.start()

    def tokens_back():
        normed_one_grad = first.total()
        normal, rate = standard(tokens[...].astype(F32))
        late.put(0, jnp.sum(normed_one_grad * normal, axis=0, keepdims=True))
        late.put(8, jnp.sum(normed_one_grad, axis=0, keepdims=True))
        r.grad[...] += standard_grad(normed_one_grad * params[0:1, :], normal, rate)
        grad_copy.start()

    def write_totals():
        for i, (sums, row) in enumerate(((late, 0), (late, 8), (early, 0), (early, 8), (early, 16))):
            vector = jnp.broadcast_to(sums.row(row), (8, width))
            turned = pltpu.roll(vector, lax.rem((planes - f) * part_rows, width), axis=1)
            r.sums[i : i + 1, :] = turned[0:1]
        for k in range(shard_blocks):
            r.sums[5:6, k * LANES : (k + 1) * LANES] = early.acc[
                pl.ds(24 + f * shard_blocks + k, 1), :
            ]

    def finish(*ended):
        for each in ended:
            each.finish()

    def finish_forward():
        finish(tok, cot, wog, x2, codes, att_swap, small_planes, wj, wo, wu, wd)

    def finish_middle():
        finish(attg, dat_swap, br_swap, dd, back)

    open_devices()
    wo_start()
    make_codes()
    codes.start()
    wj_start()
    small_planes.start()
    tok.start()
    wo.passes(1)
    take_params()
    wo.passes(2)

    def step_1(i):

        @pl.when(i == 1)
        def _():
            wu_start()
            cot.start()
            tok.near(0)
            wj.passes(1)
            tok.near(1)
            cot.near(0)
            wj.passes(2)
            tok.far()
            cot.near(1)
            wo.passes(3)

        norm_tokens(i)

    loop(0, 4, step_1)

    wog.start()
    wj.passes(3)
    codes.waits()

    def step_2(i):

        @pl.when(i == 1)
        def _():
            wd_start()
            wu.passes(1)

        project(i)

    loop(0, 4, step_2)


    def step_3(i):

        @pl.when(i == 2)
        def _():
            cot.far()
            wog.near(1)
            wog.near(0)

        attend(i)

    loop(0, 4, step_3)

    att_swap_start()
    wog.far()
    wu.passes(2)
    project_out()
    x2.start()
    wd.passes(1)
    x2.near(0)
    x2.near(1)
    wu.passes(3)

    def step_4(i):

        @pl.when(i == 2)
        def _():
            x2.far()
            wd.passes(2)

        hidden_units(i)

    loop(0, 4, step_4)

    attg.start()
    cot.waits()
    down_grad()
    wd.passes(3)
    dd.step(3)

    def step_5(i):

        @pl.when(i == 2)
        def _():
            back.first()

        feed_back(i)

    loop(0, 3, step_5)

    back.second()
    dd.step(2)
    feed_part(jnp.int32(0))
    feed_back(jnp.int32(3))
    up_weight_grad()
    attg.near(0)
    attg.near(1)
    du.step(3)
    middle_back()
    dat_start()
    dd.step(1)
    loop(1, 4, feed_part)
    attg.far()
    feed.first()
    dat_swap.waits()

    def step_6(i):

        @pl.when(i == 1)
        def _():
            early.start()
            du.step(2)
            br_start()

        @pl.when(i == 2)
        def _():
            gd.total()
            feed.second()

        @pl.when(i == 3)
        def _():
            du.step(1)

        attend_back(i)

    loop(0, 4, step_6)

    finish_forward()
    keys_back()

    def step_7(i):

        @pl.when(i == 1)
        def _():
            key_weight_grad()
            dk.step(3)
            query_weight_grad()
            dq.step(3)
            out_weight_grad()
            finish_middle()
            first.first()

        first_part(i)

    loop(0, 4, step_7)

    gd.near(1)
    gd.near(0)
    dk.step(2)
    dq.step(2)
    first.second()
    do.step(3)
    gu.total()
    dk.step(1)
    dq.step(1)
    gk.total()
    early.middle()
    gq.total()
    do.step(2)
    tokens_back()
    late.start()
    do.step(1)
    go.total()
    gu.near(0)
    gu.near(1)
    late.middle()
    gk.near(0)
    gk.near(1)
    gq.near(1)
    gd.far()
    go.near(0)
    go.near(1)
    gq.near(0)
    gu.far()
    gk.far()
    gq.far()
    go.far()
    layer_end()
    late.end()
    early.end()
    write_totals()
    totals_copy.start()
    for each in (gd, gu, go, gk, gq):
        each.waits()
    finish(gu, go, gk, gq, gd, early, late, du, do, dk, dq, feed, first)
    for copy in (layer_copy, grad_copy, totals_copy):
        copy.wait()


def shards(
    tokens,
    segment_ids,
    random_blocks,
    global_blocks,
    first_gain,
    first_bias,
    joint_weight,
    output_weight,
    second_gain,
    second_bias,
    up_weight,
    up_bias,
    down_weight,
    down_bias,
    cotangent,
):
    local, width = tokens.shape[1:]
    ctx, planes = lax.axis_size("ctx"), lax.axis_size("fsdp")
    heads = random_blocks.shape[2]
    seq = local * ctx
    blocks = seq // BLOCK
    part_rows = width // planes
    columns = width // ctx
    ff_shard = up_bias.shape[0]
    ff = ff_shard * planes
    ff_blocks = ff // LANES // ctx
    shard_blocks = ff_shard // LANES
    ff_part = ff // ctx
    assert ctx == CTX and columns == LANES and heads == 2 * ctx and blocks + SEGMENTS <= 64
    assert CTX % shard_blocks == 0 and ff // width == ff_blocks

    hbm = pl.BlockSpec(memory_space=pl.ANY)
    inputs = dict(
        tokens_in=tokens[0],
        cotangent_in=cotangent[0],
        segments_in=segment_ids,
        random_in=random_blocks[0].transpose(2, 0, 1),
        globals_in=global_blocks,
        gain_one_in=first_gain,
        bias_one_in=first_bias,
        gain_two_in=second_gain,
        bias_two_in=second_bias,
        bias_up_in=up_bias,
        bias_down_in=down_bias,
        joint=joint_weight,
        outw=output_weight,
        up=up_weight,
        down=down_weight,
    )
    outputs = dict(
        layer_out=((local, width), BF16),
        tokens_grad=((local, width), F32),
        totals=((8, width), F32),
        gk=((ctx, part_rows, 2 * columns), BF16),
        gq=((ctx, part_rows, columns), BF16),
        go=((ctx, part_rows, columns), BF16),
        gu=((ctx, part_rows, ff_part), BF16),
        gd=((shard_blocks, LANES, width), BF16),
    )
    dma = lambda n: pltpu.SemaphoreType.DMA((n,))
    v16 = lambda *shape: pltpu.VMEM(shape, BF16)
    v32 = lambda *shape: pltpu.VMEM(shape, F32)
    scatter = (
        v16(ctx, local, width), v16(4, local, width), v16(2, local // 2, width), v16(2, local, width),
        dma(1), dma(4), dma(4),
    )
    gather, swap = (dma(1), dma(ctx + 1)), (dma(1), dma(1))
    line, toward = (dma(2 * planes), dma(planes)), (dma(planes), dma(planes + 1))
    short = max(part_rows, LANES)
    vectors = lambda rows: (
        v16(rows, LANES), v32(rows, LANES), v16(rows, LANES), v16(ctx, rows, LANES),
        v16(planes, rows, LANES), swap, swap,
    )
    copied = lambda name: pltpu.VMEM(inputs[name].shape, inputs[name].dtype)
    scratch = dict(
        segments=copied("segments_in"), random=copied("random_in"), globals=copied("globals_in"),
        gain_one=copied("gain_one_in"), bias_one=copied("bias_one_in"),
        gain_two=copied("gain_two_in"), bias_two=copied("bias_two_in"),
        bias_up=copied("bias_up_in"), bias_down=copied("bias_down_in"), fetch=dma(14),
        layer=v16(local, width), grad=v32(local, width), sums=v32(8, width),
        wj=v16(width, 3 * columns), wo=v16(width, width), wu=v16(width, ff_part),
        wd=v16(ff_part, width), tokg=v16(seq, width), cotg=v16(seq, width),
        x1=v16(seq, width), x2=v16(seq, width), attg=v16(seq, width),
        codes=v32(ctx, 8, LANES), codeg=v32(ctx, 8, LANES), small=v32(16, short),
        smallg=v32(planes, 16, short), params=v32(8, width), wide=v32(8, width),
        ub=v32(1, ff_part), ubg=v32(1, ff_part), q=v16(seq, columns),
        qa=v16(2, seq, columns), ka=v16(2, seq, columns), km=v16(2, seq, columns),
        vm=v16(2, seq, columns), probs=v16(2, seq, seq), att=v16(seq, columns),
        attx=v16(ctx, local, columns), middle=v32(local, width), n2=v32(local, width),
        rate2=v32(local, LANES), hidden=v16(seq, ff_part), slope=v32(seq, ff_part),
        upg=v16(seq, ff_part), dat=v16(ctx, local, columns), brs=v16(ctx, local, columns),
        datg=v16(seq, columns), brg=v16(seq, columns), acc_k=v32(seq, columns),
        acc_v=v32(seq, columns), pg=v16(seq, 3 * columns), early=vectors(64), late=vectors(16),
        dk=v16(width, 2 * columns), dq=v16(width, columns), do=v16(width, columns),
        du=v16(width, ff_part), dwd=v16(ff_blocks, LANES, width),
        rk=v16(planes + 1, part_rows, 2 * columns), rq=v16(planes + 1, part_rows, columns),
        ro=v16(planes + 1, part_rows, columns), ru=v16(planes + 1, part_rows, ff_part),
        rd=v16(ff_blocks + 1, LANES, width),
        ak=v32(part_rows, 2 * columns), aq=v32(part_rows, columns), ao=v32(part_rows, columns),
        au=v32(part_rows, ff_part), ad=v32(LANES, width),
        tk=v16(part_rows, 2 * columns), tq=v16(part_rows, columns), to=v16(part_rows, columns),
        tu=v16(part_rows, ff_part), td=v16(LANES, width),
        stage=dma(5 + ff_blocks), own=dma(5), wd_sem=(dma(2 * ff_blocks), dma(ff_blocks)),
        dwd_sem=(dma(ff_blocks), dma(ff_blocks + 1)), back=scatter, feed=scatter, first=scatter,
        tok_sem=gather, cot_sem=gather, wog_sem=gather, x2_sem=gather, attg_sem=gather,
        gk_sem=gather, gq_sem=gather, go_sem=gather, gu_sem=gather, gd_sem=gather if shard_blocks == ctx else (dma(ctx - 1), dma(ctx)),
        code_sem=swap, att_sem=swap, dat_sem=swap, br_sem=swap,
        small_sem=swap, wj_sem=line, wo_sem=line, wu_sem=line,
        dk_sem=toward, dq_sem=toward, do_sem=toward, du_sem=toward,
    )
    shapes, scratch_tree = jax.tree.flatten(scratch)
    ins, outs = len(inputs), len(outputs)

    def kernel(*refs):
        held = dict(zip([*inputs, *outputs], refs, strict=False))
        held |= jax.tree.unflatten(scratch_tree, refs[ins + outs :])
        layer_kernel(types.SimpleNamespace(**held), planes)

    layer_out, tokens_grad, totals, gk, gq, go, gu, gd = pl.pallas_call(
        kernel,
        out_shape=[jax.ShapeDtypeStruct(shape, dtype) for shape, dtype in outputs.values()],
        in_specs=[hbm] * ins,
        out_specs=[hbm] * outs,
        scratch_shapes=shapes,
        compiler_params=pltpu.CompilerParams(
            collective_id=0, has_side_effects=True, fuse_transposed_lhs_in_matmul=True,
            vmem_limit_bytes=60 * 1024 * 1024
        ),
    )(*inputs.values())

    group = ctx
    quads = ctx // group
    steps = ff_blocks * quads

    def spread(ref, out):
        for q in range(group):
            out[:, q * columns : (q + 1) * columns] = ref[q].astype(F32)

    def finish(out_in, grad_in, totals, gk, gq, go, gu, gd, joint, outw, up, down, out, grad, *vectors):
        step = pl.program_id(0)

        @pl.when(step < quads)
        def _():
            spread(gq, joint)
            spread(go, outw)

        @pl.when((step >= quads) & (step < 3 * quads))
        def _():
            spread(gk, joint)

        spread(gu, up)
        down[...] = gd[...].reshape(down.shape).astype(F32)
        out[...] = out_in[...]
        grad[...] = grad_in[...]
        for i, vector in enumerate(vectors[:5]):
            vector[...] = totals[i : i + 1, 0:part_rows].reshape(part_rows)
        vectors[5][...] = totals[5:6, 0:ff_shard].reshape(ff_shard)

    def from_places(start, count):
        place = lambda i: jnp.clip(i - start, 0, count - 1)
        return pl.BlockSpec(
            (group, part_rows, columns), lambda i: (place(i) % quads, 0, place(i) // quads)
        )

    def to_columns(count):
        return pl.BlockSpec((part_rows, group * columns), lambda i: (0, jnp.minimum(i, count - 1)))

    down_group = max(shard_blocks // steps, 1)
    down_place = lambda i: jnp.minimum(i, shard_blocks // down_group - 1)
    whole = pl.BlockSpec(memory_space=pltpu.VMEM)
    tokens_spec = pl.BlockSpec((local // steps, width), lambda i: (i, 0))
    made = pl.pallas_call(
        finish,
        grid=(steps,),
        out_shape=[
            jax.ShapeDtypeStruct(shape, dtype)
            for shape, dtype in (
                ((part_rows, 3 * width), F32), ((part_rows, width), F32), ((part_rows, ff), F32),
                ((ff_shard, width), F32), ((local, width), BF16), ((local, width), F32),
                *([((part_rows,), F32)] * 5), ((ff_shard,), F32),
            )
        ],
        in_specs=[
            tokens_spec,
            tokens_spec,
            whole,
            from_places(quads, 2 * quads),
            from_places(0, quads),
            from_places(0, quads),
            from_places(0, steps),
            pl.BlockSpec((down_group, LANES, width), lambda i: (down_place(i), 0, 0)),
        ],
        out_specs=[
            to_columns(3 * quads),
            to_columns(quads),
            to_columns(steps),
            pl.BlockSpec((down_group * LANES, width), lambda i: (down_place(i), 0)),
            tokens_spec,
            tokens_spec,
            *([whole] * 6),
        ],
        compiler_params=pltpu.CompilerParams(vmem_limit_bytes=60 * 1024 * 1024),
    )(layer_out, tokens_grad, totals, gk, gq, go, gu, gd)
    return (
        made[4][None],
        made[5][None],
        made[6],
        made[7],
        made[0],
        made[1],
        made[8],
        made[9],
        made[2],
        made[11],
        made[3],
        made[10],
    )


def solution(mesh):
    in_specs = (
        P("fsdp", "ctx", None),
        P("fsdp", "ctx"),
        P("fsdp", "ctx", None, None),
        P("fsdp", None),
        P("fsdp"),
        P("fsdp"),
        P("fsdp", None),
        P("fsdp", None),
        P("fsdp"),
        P("fsdp"),
        P("fsdp", None),
        P("fsdp"),
        P("fsdp", None),
        P("fsdp"),
        P("fsdp", "ctx", None),
    )
    out_specs = (
        P("fsdp", "ctx", None),
        P("fsdp", "ctx", None),
        P("fsdp"),
        P("fsdp"),
        P("fsdp", None),
        P("fsdp", None),
        P("fsdp"),
        P("fsdp"),
        P("fsdp", None),
        P("fsdp"),
        P("fsdp", None),
        P("fsdp"),
    )
    return jax.shard_map(shards, mesh=mesh, in_specs=in_specs, out_specs=out_specs, check_vma=False)
```

```python
import types

import jax
import jax.numpy as jnp
from jax import lax
from jax.experimental import pallas as pl
from jax.experimental.pallas import tpu as pltpu
from jax.sharding import PartitionSpec as P

BLOCK = 64
LANES = 128
CTX = 8
SEGMENTS = 4
EPS = 1e-05
BIG = 1e30
MESH = pl.DeviceIdType.MESH
BF16 = jnp.bfloat16
F32 = jnp.float32


def dot(a, b):
    return lax.dot_general(a, b, (((1,), (0,)), ((), ())), preferred_element_type=F32)


def dot_nt(a, b):
    return lax.dot_general(a, b, (((1,), (1,)), ((), ())), preferred_element_type=F32)


def dot_tn(a, b):
    return lax.dot_general(a, b, (((0,), (0,)), ((), ())), preferred_element_type=F32)


def loop(lower, upper, body):
    lax.fori_loop(lower, upper, lambda i, carry: (body(i), carry)[1], jnp.int32(0))


def rows_of(index, size):
    return pl.ds(pl.multiple_of(index * size, size), size)


def remote(src, dst, send, recv, device):
    return pltpu.make_async_remote_copy(
        src_ref=src,
        dst_ref=dst,
        send_sem=send,
        recv_sem=recv,
        device_id=device,
        device_id_type=MESH,
    )


class Place:
    def __init__(self, planes):
        self.c = lax.axis_index("ctx")
        self.f = lax.axis_index("fsdp")
        self.planes = planes
        self.parity = lax.rem(self.c, 2)
        self.chip = lax.div(self.c, 2)
        self.partner = 2 * self.chip + 1 - self.parity

    def chip_at(self, g):
        low = lax.rem(lax.rem(self.chip, 2) + lax.rem(g, 2), 2)
        high = lax.rem(lax.div(self.chip, 2) + lax.div(g, 2), 2)
        return low + 2 * high

    def same(self, g):
        return 2 * self.chip_at(g) + self.parity

    def other(self, g):
        return 2 * self.chip_at(g) + 1 - self.parity

    def ctx_at(self, d):
        return lax.rem(self.c + d, CTX)

    def plane_at(self, d):
        return lax.rem(self.f + d, self.planes)


class Gather:
    def __init__(self, at, src, slot, bulk, send, recv):
        self.at, self.src, self.slot, self.bulk = at, src, slot, bulk
        self.send, self.recv = send.at[0], recv

    def half(self, c, i):
        block = self.slot(c)
        size = block.shape[0] // 2
        return block.at[pl.ds(i * size, size)]

    def direct(self, i):
        at = self.at
        to = at.partner if i == 0 else at.same(jnp.int32(i))
        return remote(self.src, self.slot(at.c), self.send, self.recv.at[at.c], (to, at.f))

    def across(self, i):
        at = self.at
        c, to = at.same(jnp.int32(1 + i)), at.same(jnp.int32(2 - i))
        block = self.half(c, i)
        recv = self.recv.at[c] if i == 0 else self.recv.at[CTX]
        return remote(block, block, self.send, recv, (to, at.f))

    def passed(self, g):
        at = self.at
        c = at.same(jnp.int32(g))
        block = self.slot(c)
        return remote(block, block, self.send, self.recv.at[c], (at.partner, at.f))

    def start(self):
        for i in (1, 2, 0):
            self.direct(i).start()

    def wait(self, c):
        at = self.at
        block = self.slot(c)
        remote(block, block, self.send, self.recv.at[c], (at.partner, at.f)).wait_recv()

    def near(self, i):
        self.wait(self.at.same(jnp.int32(1 + i)))
        self.across(i).start()
        self.passed(1 + i).start()

    def far(self):
        at = self.at
        for i in range(2):
            c = at.same(jnp.int32(3))
            block = self.half(c, i)
            recv = self.recv.at[c] if i == 0 else self.recv.at[CTX]
            remote(block, block, self.send, recv, (at.partner, at.f)).wait_recv()
        self.passed(3).start()

    def waits(self):
        loop(0, 4, lambda g: self.wait(self.at.other(g)))

    def finish(self):
        remote(self.bulk, self.bulk, self.send, self.recv.at[0], (self.at.partner, self.at.f)).wait_send()


class Exchange:
    def __init__(self, at, src, slot, bulk, send, recv):
        self.at, self.src, self.slot, self.bulk = at, src, slot, bulk
        self.send, self.recv = send.at[0], recv.at[0]

    def copy(self, d):
        at = self.at
        to = at.ctx_at(d)
        return remote(self.src(to), self.slot(at.c), self.send, self.recv, (to, at.f))

    def start(self):
        loop(1, CTX, lambda d: self.copy(d).start())

    def whole(self):
        return remote(self.bulk, self.bulk, self.send, self.recv, (self.at.partner, self.at.f))

    def waits(self):
        self.whole().wait_recv()

    def finish(self):
        self.whole().wait_send()


class Planes:
    def __init__(self, at, src, slot, bulk, send, recv):
        self.at, self.src, self.slot, self.bulk = at, src, slot, bulk
        self.send, self.recv = send.at[0], recv.at[0]

    def copy(self, d):
        at = self.at
        to = at.plane_at(d)
        return remote(self.src(to), self.slot(at.f), self.send, self.recv, (at.c, to))

    def start(self):
        loop(1, self.at.planes, lambda d: self.copy(d).start())

    def whole(self):
        at = self.at
        to = at.plane_at(jnp.int32(1))
        return remote(self.bulk, self.bulk, self.send, self.recv, (at.c, to))

    def waits(self):
        self.whole().wait_recv()

    def finish(self):
        self.whole().wait_send()


class Line:
    def __init__(self, at, items, owner, view, send, recv):
        self.at, self.items, self.owner, self.view = at, items, owner, view
        self.send, self.recv = send, recv

    def hop(self, i, up):
        at, block = self.at, self.view(i)
        to = jnp.minimum(at.f + 1, at.planes - 1) if up else jnp.maximum(at.f - 1, 0)
        return remote(
            block, block, self.send.at[2 * i + (1 if up else 0)], self.recv.at[i], (at.c, to)
        )

    def outward(self, i, act):
        at, owner = self.at, self.owner(i)

        @pl.when((owner <= at.f) & (at.f < at.planes - 1))
        def _():
            act(self.hop(i, True))

        @pl.when((owner >= at.f) & (at.f > 0))
        def _():
            act(self.hop(i, False))

    def start(self):
        def each(i):
            @pl.when(self.owner(i) == self.at.f)
            def _():
                self.outward(i, lambda copy: copy.start())

        loop(0, self.items, each)

    def arrive(self, i):
        self.hop(i, True).wait_recv()
        self.outward(i, lambda copy: copy.start())

    def passes(self, d):
        if d == 3:
            loop(3, self.at.planes, self.passes_from)
        elif d < self.at.planes:
            self.passes_from(d)

    def passes_from(self, d):
        def each(i):
            owner = self.owner(i)

            @pl.when((owner == self.at.f + d) | (owner == self.at.f - d))
            def _():
                self.arrive(i)

        loop(0, self.items, each)

    def finish(self):
        loop(0, self.items, lambda i: self.outward(i, lambda copy: copy.wait_send()))


class Toward:
    def __init__(self, at, items, owner, part, taken, send, recv):
        self.at, self.items, self.owner, self.part, self.taken = at, items, owner, part, taken
        self.send, self.recv = send, recv

    def hop(self, i, up):
        at = self.at
        to = jnp.minimum(at.f + 1, at.planes - 1) if up else jnp.maximum(at.f - 1, 0)
        slot = i + 1 if up else i
        return remote(
            self.part(i), self.taken.at[slot], self.send.at[i], self.recv.at[slot], (at.c, to)
        )

    def step(self, d):
        at = self.at
        if d == 3:
            loop(3, at.planes, lambda j: self.step_to(at.planes + 2 - j))
        elif d < at.planes:
            self.step_to(d)

    def step_to(self, d):
        at = self.at

        def one(i, up, comes):
            @pl.when(comes)
            def _():
                self.hop(i, up).wait_recv()
                block = self.part(i)
                come = self.taken[i + 1 if up else i].astype(F32)
                block[...] = (block[...].astype(F32) + come).astype(BF16)

            self.hop(i, up).start()

        def each(i):
            @pl.when(self.owner(i) == at.f + d)
            def _():
                one(i, True, at.f > 0)

            @pl.when(self.owner(i) == at.f - d)
            def _():
                one(i, False, at.f < at.planes - 1)

        loop(0, self.items, each)

    def total(self, i, acc):
        at = self.at
        acc[...] = self.part(i)[...].astype(F32)

        @pl.when(at.f > 0)
        def _():
            self.hop(i, True).wait_recv()
            acc[...] += self.taken[i + 1].astype(F32)

        @pl.when(at.f < at.planes - 1)
        def _():
            self.hop(i, False).wait_recv()
            acc[...] += self.taken[i].astype(F32)

    def finish(self):
        def each(i):
            @pl.when(self.owner(i) > self.at.f)
            def _():
                self.hop(i, True).wait_send()

            @pl.when(self.owner(i) < self.at.f)
            def _():
                self.hop(i, False).wait_send()

        loop(0, self.items, each)


class Scatter:
    def __init__(self, at, part, pair, halves, far, send, pair_recv, recv):
        self.at, self.part, self.pair, self.halves, self.far = at, part, pair, halves, far
        self.send, self.pair_recv, self.recv = send.at[0], pair_recv, recv
        self.size = part.shape[1] // 2

    def to_partner(self, g):
        at = self.at
        return remote(
            self.part.at[at.other(g)],
            self.pair.at[g],
            self.send,
            self.pair_recv.at[g],
            (at.partner, at.f),
        )

    def across(self, i):
        at = self.at
        return remote(
            self.part.at[at.same(jnp.int32(3)), pl.ds(i * self.size, self.size)],
            self.halves.at[i],
            self.send,
            self.recv.at[i],
            (at.same(jnp.int32(1 + i)), at.f),
        )

    def beside(self, i):
        at = self.at
        to = at.same(jnp.int32(1 + i))
        return remote(
            self.part.at[to], self.far.at[i], self.send, self.recv.at[2 + i], (to, at.f)
        )

    def add_pair(self, g):
        self.to_partner(jnp.int32(g)).wait_recv()
        own = self.at.same(jnp.int32(g))
        both = self.part[own].astype(F32) + self.pair[g].astype(F32)
        self.part[own] = both.astype(BF16)

    def first(self):
        self.add_pair(3)
        for i in range(2):
            self.across(i).start()

    def second(self):
        for i in range(2):
            self.add_pair(1 + i)
        for i in range(2):
            self.across(i).wait_recv()
            to = self.at.same(jnp.int32(2 - i))
            rows = pl.ds(i * self.size, self.size)
            both = self.part[to, rows].astype(F32) + self.halves[i].astype(F32)
            self.part[to, rows] = both.astype(BF16)
            self.beside(1 - i).start()

    def total(self):
        self.to_partner(jnp.int32(0)).wait_recv()
        for i in range(2):
            self.beside(i).wait_recv()
        both = self.part[self.at.c].astype(F32) + self.pair[0].astype(F32)
        return both + (self.far[0].astype(F32) + self.far[1].astype(F32))

    def finish(self):
        at, blocks = self.at, self.part.at[pl.ds(0, CTX - 1)]
        remote(blocks, blocks, self.send, self.recv.at[0], (at.partner, at.f)).wait_send()


def standard(values):
    centre = jnp.mean(values, axis=-1, keepdims=True)
    offset = values - centre
    spread = jnp.mean(offset * offset, axis=-1, keepdims=True)
    rate = lax.rsqrt(spread + EPS)
    return offset * rate, rate


def standard_grad(e, normal, rate):
    return rate * (
        e - jnp.mean(e, axis=-1, keepdims=True) - normal * jnp.mean(e * normal, axis=-1, keepdims=True)
    )


def write_codes(r, at, seq):
    local = r.segments.shape[1]
    blocks, local_blocks = seq // BLOCK, local // BLOCK
    draws, _, heads = r.random.shape
    half = LANES // 2
    key = lax.rem(lax.broadcasted_iota(jnp.int32, (heads, LANES), 1), half)
    lower = lax.broadcasted_iota(jnp.int32, (1, LANES), 1) < half
    diagonal = lax.broadcasted_iota(jnp.int32, (heads, heads), 0) == lax.broadcasted_iota(
        jnp.int32, (heads, heads), 1
    )
    pair = r.globals[...]
    for b in range(local_blocks):
        block = at.c * local_blocks + b
        counted = jnp.abs(key - block) <= 1
        for j in range(draws):
            row = jnp.broadcast_to(r.random[j, b : b + 1, :].astype(F32), (heads, heads))
            drawn = jnp.sum(jnp.where(diagonal, row, 0.0), axis=1, keepdims=True)
            counted = counted | (key.astype(F32) == drawn)
        for j in range(pair.shape[1]):
            chosen = pair[:, j : j + 1]
            counted = counted | (key == chosen) | (chosen == block)
        code = jnp.where(counted | (key >= blocks), 0.0, -BIG)
        for d in range(heads // 2):
            both = jnp.where(lower, code[2 * d + 1 : 2 * d + 2], code[2 * d : 2 * d + 1])
            r.codes[d, b : b + 1, :] = both
    segments = r.segments[...].astype(F32)
    for d in range(heads // 2):
        r.codes[d, local_blocks : local_blocks + 1, :] = segments


def layer_kernel(r, planes):
    at = Place(planes)
    me, f = at.c, at.f
    local, width = r.tokens_in.shape
    seq = local * CTX
    blocks, local_blocks = seq // BLOCK, local // BLOCK
    part_rows = width // planes
    columns = width // CTX
    shard = r.down.shape[0]
    ff = planes * shard
    ff_blocks = ff // LANES // CTX
    shard_blocks = shard // LANES
    full_shard = shard_blocks == CTX
    tile = 2 * local
    k_own = lax.div(f * shard_blocks, CTX)
    has_down = lax.div(me, shard_blocks) == lax.rem(f, CTX // shard_blocks)
    down_place = lax.rem(me, shard_blocks)

    def down_owner(k):
        return lax.div(CTX * k + me, shard_blocks)

    my_rows = rows_of(f, part_rows)
    my_columns = rows_of(me, columns)
    my_tokens = rows_of(me, local)
    tokens, cotangent = r.tokg.at[my_tokens], r.cotg.at[my_tokens]

    barrier = pltpu.get_barrier_semaphore()
    loop(
        1,
        CTX,
        lambda d: pl.semaphore_signal(
            barrier, inc=1, device_id=(at.ctx_at(d), f), device_id_type=MESH
        ),
    )
    loop(
        1,
        planes,
        lambda d: pl.semaphore_signal(
            barrier, inc=1, device_id=(me, at.plane_at(d)), device_id_type=MESH
        ),
    )

    fetched = (
        (r.tokens_in, tokens), (r.gain_one_in, r.gain_one), (r.bias_one_in, r.bias_one),
        (r.gain_two_in, r.gain_two), (r.bias_two_in, r.bias_two), (r.bias_down_in, r.bias_down),
        (r.bias_up_in, r.bias_up), (r.segments_in, r.segments), (r.random_in, r.random),
        (r.globals_in, r.globals), (r.cotangent_in, cotangent),
    )
    fetch = [
        pltpu.make_async_copy(src, dst, r.fetch.at[i]) for i, (src, dst) in enumerate(fetched)
    ]
    for copy in fetch:
        copy.start()
    layer_copy = pltpu.make_async_copy(r.layer, r.layer_out, r.fetch.at[len(fetch)])
    grad_copy = pltpu.make_async_copy(r.grad, r.tokens_grad, r.fetch.at[len(fetch) + 1])
    totals_copy = pltpu.make_async_copy(r.sums, r.totals, r.fetch.at[len(fetch) + 2])
    stage_j = [
        pltpu.make_async_copy(
            r.joint.at[:, pl.ds(pl.multiple_of(width * j + columns * me, LANES), columns)],
            r.wj.at[my_rows, pl.ds(columns * j, columns)],
            r.stage.at[j],
        )
        for j in range(3)
    ]
    stage_o = pltpu.make_async_copy(
        r.outw.at[:, my_columns], r.wo.at[my_rows, my_columns], r.stage.at[3]
    )
    stage_u = [
        pltpu.make_async_copy(
            r.up.at[:, pl.ds(pl.multiple_of(CTX * LANES * k + LANES * me, LANES), LANES)],
            r.wu.at[my_rows, pl.ds(LANES * k, LANES)],
            r.stage.at[4 + k],
        )
        for k in range(ff_blocks)
    ]
    stage_d = pltpu.make_async_copy(
        r.down.at[rows_of(down_place, LANES), :],
        r.wd.at[rows_of(k_own, LANES), :],
        r.stage.at[4 + ff_blocks],
    )
    for copy in [*stage_j, stage_o, *stage_u]:
        copy.start()

    @pl.when(has_down)
    def _():
        stage_d.start()

    for copy in fetch[1:10]:
        copy.wait()
    small, short = r.small, r.small.shape[1]
    small[...] = jnp.zeros_like(small)
    for i, vector in enumerate((r.gain_one, r.bias_one, r.gain_two, r.bias_two, r.bias_down)):
        small[i : i + 1, 0:part_rows] = vector[...].astype(F32).reshape(1, part_rows)
    for i in range(shard // short):
        piece = r.bias_up[i * short : (i + 1) * short]
        small[5 + i : 6 + i, :] = piece.astype(F32).reshape(1, short)

    def token_gather(src, dst, sems):
        bulk = dst.at[pl.ds(0, (CTX - 1) * local)]
        return Gather(at, src, lambda c: dst.at[rows_of(c, local)], bulk, *sems)

    tok = token_gather(tokens, r.tokg, r.tok_sem)
    cot = token_gather(cotangent, r.cotg, r.cot_sem)
    x2 = token_gather(r.x2.at[my_tokens], r.x2, r.x2_sem)
    attg = token_gather(r.attg.at[my_tokens], r.attg, r.attg_sem)
    wog = Gather(
        at, r.wo.at[:, my_columns], lambda c: r.wo.at[:, rows_of(c, columns)],
        r.wo.at[:, pl.ds(0, (CTX - 1) * columns)], *r.wog_sem
    )
    seven = pl.ds(0, CTX - 1)
    codes = Exchange(
        at, lambda c: r.codes.at[c], lambda c: r.codeg.at[c], r.codeg.at[seven], *r.code_sem
    )
    att_swap = Exchange(
        at, lambda c: r.att.at[rows_of(c, local)], lambda c: r.attx.at[c], r.attx.at[seven], *r.att_sem
    )

    def token_swap(src, dst, sems):
        return Exchange(
            at, lambda c: src.at[c], lambda c: dst.at[rows_of(c, local)], src.at[seven], *sems
        )

    dat_swap = token_swap(r.dat, r.datg, r.dat_sem)
    br_swap = token_swap(r.brs, r.brg, r.br_sem)
    rest = pl.ds(0, planes - 1)
    small_planes = Planes(
        at, lambda to: small, lambda p: r.smallg.at[p], r.smallg.at[rest], *r.small_sem
    )

    def weight_line(ref, sems, width_ds):
        return Line(
            at, planes, lambda i: i, lambda i: ref.at[rows_of(i, part_rows), width_ds], *sems
        )

    wj = weight_line(r.wj, r.wj_sem, slice(None))
    wo = weight_line(r.wo, r.wo_sem, my_columns)
    wu = weight_line(r.wu, r.wu_sem, slice(None))
    wd = Line(at, ff_blocks, down_owner, lambda k: r.wd.at[rows_of(k, LANES), :], *r.wd_sem)
    back, feed, first = (Scatter(at, *group) for group in (r.back, r.feed, r.first))

    def grad_line(grad, taken, sems):
        return Toward(
            at, planes, lambda i: i, lambda i: grad.at[rows_of(i, part_rows), :], taken, *sems
        )

    dd = Toward(at, ff_blocks, down_owner, lambda k: r.dwd.at[k], r.rd, *r.dwd_sem)
    du = grad_line(r.du, r.ru, r.du_sem)
    do = grad_line(r.do, r.ro, r.do_sem)
    dk = grad_line(r.dk, r.rk, r.dk_sem)
    dq = grad_line(r.dq, r.rq, r.dq_sem)

    class Owned:
        def __init__(self, number, line, acc, total, out, sems):
            self.line, self.acc, self.sum = line, acc, total
            self.gather = Gather(at, total, lambda c: out.at[c], out.at[seven], *sems)
            self.own = pltpu.make_async_copy(total, out.at[me], r.own.at[number])

        def total(self):
            self.line.total(f, self.acc)
            self.sum[...] = self.acc[...].astype(BF16)
            self.gather.start()
            self.own.start()

        def near(self, i):
            self.gather.near(i)

        def far(self):
            self.gather.far()

        def waits(self):
            self.gather.waits()
            self.own.wait()

        def finish(self):
            self.gather.finish()

    gu = Owned(0, du, r.au, r.tu, r.gu, r.gu_sem)
    go = Owned(1, do, r.ao, r.to, r.go, r.go_sem)
    gk = Owned(2, dk, r.ak, r.tk, r.gk, r.gk_sem)
    gq = Owned(3, dq, r.aq, r.tq, r.gq, r.gq_sem)

    class OwnedDown:
        def __init__(self):
            if full_shard:
                self.gather = Gather(at, r.td, lambda c: r.gd.at[c], r.gd.at[seven], *r.gd_sem)
            self.own = pltpu.make_async_copy(r.td, r.gd.at[down_place], r.own.at[4])

        def copy(self, d):
            send, recv = r.gd_sem
            block = r.gd.at[down_place]
            return remote(r.td, block, send.at[d - 1], recv.at[down_place], (at.ctx_at(d), f))

        def total(self):
            @pl.when(has_down)
            def _():
                dd.total(k_own, r.ad)
                r.td[...] = r.ad[...].astype(BF16)
                self.own.start()
                if not full_shard:
                    loop(1, CTX, lambda d: self.copy(d).start())

            if full_shard:
                self.gather.start()

        def near(self, i):
            if full_shard:
                self.gather.near(i)

        def far(self):
            if full_shard:
                self.gather.far()

        def waits(self):
            @pl.when(has_down)
            def _():
                self.own.wait()

            if full_shard:
                self.gather.waits()
                return

            def take(b):
                @pl.when(me != lax.rem(f * shard_blocks + b, CTX))
                def _():
                    block, (send, recv) = r.gd.at[b], r.gd_sem
                    to = (at.ctx_at(jnp.int32(1)), f)
                    remote(block, block, send.at[0], recv.at[b], to).wait_recv()

            loop(0, shard_blocks, take)

        def finish(self):
            if full_shard:
                self.gather.finish()
                return

            @pl.when(has_down)
            def _():
                loop(1, CTX, lambda d: self.copy(d).wait_send())

    gd = OwnedDown()

    class Sums:
        def __init__(self, own, acc, sent, ctx_in, plane_in, ctx_sems, plane_sems):
            self.own, self.acc, self.sent, self.ctx_in, self.plane_in = own, acc, sent, ctx_in, plane_in
            self.swap = Exchange(
                at, lambda c: own, lambda c: ctx_in.at[c], ctx_in.at[seven], *ctx_sems
            )
            self.planes = Planes(
                at, lambda to: sent, lambda p: plane_in.at[p], plane_in.at[rest], *plane_sems
            )

        def put(self, row, vector):
            for k in range(width // LANES):
                self.acc[row + k : row + k + 1, :] = vector[:, k * LANES : (k + 1) * LANES]

        def start(self):
            self.own[...] = self.acc[...].astype(BF16)
            self.swap.start()

        def middle(self):
            self.swap.waits()

            def add(d):
                self.acc[...] += self.ctx_in[at.ctx_at(d)].astype(F32)

            loop(1, CTX, add)
            self.sent[...] = self.acc[...].astype(BF16)
            self.planes.start()

        def end(self):
            self.planes.waits()

            def add(d):
                self.acc[...] += self.plane_in[at.plane_at(d)].astype(F32)

            loop(1, planes, add)

        def row(self, row):
            for k in range(width // LANES):
                r.wide[0:1, k * LANES : (k + 1) * LANES] = self.acc[row + k : row + k + 1, :]
            return r.wide[0:1, :]

        def finish(self):
            self.swap.finish()
            self.planes.finish()

    early, late = Sums(*r.early), Sums(*r.late)
    params = r.params

    def open_devices():
        pl.semaphore_wait(barrier, CTX - 1 + planes - 1)
        fetch[0].wait()
        fetch[10].wait()

    def wj_start():
        for copy in stage_j:
            copy.wait()
        wj.start()

    def wo_start():
        stage_o.wait()
        wo.start()

    def wu_start():
        for copy in stage_u:
            copy.wait()
        wu.start()

    def wd_start():
        @pl.when(has_down)
        def _():
            stage_d.wait()

        wd.start()

    def make_codes():
        write_codes(r, at, seq)
        r.codeg[me] = r.codes[me]

    def take_params():
        r.smallg[f] = small[...]
        small_planes.waits()
        params[...] = jnp.zeros_like(params)
        r.wide[...] = jnp.zeros_like(r.wide)

        def add(p):
            r.wide[:, 0:short] = r.smallg[p, 0:8, :]
            params[...] += pltpu.roll(r.wide[...], p * part_rows, axis=1)

        loop(0, planes, add)
        for k in range(ff_blocks):
            block = CTX * k + me
            place = lax.rem(block, shard_blocks) * LANES
            lanes = pl.ds(pl.multiple_of(lax.rem(place, short), LANES), LANES)
            rows = r.smallg[down_owner(k), :, lanes]
            number = lax.broadcasted_iota(jnp.int32, rows.shape, 0)
            r.ub[0:1, k * LANES : (k + 1) * LANES] = jnp.sum(
                jnp.where(number == 5 + lax.div(place, short), rows, 0.0), axis=0, keepdims=True
            )

    def norm_tokens(g):
        tok.wait(at.other(g))
        rows = rows_of(at.chip_at(g), tile)
        normal, _ = standard(r.tokg[rows, :].astype(F32))
        r.x1[rows, :] = (normal * params[0:1, :] + params[1:2, :]).astype(BF16)

    lane = lax.broadcasted_iota(jnp.int32, (tile, columns), 1)
    low = lane < columns // 2
    zero_tile = jnp.zeros((tile, columns), BF16)

    def project(i):
        rows = rows_of(i, tile)
        projected = dot(r.x1[rows, :], r.wj[...]).astype(BF16)
        q = projected[:, :columns] * jnp.array(0.125, BF16)
        k = projected[:, columns : 2 * columns]
        v = projected[:, 2 * columns :]
        half = lax.rem(lane, columns // 2)
        segment_place = lax.rem(lax.broadcasted_iota(jnp.int32, (LANES, local), 0), LANES // 2) - blocks
        parts = []
        for e in range(2):
            code = r.codeg[2 * i + e]
            hot = jnp.where(
                code[local_blocks : local_blocks + 1] == segment_place.astype(F32), 1.0, 0.0
            ).T
            for b in range(local_blocks):
                parts.append(hot[b * BLOCK : (b + 1) * BLOCK] + code[b : b + 1])
        ext = jnp.concatenate(parts, axis=0)
        token = lax.broadcasted_iota(jnp.int32, (tile, columns), 0) + i * tile
        hot = jnp.where(half == lax.div(token, BLOCK), 1.0, 0.0)
        k_ext = jnp.where(
            half < blocks, hot, jnp.where(half < blocks + SEGMENTS, (1.0 - ext) * -BIG, 0.0)
        ).astype(BF16)
        ext = ext.astype(BF16)
        r.q[rows, :] = q
        r.qa[0, rows, :] = jnp.where(low, q, ext)
        r.qa[1, rows, :] = jnp.where(low, ext, q)
        r.ka[0, rows, :] = jnp.where(low, k, k_ext)
        r.ka[1, rows, :] = jnp.where(low, k_ext, k)
        r.km[0, rows, :] = jnp.where(low, k, zero_tile)
        r.km[1, rows, :] = jnp.where(low, zero_tile, k)
        r.vm[0, rows, :] = jnp.where(low, v, zero_tile)
        r.vm[1, rows, :] = jnp.where(low, zero_tile, v)

    def attend(i):
        rows = rows_of(i, tile)
        out = None
        for h in range(2):
            scores = dot_nt(r.qa[h, rows, :], r.ka[h])
            weights = jnp.exp(scores - jnp.max(scores, axis=1, keepdims=True))
            shares = (weights / jnp.sum(weights, axis=1, keepdims=True)).astype(BF16)
            r.probs[h, rows, :] = shares
            term = dot(shares, r.vm[h])
            out = term if out is None else out + term
        r.att[rows, :] = out.astype(BF16)

    def att_swap_start():
        att_swap.start()
        r.attx[me] = r.att[my_tokens, :]

    def project_out():
        att_swap.waits()
        for c in range(CTX):
            r.attg[my_tokens, c * columns : (c + 1) * columns] = r.attx[c]
        wog.waits()
        middle = tokens[...].astype(F32) + dot(r.attg[my_tokens, :], r.wo[...])
        normal, rate = standard(middle)
        r.middle[...] = middle
        r.n2[...] = normal
        r.rate2[...] = jnp.broadcast_to(rate, r.rate2.shape)
        r.x2[my_tokens, :] = (normal * params[2:3, :] + params[3:4, :]).astype(BF16)

    r.ubg[...] = jnp.zeros_like(r.ubg)

    def hidden_units(g):
        x2.wait(at.other(g))
        rows = rows_of(at.chip_at(g), tile)
        up_sum = dot(r.x2[rows, :], r.wu[...]) + r.ub[...]
        share = 0.5 * (1.0 + lax.erf(up_sum * 0.7071067811865476))
        r.hidden[rows, :] = (up_sum * share).astype(BF16)
        r.slope[rows, :] = share + up_sum * jnp.exp(-0.5 * up_sum * up_sum) * 0.3989422804014327

    def down_grad():
        def one(k):
            r.dwd[k] = dot_tn(r.hidden[:, rows_of(k, LANES)], r.cotg[...]).astype(BF16)

        loop(0, ff_blocks, one)

    def far_first(j):
        return jnp.where(j == 0, 3, jnp.where(j == 3, 0, j))

    def put_part(scatter, g, part):
        chip = at.chip_at(g)
        part = part.astype(BF16)
        scatter.part[2 * chip] = part[:local]
        scatter.part[2 * chip + 1] = part[local:]
        scatter.to_partner(g).start()

    def feed_back(j):
        g = far_first(j)
        rows = rows_of(at.chip_at(g), tile)
        up_grad = (dot_nt(r.cotg[rows, :], r.wd[...]) * r.slope[rows, :]).astype(BF16)
        r.upg[rows, :] = up_grad
        r.ubg[...] += jnp.sum(up_grad.astype(F32), axis=0, keepdims=True)
        put_part(back, g, dot_nt(up_grad, r.wu[...]))

    def feed_part(j):
        g = far_first(j)
        put_part(feed, g, dot(r.hidden[rows_of(at.chip_at(g), tile), :], r.wd[...]))

    def first_part(j):
        g = far_first(j)
        put_part(first, g, dot_nt(r.pg[rows_of(at.chip_at(g), tile), :], r.wj[...]))

    rows_tile = min(tile, width)

    def weight_grad(out, left, right, lanes=slice(None)):
        def body(i):
            out[rows_of(i, rows_tile), :] = dot_tn(
                left[:, rows_of(i, rows_tile)], right[:, lanes]
            ).astype(BF16)

        loop(0, width // rows_tile, body)

    def up_weight_grad():
        weight_grad(r.du, r.x2, r.upg)

    def middle_back():
        normed_two_grad = back.total()
        normal = r.n2[...]
        cot_own = cotangent[...].astype(F32)
        early.acc[...] = jnp.zeros_like(early.acc)
        early.put(0, jnp.sum(normed_two_grad * normal, axis=0, keepdims=True))
        early.put(8, jnp.sum(normed_two_grad, axis=0, keepdims=True))
        early.put(16, jnp.sum(cot_own, axis=0, keepdims=True))
        for k in range(ff_blocks):
            early.acc[pl.ds(24 + CTX * k + me, 1), :] = r.ubg[0:1, k * LANES : (k + 1) * LANES]
        middle_grad = cot_own + standard_grad(
            normed_two_grad * params[2:3, :], normal, r.rate2[:, 0:1]
        )
        r.grad[...] = middle_grad
        branch = middle_grad.astype(BF16)
        attended_grad = dot_nt(branch, r.wo[...]).astype(BF16)
        for c in range(CTX):
            r.dat[c] = attended_grad[:, c * columns : (c + 1) * columns]
            r.brs[c] = branch[:, c * columns : (c + 1) * columns]
        r.acc_k[...] = jnp.zeros_like(r.acc_k)
        r.acc_v[...] = jnp.zeros_like(r.acc_v)

    def dat_start():
        dat_swap.start()
        r.datg[my_tokens, :] = r.dat[me]

    def br_start():
        br_swap.start()
        r.brg[my_tokens, :] = r.brs[me]

    def attend_back(i):
        rows = rows_of(i, tile)
        grad = r.datg[rows, :]
        both = grad.astype(F32) * r.att[rows, :].astype(F32)
        q = r.q[rows, :]
        query_grad = None
        for h in range(2):
            keep = low if h == 0 else ~low
            delta = jnp.sum(jnp.where(keep, both, 0.0), axis=1, keepdims=True)
            probs = r.probs[h, rows, :]
            prob_grad = dot_nt(grad, r.vm[h])
            score_grad = (probs.astype(F32) * (prob_grad - delta)).astype(BF16)
            term = dot(score_grad, r.km[h])
            query_grad = term if query_grad is None else query_grad + term
            r.acc_k[...] += dot_tn(score_grad, jnp.where(keep, q, zero_tile))
            r.acc_v[...] += dot_tn(probs, jnp.where(keep, grad, zero_tile))
        r.pg[rows, :columns] = (query_grad * 0.125).astype(BF16)

    def keys_back():
        r.pg[:, columns : 2 * columns] = r.acc_k[...].astype(BF16)
        r.pg[:, 2 * columns :] = r.acc_v[...].astype(BF16)

    def key_weight_grad():
        weight_grad(r.dk, r.x1, r.pg, slice(columns, None))

    def query_weight_grad():
        weight_grad(r.dq, r.x1, r.pg, slice(0, columns))

    def out_weight_grad():
        attg.waits()
        br_swap.waits()
        weight_grad(r.do, r.attg, r.brg)

    def layer_end():
        r.layer[...] = (r.middle[...] + feed.total() + params[4:5, :]).astype(BF16)
        layer_copy.start()

    def tokens_back():
        normed_one_grad = first.total()
        normal, rate = standard(tokens[...].astype(F32))
        late.put(0, jnp.sum(normed_one_grad * normal, axis=0, keepdims=True))
        late.put(8, jnp.sum(normed_one_grad, axis=0, keepdims=True))
        r.grad[...] += standard_grad(normed_one_grad * params[0:1, :], normal, rate)
        grad_copy.start()

    def write_totals():
        for i, (sums, row) in enumerate(((late, 0), (late, 8), (early, 0), (early, 8), (early, 16))):
            vector = jnp.broadcast_to(sums.row(row), (8, width))
            turned = pltpu.roll(vector, lax.rem((planes - f) * part_rows, width), axis=1)
            r.sums[i : i + 1, :] = turned[0:1]
        for k in range(shard_blocks):
            r.sums[5:6, k * LANES : (k + 1) * LANES] = early.acc[
                pl.ds(24 + f * shard_blocks + k, 1), :
            ]

    def finish(*ended):
        for each in ended:
            each.finish()

    def finish_forward():
        finish(tok, cot, wog, x2, codes, att_swap, small_planes, wj, wo, wu, wd)

    def finish_middle():
        finish(attg, dat_swap, br_swap, dd, back)

    open_devices()
    wo_start()
    make_codes()
    codes.start()
    wj_start()
    small_planes.start()
    tok.start()
    wo.passes(1)
    take_params()
    wo.passes(2)

    def step_1(i):

        @pl.when(i == 1)
        def _():
            wu_start()
            cot.start()
            tok.near(0)
            wj.passes(1)
            tok.near(1)
            cot.near(0)
            wj.passes(2)
            tok.far()
            cot.near(1)
            wo.passes(3)

        norm_tokens(i)

    loop(0, 4, step_1)

    wog.start()
    wj.passes(3)
    codes.waits()

    def step_2(i):

        @pl.when(i == 1)
        def _():
            wd_start()
            wu.passes(1)

        project(i)

    loop(0, 4, step_2)


    def step_3(i):

        @pl.when(i == 2)
        def _():
            cot.far()
            wog.near(1)
            wog.near(0)

        attend(i)

    loop(0, 4, step_3)

    att_swap_start()
    wog.far()
    wu.passes(2)
    project_out()
    x2.start()
    wd.passes(1)
    x2.near(0)
    x2.near(1)
    wu.passes(3)

    def step_4(i):

        @pl.when(i == 2)
        def _():
            x2.far()
            wd.passes(2)

        hidden_units(i)

    loop(0, 4, step_4)

    attg.start()
    cot.waits()
    down_grad()
    wd.passes(3)
    dd.step(3)

    def step_5(i):

        @pl.when(i == 2)
        def _():
            back.first()

        feed_back(i)

    loop(0, 3, step_5)

    back.second()
    attg.near(0)
    attg.near(1)
    dd.step(2)
    feed_part(jnp.int32(0))
    feed_back(jnp.int32(3))
    up_weight_grad()
    du.step(3)
    middle_back()
    dat_start()
    early.start()
    dd.step(1)
    loop(1, 4, feed_part)
    attg.far()
    feed.first()
    dat_swap.waits()

    def step_6(i):

        @pl.when(i == 1)
        def _():
            du.step(2)
            br_start()

        @pl.when(i == 2)
        def _():
            gd.total()
            feed.second()

        @pl.when(i == 3)
        def _():
            early.middle()
            du.step(1)

        attend_back(i)

    loop(0, 4, step_6)

    finish_forward()
    keys_back()

    def step_7(i):

        @pl.when(i == 1)
        def _():
            key_weight_grad()
            dk.step(3)
            query_weight_grad()
            dq.step(3)
            out_weight_grad()
            finish_middle()
            first.first()

        first_part(i)

    loop(0, 4, step_7)

    gd.near(1)
    gd.near(0)
    dk.step(2)
    dq.step(2)
    first.second()
    do.step(3)
    gu.total()
    dk.step(1)
    dq.step(1)
    gk.total()
    gq.total()
    do.step(2)
    tokens_back()
    late.start()
    do.step(1)
    go.total()
    gu.near(0)
    gu.near(1)
    late.middle()
    gk.near(0)
    gk.near(1)
    gq.near(1)
    gd.far()
    go.near(0)
    go.near(1)
    gq.near(0)
    gu.far()
    gk.far()
    gq.far()
    go.far()
    layer_end()
    late.end()
    early.end()
    write_totals()
    totals_copy.start()
    for each in (gd, gu, go, gk, gq):
        each.waits()
    finish(gu, go, gk, gq, gd, early, late, du, do, dk, dq, feed, first)
    for copy in (layer_copy, grad_copy, totals_copy):
        copy.wait()


def shards(
    tokens,
    segment_ids,
    random_blocks,
    global_blocks,
    first_gain,
    first_bias,
    joint_weight,
    output_weight,
    second_gain,
    second_bias,
    up_weight,
    up_bias,
    down_weight,
    down_bias,
    cotangent,
):
    local, width = tokens.shape[1:]
    ctx, planes = lax.axis_size("ctx"), lax.axis_size("fsdp")
    heads = random_blocks.shape[2]
    seq = local * ctx
    blocks = seq // BLOCK
    part_rows = width // planes
    columns = width // ctx
    ff_shard = up_bias.shape[0]
    ff = ff_shard * planes
    ff_blocks = ff // LANES // ctx
    shard_blocks = ff_shard // LANES
    ff_part = ff // ctx
    assert ctx == CTX and columns == LANES and heads == 2 * ctx and blocks + SEGMENTS <= 64
    assert CTX % shard_blocks == 0 and ff // width == ff_blocks

    hbm = pl.BlockSpec(memory_space=pl.ANY)
    inputs = dict(
        tokens_in=tokens[0],
        cotangent_in=cotangent[0],
        segments_in=segment_ids,
        random_in=random_blocks[0].transpose(2, 0, 1),
        globals_in=global_blocks,
        gain_one_in=first_gain,
        bias_one_in=first_bias,
        gain_two_in=second_gain,
        bias_two_in=second_bias,
        bias_up_in=up_bias,
        bias_down_in=down_bias,
        joint=joint_weight,
        outw=output_weight,
        up=up_weight,
        down=down_weight,
    )
    outputs = dict(
        layer_out=((local, width), BF16),
        tokens_grad=((local, width), F32),
        totals=((8, width), F32),
        gk=((ctx, part_rows, 2 * columns), BF16),
        gq=((ctx, part_rows, columns), BF16),
        go=((ctx, part_rows, columns), BF16),
        gu=((ctx, part_rows, ff_part), BF16),
        gd=((shard_blocks, LANES, width), BF16),
    )
    dma = lambda n: pltpu.SemaphoreType.DMA((n,))
    v16 = lambda *shape: pltpu.VMEM(shape, BF16)
    v32 = lambda *shape: pltpu.VMEM(shape, F32)
    scatter = (
        v16(ctx, local, width), v16(4, local, width), v16(2, local // 2, width), v16(2, local, width),
        dma(1), dma(4), dma(4),
    )
    gather, swap = (dma(1), dma(ctx + 1)), (dma(1), dma(1))
    line, toward = (dma(2 * planes), dma(planes)), (dma(planes), dma(planes + 1))
    short = max(part_rows, LANES)
    vectors = lambda rows: (
        v16(rows, LANES), v32(rows, LANES), v16(rows, LANES), v16(ctx, rows, LANES),
        v16(planes, rows, LANES), swap, swap,
    )
    copied = lambda name: pltpu.VMEM(inputs[name].shape, inputs[name].dtype)
    scratch = dict(
        segments=copied("segments_in"), random=copied("random_in"), globals=copied("globals_in"),
        gain_one=copied("gain_one_in"), bias_one=copied("bias_one_in"),
        gain_two=copied("gain_two_in"), bias_two=copied("bias_two_in"),
        bias_up=copied("bias_up_in"), bias_down=copied("bias_down_in"), fetch=dma(14),
        layer=v16(local, width), grad=v32(local, width), sums=v32(8, width),
        wj=v16(width, 3 * columns), wo=v16(width, width), wu=v16(width, ff_part),
        wd=v16(ff_part, width), tokg=v16(seq, width), cotg=v16(seq, width),
        x1=v16(seq, width), x2=v16(seq, width), attg=v16(seq, width),
        codes=v32(ctx, 8, LANES), codeg=v32(ctx, 8, LANES), small=v32(16, short),
        smallg=v32(planes, 16, short), params=v32(8, width), wide=v32(8, width),
        ub=v32(1, ff_part), ubg=v32(1, ff_part), q=v16(seq, columns),
        qa=v16(2, seq, columns), ka=v16(2, seq, columns), km=v16(2, seq, columns),
        vm=v16(2, seq, columns), probs=v16(2, seq, seq), att=v16(seq, columns),
        attx=v16(ctx, local, columns), middle=v32(local, width), n2=v32(local, width),
        rate2=v32(local, LANES), hidden=v16(seq, ff_part), slope=v32(seq, ff_part),
        upg=v16(seq, ff_part), dat=v16(ctx, local, columns), brs=v16(ctx, local, columns),
        datg=v16(seq, columns), brg=v16(seq, columns), acc_k=v32(seq, columns),
        acc_v=v32(seq, columns), pg=v16(seq, 3 * columns), early=vectors(64), late=vectors(16),
        dk=v16(width, 2 * columns), dq=v16(width, columns), do=v16(width, columns),
        du=v16(width, ff_part), dwd=v16(ff_blocks, LANES, width),
        rk=v16(planes + 1, part_rows, 2 * columns), rq=v16(planes + 1, part_rows, columns),
        ro=v16(planes + 1, part_rows, columns), ru=v16(planes + 1, part_rows, ff_part),
        rd=v16(ff_blocks + 1, LANES, width),
        ak=v32(part_rows, 2 * columns), aq=v32(part_rows, columns), ao=v32(part_rows, columns),
        au=v32(part_rows, ff_part), ad=v32(LANES, width),
        tk=v16(part_rows, 2 * columns), tq=v16(part_rows, columns), to=v16(part_rows, columns),
        tu=v16(part_rows, ff_part), td=v16(LANES, width),
        stage=dma(5 + ff_blocks), own=dma(5), wd_sem=(dma(2 * ff_blocks), dma(ff_blocks)),
        dwd_sem=(dma(ff_blocks), dma(ff_blocks + 1)), back=scatter, feed=scatter, first=scatter,
        tok_sem=gather, cot_sem=gather, wog_sem=gather, x2_sem=gather, attg_sem=gather,
        gk_sem=gather, gq_sem=gather, go_sem=gather, gu_sem=gather, gd_sem=gather if shard_blocks == ctx else (dma(ctx - 1), dma(ctx)),
        code_sem=swap, att_sem=swap, dat_sem=swap, br_sem=swap,
        small_sem=swap, wj_sem=line, wo_sem=line, wu_sem=line,
        dk_sem=toward, dq_sem=toward, do_sem=toward, du_sem=toward,
    )
    shapes, scratch_tree = jax.tree.flatten(scratch)
    ins, outs = len(inputs), len(outputs)

    def kernel(*refs):
        held = dict(zip([*inputs, *outputs], refs, strict=False))
        held |= jax.tree.unflatten(scratch_tree, refs[ins + outs :])
        layer_kernel(types.SimpleNamespace(**held), planes)

    layer_out, tokens_grad, totals, gk, gq, go, gu, gd = pl.pallas_call(
        kernel,
        out_shape=[jax.ShapeDtypeStruct(shape, dtype) for shape, dtype in outputs.values()],
        in_specs=[hbm] * ins,
        out_specs=[hbm] * outs,
        scratch_shapes=shapes,
        compiler_params=pltpu.CompilerParams(
            collective_id=0, has_side_effects=True, fuse_transposed_lhs_in_matmul=True,
            vmem_limit_bytes=60 * 1024 * 1024
        ),
    )(*inputs.values())

    group = ctx
    quads = ctx // group
    steps = ff_blocks * quads

    def spread(ref, out):
        for q in range(group):
            out[:, q * columns : (q + 1) * columns] = ref[q].astype(F32)

    def finish(out_in, grad_in, totals, gk, gq, go, gu, gd, joint, outw, up, down, out, grad, *vectors):
        step = pl.program_id(0)

        @pl.when(step < quads)
        def _():
            spread(gq, joint)
            spread(go, outw)

        @pl.when((step >= quads) & (step < 3 * quads))
        def _():
            spread(gk, joint)

        spread(gu, up)
        down[...] = gd[...].reshape(down.shape).astype(F32)
        out[...] = out_in[...]
        grad[...] = grad_in[...]
        for i, vector in enumerate(vectors[:5]):
            vector[...] = totals[i : i + 1, 0:part_rows].reshape(part_rows)
        vectors[5][...] = totals[5:6, 0:ff_shard].reshape(ff_shard)

    def from_places(start, count):
        place = lambda i: jnp.clip(i - start, 0, count - 1)
        return pl.BlockSpec(
            (group, part_rows, columns), lambda i: (place(i) % quads, 0, place(i) // quads)
        )

    def to_columns(count):
        return pl.BlockSpec((part_rows, group * columns), lambda i: (0, jnp.minimum(i, count - 1)))

    down_group = max(shard_blocks // steps, 1)
    down_place = lambda i: jnp.minimum(i, shard_blocks // down_group - 1)
    whole = pl.BlockSpec(memory_space=pltpu.VMEM)
    tokens_spec = pl.BlockSpec((local // steps, width), lambda i: (i, 0))
    made = pl.pallas_call(
        finish,
        grid=(steps,),
        out_shape=[
            jax.ShapeDtypeStruct(shape, dtype)
            for shape, dtype in (
                ((part_rows, 3 * width), F32), ((part_rows, width), F32), ((part_rows, ff), F32),
                ((ff_shard, width), F32), ((local, width), BF16), ((local, width), F32),
                *([((part_rows,), F32)] * 5), ((ff_shard,), F32),
            )
        ],
        in_specs=[
            tokens_spec,
            tokens_spec,
            whole,
            from_places(quads, 2 * quads),
            from_places(0, quads),
            from_places(0, quads),
            from_places(0, steps),
            pl.BlockSpec((down_group, LANES, width), lambda i: (down_place(i), 0, 0)),
        ],
        out_specs=[
            to_columns(3 * quads),
            to_columns(quads),
            to_columns(steps),
            pl.BlockSpec((down_group * LANES, width), lambda i: (down_place(i), 0)),
            tokens_spec,
            tokens_spec,
            *([whole] * 6),
        ],
        compiler_params=pltpu.CompilerParams(vmem_limit_bytes=60 * 1024 * 1024),
    )(layer_out, tokens_grad, totals, gk, gq, go, gu, gd)
    return (
        made[4][None],
        made[5][None],
        made[6],
        made[7],
        made[0],
        made[1],
        made[8],
        made[9],
        made[2],
        made[11],
        made[3],
        made[10],
    )


def solution(mesh):
    in_specs = (
        P("fsdp", "ctx", None),
        P("fsdp", "ctx"),
        P("fsdp", "ctx", None, None),
        P("fsdp", None),
        P("fsdp"),
        P("fsdp"),
        P("fsdp", None),
        P("fsdp", None),
        P("fsdp"),
        P("fsdp"),
        P("fsdp", None),
        P("fsdp"),
        P("fsdp", None),
        P("fsdp"),
        P("fsdp", "ctx", None),
    )
    out_specs = (
        P("fsdp", "ctx", None),
        P("fsdp", "ctx", None),
        P("fsdp"),
        P("fsdp"),
        P("fsdp", None),
        P("fsdp", None),
        P("fsdp"),
        P("fsdp"),
        P("fsdp", None),
        P("fsdp"),
        P("fsdp", None),
        P("fsdp"),
    )
    return jax.shard_map(shards, mesh=mesh, in_specs=in_specs, out_specs=out_specs, check_vma=False)
```

```python
import types

import jax
import jax.numpy as jnp
from jax import lax
from jax.experimental import pallas as pl
from jax.experimental.pallas import tpu as pltpu
from jax.sharding import PartitionSpec as P

BLOCK = 64
LANES = 128
CTX = 8
SEGMENTS = 4
EPS = 1e-05
BIG = 1e30
MESH = pl.DeviceIdType.MESH
BF16 = jnp.bfloat16
F32 = jnp.float32


def dot(a, b):
    return lax.dot_general(a, b, (((1,), (0,)), ((), ())), preferred_element_type=F32)


def dot_nt(a, b):
    return lax.dot_general(a, b, (((1,), (1,)), ((), ())), preferred_element_type=F32)


def dot_tn(a, b):
    return lax.dot_general(a, b, (((0,), (0,)), ((), ())), preferred_element_type=F32)


def loop(lower, upper, body):
    lax.fori_loop(lower, upper, lambda i, carry: (body(i), carry)[1], jnp.int32(0))


def rows_of(index, size):
    return pl.ds(pl.multiple_of(index * size, size), size)


def remote(src, dst, send, recv, device):
    return pltpu.make_async_remote_copy(
        src_ref=src,
        dst_ref=dst,
        send_sem=send,
        recv_sem=recv,
        device_id=device,
        device_id_type=MESH,
    )


class Place:
    def __init__(self, planes):
        self.c = lax.axis_index("ctx")
        self.f = lax.axis_index("fsdp")
        self.planes = planes
        self.parity = lax.rem(self.c, 2)
        self.chip = lax.div(self.c, 2)
        self.partner = 2 * self.chip + 1 - self.parity

    def chip_at(self, g):
        low = lax.rem(lax.rem(self.chip, 2) + lax.rem(g, 2), 2)
        high = lax.rem(lax.div(self.chip, 2) + lax.div(g, 2), 2)
        return low + 2 * high

    def same(self, g):
        return 2 * self.chip_at(g) + self.parity

    def other(self, g):
        return 2 * self.chip_at(g) + 1 - self.parity

    def ctx_at(self, d):
        return lax.rem(self.c + d, CTX)

    def plane_at(self, d):
        return lax.rem(self.f + d, self.planes)


class Gather:
    def __init__(self, at, src, slot, bulk, send, recv):
        self.at, self.src, self.slot, self.bulk = at, src, slot, bulk
        self.send, self.recv = send.at[0], recv

    def half(self, c, i):
        block = self.slot(c)
        size = block.shape[0] // 2
        return block.at[pl.ds(i * size, size)]

    def direct(self, i):
        at = self.at
        to = at.partner if i == 0 else at.same(jnp.int32(i))
        return remote(self.src, self.slot(at.c), self.send, self.recv.at[at.c], (to, at.f))

    def across(self, i):
        at = self.at
        c, to = at.same(jnp.int32(1 + i)), at.same(jnp.int32(2 - i))
        block = self.half(c, i)
        return remote(block, block, self.send, self.recv.at[c], (to, at.f))

    def passed(self, g):
        at = self.at
        c = at.same(jnp.int32(g))
        block = self.slot(c)
        return remote(block, block, self.send, self.recv.at[c], (at.partner, at.f))

    def start(self):
        for i in (1, 2, 0):
            self.direct(i).start()

    def wait(self, c):
        at = self.at
        block = self.slot(c)
        remote(block, block, self.send, self.recv.at[c], (at.partner, at.f)).wait_recv()

    def near(self, i):
        self.wait(self.at.same(jnp.int32(1 + i)))
        self.across(i).start()
        self.passed(1 + i).start()

    def far(self):
        self.wait(self.at.same(jnp.int32(3)))
        self.passed(3).start()

    def waits(self):
        loop(0, 4, lambda g: self.wait(self.at.other(g)))

    def finish(self):
        remote(self.bulk, self.bulk, self.send, self.recv.at[0], (self.at.partner, self.at.f)).wait_send()


class Exchange:
    def __init__(self, at, src, slot, bulk, send, recv):
        self.at, self.src, self.slot, self.bulk = at, src, slot, bulk
        self.send, self.recv = send.at[0], recv.at[0]

    def copy(self, d):
        at = self.at
        to = at.ctx_at(d)
        return remote(self.src(to), self.slot(at.c), self.send, self.recv, (to, at.f))

    def start(self):
        loop(1, CTX, lambda d: self.copy(d).start())

    def whole(self):
        return remote(self.bulk, self.bulk, self.send, self.recv, (self.at.partner, self.at.f))

    def waits(self):
        self.whole().wait_recv()

    def finish(self):
        self.whole().wait_send()


class Planes:
    def __init__(self, at, src, slot, bulk, send, recv):
        self.at, self.src, self.slot, self.bulk = at, src, slot, bulk
        self.send, self.recv = send.at[0], recv.at[0]

    def copy(self, d):
        at = self.at
        to = at.plane_at(d)
        return remote(self.src(to), self.slot(at.f), self.send, self.recv, (at.c, to))

    def start(self):
        loop(1, self.at.planes, lambda d: self.copy(d).start())

    def whole(self):
        at = self.at
        to = at.plane_at(jnp.int32(1))
        return remote(self.bulk, self.bulk, self.send, self.recv, (at.c, to))

    def waits(self):
        self.whole().wait_recv()

    def finish(self):
        self.whole().wait_send()


class Line:
    def __init__(self, at, items, owner, view, send, recv):
        self.at, self.items, self.owner, self.view = at, items, owner, view
        self.send, self.recv = send, recv

    def hop(self, i, up):
        at, block = self.at, self.view(i)
        to = jnp.minimum(at.f + 1, at.planes - 1) if up else jnp.maximum(at.f - 1, 0)
        return remote(
            block, block, self.send.at[2 * i + (1 if up else 0)], self.recv.at[i], (at.c, to)
        )

    def outward(self, i, act):
        at, owner = self.at, self.owner(i)

        @pl.when((owner <= at.f) & (at.f < at.planes - 1))
        def _():
            act(self.hop(i, True))

        @pl.when((owner >= at.f) & (at.f > 0))
        def _():
            act(self.hop(i, False))

    def start(self):
        def each(i):
            @pl.when(self.owner(i) == self.at.f)
            def _():
                self.outward(i, lambda copy: copy.start())

        loop(0, self.items, each)

    def arrive(self, i):
        self.hop(i, True).wait_recv()
        self.outward(i, lambda copy: copy.start())

    def passes(self, d):
        if d == 3:
            loop(3, self.at.planes, self.passes_from)
        elif d < self.at.planes:
            self.passes_from(d)

    def passes_from(self, d):
        def each(i):
            owner = self.owner(i)

            @pl.when((owner == self.at.f + d) | (owner == self.at.f - d))
            def _():
                self.arrive(i)

        loop(0, self.items, each)

    def finish(self):
        loop(0, self.items, lambda i: self.outward(i, lambda copy: copy.wait_send()))


class Toward:
    def __init__(self, at, items, owner, part, taken, send, recv):
        self.at, self.items, self.owner, self.part, self.taken = at, items, owner, part, taken
        self.send, self.recv = send, recv

    def hop(self, i, up):
        at = self.at
        to = jnp.minimum(at.f + 1, at.planes - 1) if up else jnp.maximum(at.f - 1, 0)
        slot = i + 1 if up else i
        return remote(
            self.part(i), self.taken.at[slot], self.send.at[i], self.recv.at[slot], (at.c, to)
        )

    def step(self, d):
        at = self.at
        if d == 3:
            loop(3, at.planes, lambda j: self.step_to(at.planes + 2 - j))
        elif d < at.planes:
            self.step_to(d)

    def step_to(self, d):
        at = self.at

        def one(i, up, comes):
            @pl.when(comes)
            def _():
                self.hop(i, up).wait_recv()
                block = self.part(i)
                come = self.taken[i + 1 if up else i].astype(F32)
                block[...] = (block[...].astype(F32) + come).astype(BF16)

            self.hop(i, up).start()

        def each(i):
            @pl.when(self.owner(i) == at.f + d)
            def _():
                one(i, True, at.f > 0)

            @pl.when(self.owner(i) == at.f - d)
            def _():
                one(i, False, at.f < at.planes - 1)

        loop(0, self.items, each)

    def total(self, i, acc):
        at = self.at
        acc[...] = self.part(i)[...].astype(F32)

        @pl.when(at.f > 0)
        def _():
            self.hop(i, True).wait_recv()
            acc[...] += self.taken[i + 1].astype(F32)

        @pl.when(at.f < at.planes - 1)
        def _():
            self.hop(i, False).wait_recv()
            acc[...] += self.taken[i].astype(F32)

    def finish(self):
        def each(i):
            @pl.when(self.owner(i) > self.at.f)
            def _():
                self.hop(i, True).wait_send()

            @pl.when(self.owner(i) < self.at.f)
            def _():
                self.hop(i, False).wait_send()

        loop(0, self.items, each)


class Scatter:
    def __init__(self, at, part, pair, halves, far, send, pair_recv, recv):
        self.at, self.part, self.pair, self.halves, self.far = at, part, pair, halves, far
        self.send, self.pair_recv, self.recv = send.at[0], pair_recv, recv
        self.size = part.shape[1] // 2

    def to_partner(self, g):
        at = self.at
        return remote(
            self.part.at[at.other(g)],
            self.pair.at[g],
            self.send,
            self.pair_recv.at[g],
            (at.partner, at.f),
        )

    def across(self, i):
        at = self.at
        return remote(
            self.part.at[at.same(jnp.int32(3)), pl.ds(i * self.size, self.size)],
            self.halves.at[i],
            self.send,
            self.recv.at[i],
            (at.same(jnp.int32(1 + i)), at.f),
        )

    def beside(self, i):
        at = self.at
        to = at.same(jnp.int32(1 + i))
        return remote(
            self.part.at[to], self.far.at[i], self.send, self.recv.at[2 + i], (to, at.f)
        )

    def add_pair(self, g):
        self.to_partner(jnp.int32(g)).wait_recv()
        own = self.at.same(jnp.int32(g))
        both = self.part[own].astype(F32) + self.pair[g].astype(F32)
        self.part[own] = both.astype(BF16)

    def first(self):
        self.add_pair(3)
        for i in range(2):
            self.across(i).start()

    def second(self):
        for i in range(2):
            self.add_pair(1 + i)
        for i in range(2):
            self.across(i).wait_recv()
            to = self.at.same(jnp.int32(2 - i))
            rows = pl.ds(i * self.size, self.size)
            both = self.part[to, rows].astype(F32) + self.halves[i].astype(F32)
            self.part[to, rows] = both.astype(BF16)
            self.beside(1 - i).start()

    def total(self):
        self.to_partner(jnp.int32(0)).wait_recv()
        for i in range(2):
            self.beside(i).wait_recv()
        both = self.part[self.at.c].astype(F32) + self.pair[0].astype(F32)
        return both + (self.far[0].astype(F32) + self.far[1].astype(F32))

    def finish(self):
        at, blocks = self.at, self.part.at[pl.ds(0, CTX - 1)]
        remote(blocks, blocks, self.send, self.recv.at[0], (at.partner, at.f)).wait_send()


def standard(values):
    centre = jnp.mean(values, axis=-1, keepdims=True)
    offset = values - centre
    spread = jnp.mean(offset * offset, axis=-1, keepdims=True)
    rate = lax.rsqrt(spread + EPS)
    return offset * rate, rate


def standard_grad(e, normal, rate):
    return rate * (
        e - jnp.mean(e, axis=-1, keepdims=True) - normal * jnp.mean(e * normal, axis=-1, keepdims=True)
    )


def write_codes(r, at, seq):
    local = r.segments.shape[1]
    blocks, local_blocks = seq // BLOCK, local // BLOCK
    draws, _, heads = r.random.shape
    half = LANES // 2
    key = lax.rem(lax.broadcasted_iota(jnp.int32, (heads, LANES), 1), half)
    lower = lax.broadcasted_iota(jnp.int32, (1, LANES), 1) < half
    diagonal = lax.broadcasted_iota(jnp.int32, (heads, heads), 0) == lax.broadcasted_iota(
        jnp.int32, (heads, heads), 1
    )
    pair = r.globals[...]
    for b in range(local_blocks):
        block = at.c * local_blocks + b
        counted = jnp.abs(key - block) <= 1
        for j in range(draws):
            row = jnp.broadcast_to(r.random[j, b : b + 1, :].astype(F32), (heads, heads))
            drawn = jnp.sum(jnp.where(diagonal, row, 0.0), axis=1, keepdims=True)
            counted = counted | (key.astype(F32) == drawn)
        for j in range(pair.shape[1]):
            chosen = pair[:, j : j + 1]
            counted = counted | (key == chosen) | (chosen == block)
        code = jnp.where(counted | (key >= blocks), 0.0, -BIG)
        for d in range(heads // 2):
            both = jnp.where(lower, code[2 * d + 1 : 2 * d + 2], code[2 * d : 2 * d + 1])
            r.codes[d, b : b + 1, :] = both
    segments = r.segments[...].astype(F32)
    for d in range(heads // 2):
        r.codes[d, local_blocks : local_blocks + 1, :] = segments


def layer_kernel(r, planes):
    at = Place(planes)
    me, f = at.c, at.f
    local, width = r.tokens_in.shape
    seq = local * CTX
    blocks, local_blocks = seq // BLOCK, local // BLOCK
    part_rows = width // planes
    columns = width // CTX
    shard = r.down.shape[0]
    ff = planes * shard
    ff_blocks = ff // LANES // CTX
    shard_blocks = shard // LANES
    full_shard = shard_blocks == CTX
    tile = 2 * local
    k_own = lax.div(f * shard_blocks, CTX)
    has_down = lax.div(me, shard_blocks) == lax.rem(f, CTX // shard_blocks)
    down_place = lax.rem(me, shard_blocks)

    def down_owner(k):
        return lax.div(CTX * k + me, shard_blocks)

    my_rows = rows_of(f, part_rows)
    my_columns = rows_of(me, columns)
    my_tokens = rows_of(me, local)
    tokens, cotangent = r.tokg.at[my_tokens], r.cotg.at[my_tokens]

    barrier = pltpu.get_barrier_semaphore()
    loop(
        1,
        CTX,
        lambda d: pl.semaphore_signal(
            barrier, inc=1, device_id=(at.ctx_at(d), f), device_id_type=MESH
        ),
    )
    loop(
        1,
        planes,
        lambda d: pl.semaphore_signal(
            barrier, inc=1, device_id=(me, at.plane_at(d)), device_id_type=MESH
        ),
    )

    fetched = (
        (r.tokens_in, tokens), (r.gain_one_in, r.gain_one), (r.bias_one_in, r.bias_one),
        (r.gain_two_in, r.gain_two), (r.bias_two_in, r.bias_two), (r.bias_down_in, r.bias_down),
        (r.bias_up_in, r.bias_up), (r.segments_in, r.segments), (r.random_in, r.random),
        (r.globals_in, r.globals), (r.cotangent_in, cotangent),
    )
    fetch = [
        pltpu.make_async_copy(src, dst, r.fetch.at[i]) for i, (src, dst) in enumerate(fetched)
    ]
    for copy in fetch:
        copy.start()
    layer_copy = pltpu.make_async_copy(r.layer, r.layer_out, r.fetch.at[len(fetch)])
    grad_copy = pltpu.make_async_copy(r.grad, r.tokens_grad, r.fetch.at[len(fetch) + 1])
    totals_copy = pltpu.make_async_copy(r.sums, r.totals, r.fetch.at[len(fetch) + 2])
    stage_j = [
        pltpu.make_async_copy(
            r.joint.at[:, pl.ds(pl.multiple_of(width * j + columns * me, LANES), columns)],
            r.wj.at[my_rows, pl.ds(columns * j, columns)],
            r.stage.at[j],
        )
        for j in range(3)
    ]
    stage_o = pltpu.make_async_copy(
        r.outw.at[:, my_columns], r.wo.at[my_rows, my_columns], r.stage.at[3]
    )
    stage_u = [
        pltpu.make_async_copy(
            r.up.at[:, pl.ds(pl.multiple_of(CTX * LANES * k + LANES * me, LANES), LANES)],
            r.wu.at[my_rows, pl.ds(LANES * k, LANES)],
            r.stage.at[4 + k],
        )
        for k in range(ff_blocks)
    ]
    stage_d = pltpu.make_async_copy(
        r.down.at[rows_of(down_place, LANES), :],
        r.wd.at[rows_of(k_own, LANES), :],
        r.stage.at[4 + ff_blocks],
    )
    for copy in [*stage_j, stage_o, *stage_u]:
        copy.start()

    @pl.when(has_down)
    def _():
        stage_d.start()

    for copy in fetch[1:10]:
        copy.wait()
    small, short = r.small, r.small.shape[1]
    small[...] = jnp.zeros_like(small)
    for i, vector in enumerate((r.gain_one, r.bias_one, r.gain_two, r.bias_two, r.bias_down)):
        small[i : i + 1, 0:part_rows] = vector[...].astype(F32).reshape(1, part_rows)
    for i in range(shard // short):
        piece = r.bias_up[i * short : (i + 1) * short]
        small[5 + i : 6 + i, :] = piece.astype(F32).reshape(1, short)

    def token_gather(src, dst, sems):
        bulk = dst.at[pl.ds(0, (CTX - 1) * local)]
        return Gather(at, src, lambda c: dst.at[rows_of(c, local)], bulk, *sems)

    tok = token_gather(tokens, r.tokg, r.tok_sem)
    cot = token_gather(cotangent, r.cotg, r.cot_sem)
    x2 = token_gather(r.x2.at[my_tokens], r.x2, r.x2_sem)
    attg = token_gather(r.attg.at[my_tokens], r.attg, r.attg_sem)
    wog = Gather(
        at, r.wo.at[:, my_columns], lambda c: r.wo.at[:, rows_of(c, columns)],
        r.wo.at[:, pl.ds(0, (CTX - 1) * columns)], *r.wog_sem
    )
    seven = pl.ds(0, CTX - 1)
    codes = Exchange(
        at, lambda c: r.codes.at[c], lambda c: r.codeg.at[c], r.codeg.at[seven], *r.code_sem
    )
    att_swap = Exchange(
        at, lambda c: r.att.at[rows_of(c, local)], lambda c: r.attx.at[c], r.attx.at[seven], *r.att_sem
    )

    def token_swap(src, dst, sems):
        return Exchange(
            at, lambda c: src.at[c], lambda c: dst.at[rows_of(c, local)], src.at[seven], *sems
        )

    dat_swap = token_swap(r.dat, r.datg, r.dat_sem)
    br_swap = token_swap(r.brs, r.brg, r.br_sem)
    rest = pl.ds(0, planes - 1)
    small_planes = Planes(
        at, lambda to: small, lambda p: r.smallg.at[p], r.smallg.at[rest], *r.small_sem
    )

    def weight_line(ref, sems, width_ds):
        return Line(
            at, planes, lambda i: i, lambda i: ref.at[rows_of(i, part_rows), width_ds], *sems
        )

    wj = weight_line(r.wj, r.wj_sem, slice(None))
    wo = weight_line(r.wo, r.wo_sem, my_columns)
    wu = weight_line(r.wu, r.wu_sem, slice(None))
    wd = Line(at, ff_blocks, down_owner, lambda k: r.wd.at[rows_of(k, LANES), :], *r.wd_sem)
    back, feed, first = (Scatter(at, *group) for group in (r.back, r.feed, r.first))

    def grad_line(grad, taken, sems):
        return Toward(
            at, planes, lambda i: i, lambda i: grad.at[rows_of(i, part_rows), :], taken, *sems
        )

    dd = Toward(at, ff_blocks, down_owner, lambda k: r.dwd.at[k], r.rd, *r.dwd_sem)
    du = grad_line(r.du, r.ru, r.du_sem)
    do = grad_line(r.do, r.ro, r.do_sem)
    dk = grad_line(r.dk, r.rk, r.dk_sem)
    dq = grad_line(r.dq, r.rq, r.dq_sem)

    class Owned:
        def __init__(self, number, line, acc, total, out, sems):
            self.line, self.acc, self.sum = line, acc, total
            self.gather = Gather(at, total, lambda c: out.at[c], out.at[seven], *sems)
            self.own = pltpu.make_async_copy(total, out.at[me], r.own.at[number])

        def total(self):
            self.line.total(f, self.acc)
            self.sum[...] = self.acc[...].astype(BF16)
            self.gather.start()
            self.own.start()

        def near(self, i):
            self.gather.near(i)

        def far(self):
            self.gather.far()

        def waits(self):
            self.gather.waits()
            self.own.wait()

        def finish(self):
            self.gather.finish()

    gu = Owned(0, du, r.au, r.tu, r.gu, r.gu_sem)
    go = Owned(1, do, r.ao, r.to, r.go, r.go_sem)
    gk = Owned(2, dk, r.ak, r.tk, r.gk, r.gk_sem)
    gq = Owned(3, dq, r.aq, r.tq, r.gq, r.gq_sem)

    class OwnedDown:
        def __init__(self):
            if full_shard:
                self.gather = Gather(at, r.td, lambda c: r.gd.at[c], r.gd.at[seven], *r.gd_sem)
            self.own = pltpu.make_async_copy(r.td, r.gd.at[down_place], r.own.at[4])

        def copy(self, d):
            send, recv = r.gd_sem
            block = r.gd.at[down_place]
            return remote(r.td, block, send.at[d - 1], recv.at[down_place], (at.ctx_at(d), f))

        def total(self):
            @pl.when(has_down)
            def _():
                dd.total(k_own, r.ad)
                r.td[...] = r.ad[...].astype(BF16)
                self.own.start()
                if not full_shard:
                    loop(1, CTX, lambda d: self.copy(d).start())

            if full_shard:
                self.gather.start()

        def near(self, i):
            if full_shard:
                self.gather.near(i)

        def far(self):
            if full_shard:
                self.gather.far()

        def waits(self):
            @pl.when(has_down)
            def _():
                self.own.wait()

            if full_shard:
                self.gather.waits()
                return

            def take(b):
                @pl.when(me != lax.rem(f * shard_blocks + b, CTX))
                def _():
                    block, (send, recv) = r.gd.at[b], r.gd_sem
                    to = (at.ctx_at(jnp.int32(1)), f)
                    remote(block, block, send.at[0], recv.at[b], to).wait_recv()

            loop(0, shard_blocks, take)

        def finish(self):
            if full_shard:
                self.gather.finish()
                return

            @pl.when(has_down)
            def _():
                loop(1, CTX, lambda d: self.copy(d).wait_send())

    gd = OwnedDown()

    class Sums:
        def __init__(self, own, acc, sent, ctx_in, plane_in, ctx_sems, plane_sems):
            self.own, self.acc, self.sent, self.ctx_in, self.plane_in = own, acc, sent, ctx_in, plane_in
            self.swap = Exchange(
                at, lambda c: own, lambda c: ctx_in.at[c], ctx_in.at[seven], *ctx_sems
            )
            self.planes = Planes(
                at, lambda to: sent, lambda p: plane_in.at[p], plane_in.at[rest], *plane_sems
            )

        def put(self, row, vector):
            for k in range(width // LANES):
                self.acc[row + k : row + k + 1, :] = vector[:, k * LANES : (k + 1) * LANES]

        def start(self):
            self.own[...] = self.acc[...].astype(BF16)
            self.swap.start()

        def middle(self):
            self.swap.waits()

            def add(d):
                self.acc[...] += self.ctx_in[at.ctx_at(d)].astype(F32)

            loop(1, CTX, add)
            self.sent[...] = self.acc[...].astype(BF16)
            self.planes.start()

        def end(self):
            self.planes.waits()

            def add(d):
                self.acc[...] += self.plane_in[at.plane_at(d)].astype(F32)

            loop(1, planes, add)

        def row(self, row):
            for k in range(width // LANES):
                r.wide[0:1, k * LANES : (k + 1) * LANES] = self.acc[row + k : row + k + 1, :]
            return r.wide[0:1, :]

        def finish(self):
            self.swap.finish()
            self.planes.finish()

    early, late = Sums(*r.early), Sums(*r.late)
    params = r.params

    def open_devices():
        pl.semaphore_wait(barrier, CTX - 1 + planes - 1)
        fetch[0].wait()
        fetch[10].wait()

    def wj_start():
        for copy in stage_j:
            copy.wait()
        wj.start()

    def wo_start():
        stage_o.wait()
        wo.start()

    def wu_start():
        for copy in stage_u:
            copy.wait()
        wu.start()

    def wd_start():
        @pl.when(has_down)
        def _():
            stage_d.wait()

        wd.start()

    def make_codes():
        write_codes(r, at, seq)
        r.codeg[me] = r.codes[me]

    def take_params():
        r.smallg[f] = small[...]
        small_planes.waits()
        params[...] = jnp.zeros_like(params)
        r.wide[...] = jnp.zeros_like(r.wide)

        def add(p):
            r.wide[:, 0:short] = r.smallg[p, 0:8, :]
            params[...] += pltpu.roll(r.wide[...], p * part_rows, axis=1)

        loop(0, planes, add)
        for k in range(ff_blocks):
            block = CTX * k + me
            place = lax.rem(block, shard_blocks) * LANES
            lanes = pl.ds(pl.multiple_of(lax.rem(place, short), LANES), LANES)
            rows = r.smallg[down_owner(k), :, lanes]
            number = lax.broadcasted_iota(jnp.int32, rows.shape, 0)
            r.ub[0:1, k * LANES : (k + 1) * LANES] = jnp.sum(
                jnp.where(number == 5 + lax.div(place, short), rows, 0.0), axis=0, keepdims=True
            )

    def norm_tokens(g):
        tok.wait(at.other(g))
        rows = rows_of(at.chip_at(g), tile)
        normal, _ = standard(r.tokg[rows, :].astype(F32))
        r.x1[rows, :] = (normal * params[0:1, :] + params[1:2, :]).astype(BF16)

    lane = lax.broadcasted_iota(jnp.int32, (tile, columns), 1)
    low = lane < columns // 2
    zero_tile = jnp.zeros((tile, columns), BF16)

    def project(i):
        rows = rows_of(i, tile)
        projected = dot(r.x1[rows, :], r.wj[...]).astype(BF16)
        q = projected[:, :columns] * jnp.array(0.125, BF16)
        k = projected[:, columns : 2 * columns]
        v = projected[:, 2 * columns :]
        half = lax.rem(lane, columns // 2)
        segment_place = lax.rem(lax.broadcasted_iota(jnp.int32, (LANES, local), 0), LANES // 2) - blocks
        parts = []
        for e in range(2):
            code = r.codeg[2 * i + e]
            hot = jnp.where(
                code[local_blocks : local_blocks + 1] == segment_place.astype(F32), 1.0, 0.0
            ).T
            for b in range(local_blocks):
                parts.append(hot[b * BLOCK : (b + 1) * BLOCK] + code[b : b + 1])
        ext = jnp.concatenate(parts, axis=0)
        token = lax.broadcasted_iota(jnp.int32, (tile, columns), 0) + i * tile
        hot = jnp.where(half == lax.div(token, BLOCK), 1.0, 0.0)
        k_ext = jnp.where(
            half < blocks, hot, jnp.where(half < blocks + SEGMENTS, (1.0 - ext) * -BIG, 0.0)
        ).astype(BF16)
        ext = ext.astype(BF16)
        r.q[rows, :] = q
        r.qa[0, rows, :] = jnp.where(low, q, ext)
        r.qa[1, rows, :] = jnp.where(low, ext, q)
        r.ka[0, rows, :] = jnp.where(low, k, k_ext)
        r.ka[1, rows, :] = jnp.where(low, k_ext, k)
        r.km[0, rows, :] = jnp.where(low, k, zero_tile)
        r.km[1, rows, :] = jnp.where(low, zero_tile, k)
        r.vm[0, rows, :] = jnp.where(low, v, zero_tile)
        r.vm[1, rows, :] = jnp.where(low, zero_tile, v)

    def attend(i):
        rows = rows_of(i, tile)
        out = None
        for h in range(2):
            scores = dot_nt(r.qa[h, rows, :], r.ka[h])
            weights = jnp.exp(scores - jnp.max(scores, axis=1, keepdims=True))
            shares = (weights / jnp.sum(weights, axis=1, keepdims=True)).astype(BF16)
            r.probs[h, rows, :] = shares
            term = dot(shares, r.vm[h])
            out = term if out is None else out + term
        r.att[rows, :] = out.astype(BF16)

    def att_swap_start():
        att_swap.start()
        r.attx[me] = r.att[my_tokens, :]

    def project_out():
        att_swap.waits()
        for c in range(CTX):
            r.attg[my_tokens, c * columns : (c + 1) * columns] = r.attx[c]
        wog.waits()
        middle = tokens[...].astype(F32) + dot(r.attg[my_tokens, :], r.wo[...])
        normal, rate = standard(middle)
        r.middle[...] = middle
        r.n2[...] = normal
        r.rate2[...] = jnp.broadcast_to(rate, r.rate2.shape)
        r.x2[my_tokens, :] = (normal * params[2:3, :] + params[3:4, :]).astype(BF16)

    r.ubg[...] = jnp.zeros_like(r.ubg)

    def hidden_units(g):
        x2.wait(at.other(g))
        rows = rows_of(at.chip_at(g), tile)
        up_sum = dot(r.x2[rows, :], r.wu[...]) + r.ub[...]
        share = 0.5 * (1.0 + lax.erf(up_sum * 0.7071067811865476))
        r.hidden[rows, :] = (up_sum * share).astype(BF16)
        r.slope[rows, :] = share + up_sum * jnp.exp(-0.5 * up_sum * up_sum) * 0.3989422804014327

    def down_grad():
        def one(k):
            r.dwd[k] = dot_tn(r.hidden[:, rows_of(k, LANES)], r.cotg[...]).astype(BF16)

        loop(0, ff_blocks, one)

    def far_first(j):
        return jnp.where(j == 0, 3, jnp.where(j == 3, 0, j))

    def put_part(scatter, g, part):
        chip = at.chip_at(g)
        part = part.astype(BF16)
        scatter.part[2 * chip] = part[:local]
        scatter.part[2 * chip + 1] = part[local:]
        scatter.to_partner(g).start()

    def feed_back(j):
        g = far_first(j)
        rows = rows_of(at.chip_at(g), tile)
        up_grad = (dot_nt(r.cotg[rows, :], r.wd[...]) * r.slope[rows, :]).astype(BF16)
        r.upg[rows, :] = up_grad
        r.ubg[...] += jnp.sum(up_grad.astype(F32), axis=0, keepdims=True)
        put_part(back, g, dot_nt(up_grad, r.wu[...]))

    def feed_part(j):
        g = far_first(j)
        put_part(feed, g, dot(r.hidden[rows_of(at.chip_at(g), tile), :], r.wd[...]))

    def first_part(j):
        g = far_first(j)
        put_part(first, g, dot_nt(r.pg[rows_of(at.chip_at(g), tile), :], r.wj[...]))

    rows_tile = min(tile, width)

    def weight_grad(out, left, right, lanes=slice(None)):
        def body(i):
            out[rows_of(i, rows_tile), :] = dot_tn(
                left[:, rows_of(i, rows_tile)], right[:, lanes]
            ).astype(BF16)

        loop(0, width // rows_tile, body)

    def up_weight_grad():
        weight_grad(r.du, r.x2, r.upg)

    def middle_back():
        normed_two_grad = back.total()
        normal = r.n2[...]
        cot_own = cotangent[...].astype(F32)
        early.acc[...] = jnp.zeros_like(early.acc)
        early.put(0, jnp.sum(normed_two_grad * normal, axis=0, keepdims=True))
        early.put(8, jnp.sum(normed_two_grad, axis=0, keepdims=True))
        early.put(16, jnp.sum(cot_own, axis=0, keepdims=True))
        for k in range(ff_blocks):
            early.acc[pl.ds(24 + CTX * k + me, 1), :] = r.ubg[0:1, k * LANES : (k + 1) * LANES]
        middle_grad = cot_own + standard_grad(
            normed_two_grad * params[2:3, :], normal, r.rate2[:, 0:1]
        )
        r.grad[...] = middle_grad
        branch = middle_grad.astype(BF16)
        attended_grad = dot_nt(branch, r.wo[...]).astype(BF16)
        for c in range(CTX):
            r.dat[c] = attended_grad[:, c * columns : (c + 1) * columns]
            r.brs[c] = branch[:, c * columns : (c + 1) * columns]
        r.acc_k[...] = jnp.zeros_like(r.acc_k)
        r.acc_v[...] = jnp.zeros_like(r.acc_v)

    def dat_start():
        dat_swap.start()
        r.datg[my_tokens, :] = r.dat[me]

    def br_start():
        br_swap.start()
        r.brg[my_tokens, :] = r.brs[me]

    def attend_back(i):
        rows = rows_of(i, tile)
        grad = r.datg[rows, :]
        both = grad.astype(F32) * r.att[rows, :].astype(F32)
        q = r.q[rows, :]
        query_grad = None
        for h in range(2):
            keep = low if h == 0 else ~low
            delta = jnp.sum(jnp.where(keep, both, 0.0), axis=1, keepdims=True)
            probs = r.probs[h, rows, :]
            prob_grad = dot_nt(grad, r.vm[h])
            score_grad = (probs.astype(F32) * (prob_grad - delta)).astype(BF16)
            term = dot(score_grad, r.km[h])
            query_grad = term if query_grad is None else query_grad + term
            r.acc_k[...] += dot_tn(score_grad, jnp.where(keep, q, zero_tile))
            r.acc_v[...] += dot_tn(probs, jnp.where(keep, grad, zero_tile))
        r.pg[rows, :columns] = (query_grad * 0.125).astype(BF16)

    def keys_back():
        r.pg[:, columns : 2 * columns] = r.acc_k[...].astype(BF16)
        r.pg[:, 2 * columns :] = r.acc_v[...].astype(BF16)

    def key_weight_grad():
        weight_grad(r.dk, r.x1, r.pg, slice(columns, None))

    def query_weight_grad():
        weight_grad(r.dq, r.x1, r.pg, slice(0, columns))

    def out_weight_grad():
        attg.waits()
        br_swap.waits()
        weight_grad(r.do, r.attg, r.brg)

    def layer_end():
        r.layer[...] = (r.middle[...] + feed.total() + params[4:5, :]).astype(BF16)
        layer_copy.start()

    def tokens_back():
        normed_one_grad = first.total()
        normal, rate = standard(tokens[...].astype(F32))
        late.put(0, jnp.sum(normed_one_grad * normal, axis=0, keepdims=True))
        late.put(8, jnp.sum(normed_one_grad, axis=0, keepdims=True))
        r.grad[...] += standard_grad(normed_one_grad * params[0:1, :], normal, rate)
        grad_copy.start()

    def write_totals():
        for i, (sums, row) in enumerate(((late, 0), (late, 8), (early, 0), (early, 8), (early, 16))):
            vector = jnp.broadcast_to(sums.row(row), (8, width))
            turned = pltpu.roll(vector, lax.rem((planes - f) * part_rows, width), axis=1)
            r.sums[i : i + 1, :] = turned[0:1]
        for k in range(shard_blocks):
            r.sums[5:6, k * LANES : (k + 1) * LANES] = early.acc[
                pl.ds(24 + f * shard_blocks + k, 1), :
            ]

    def finish(*ended):
        for each in ended:
            each.finish()

    def finish_forward():
        finish(tok, cot, wog, x2, codes, att_swap, small_planes, wj, wo, wu, wd)

    def finish_middle():
        finish(attg, dat_swap, br_swap, dd, back)

    open_devices()
    wo_start()
    make_codes()
    codes.start()
    wj_start()
    small_planes.start()
    tok.start()
    wo.passes(1)
    take_params()
    wo.passes(2)

    def step_1(i):

        @pl.when(i == 1)
        def _():
            wu_start()
            cot.start()
            tok.near(0)
            wj.passes(1)
            tok.near(1)
            cot.near(0)
            wj.passes(2)
            tok.far()
            cot.near(1)
            wo.passes(3)

        norm_tokens(i)

    loop(0, 4, step_1)

    wog.start()
    wj.passes(3)
    codes.waits()

    def step_2(i):

        @pl.when(i == 1)
        def _():
            wd_start()
            wu.passes(1)

        project(i)

    loop(0, 4, step_2)


    def step_3(i):

        @pl.when(i == 2)
        def _():
            wog.near(1)
            wog.near(0)

        attend(i)

    loop(0, 4, step_3)

    att_swap_start()
    cot.far()
    wog.far()
    wu.passes(2)
    project_out()
    x2.start()
    wd.passes(1)
    x2.near(0)
    x2.near(1)
    wu.passes(3)

    def step_4(i):

        @pl.when(i == 2)
        def _():
            x2.far()
            wd.passes(2)

        hidden_units(i)

    loop(0, 4, step_4)

    attg.start()
    cot.waits()
    down_grad()
    wd.passes(3)
    dd.step(3)

    def step_5(i):

        @pl.when(i == 2)
        def _():
            back.first()

        feed_back(i)

    loop(0, 3, step_5)

    back.second()
    attg.near(0)
    attg.near(1)
    dd.step(2)
    feed_part(jnp.int32(0))
    feed_back(jnp.int32(3))
    up_weight_grad()
    du.step(3)
    middle_back()
    dat_start()
    early.start()
    dd.step(1)
    loop(1, 4, feed_part)
    attg.far()
    feed.first()
    dat_swap.waits()

    def step_6(i):

        @pl.when(i == 1)
        def _():
            du.step(2)
            br_start()

        @pl.when(i == 2)
        def _():
            gd.total()
            feed.second()

        @pl.when(i == 3)
        def _():
            early.middle()
            du.step(1)

        attend_back(i)

    loop(0, 4, step_6)

    finish_forward()
    keys_back()

    def step_7(i):

        @pl.when(i == 1)
        def _():
            key_weight_grad()
            dk.step(3)
            query_weight_grad()
            dq.step(3)
            out_weight_grad()
            finish_middle()
            first.first()

        first_part(i)

    loop(0, 4, step_7)

    gd.near(1)
    gd.near(0)
    dk.step(2)
    dq.step(2)
    first.second()
    do.step(3)
    gu.total()
    dk.step(1)
    dq.step(1)
    gk.total()
    gq.total()
    do.step(2)
    tokens_back()
    late.start()
    do.step(1)
    go.total()
    gu.near(0)
    gu.near(1)
    late.middle()
    gk.near(0)
    gk.near(1)
    gq.near(1)
    gd.far()
    go.near(0)
    go.near(1)
    gq.near(0)
    gu.far()
    gk.far()
    gq.far()
    go.far()
    layer_end()
    late.end()
    early.end()
    write_totals()
    totals_copy.start()
    for each in (gd, gu, go, gk, gq):
        each.waits()
    finish(gu, go, gk, gq, gd, early, late, du, do, dk, dq, feed, first)
    for copy in (layer_copy, grad_copy, totals_copy):
        copy.wait()


def shards(
    tokens,
    segment_ids,
    random_blocks,
    global_blocks,
    first_gain,
    first_bias,
    joint_weight,
    output_weight,
    second_gain,
    second_bias,
    up_weight,
    up_bias,
    down_weight,
    down_bias,
    cotangent,
):
    local, width = tokens.shape[1:]
    ctx, planes = lax.axis_size("ctx"), lax.axis_size("fsdp")
    heads = random_blocks.shape[2]
    seq = local * ctx
    blocks = seq // BLOCK
    part_rows = width // planes
    columns = width // ctx
    ff_shard = up_bias.shape[0]
    ff = ff_shard * planes
    ff_blocks = ff // LANES // ctx
    shard_blocks = ff_shard // LANES
    ff_part = ff // ctx
    assert ctx == CTX and columns == LANES and heads == 2 * ctx and blocks + SEGMENTS <= 64
    assert CTX % shard_blocks == 0 and ff // width == ff_blocks

    hbm = pl.BlockSpec(memory_space=pl.ANY)
    inputs = dict(
        tokens_in=tokens[0],
        cotangent_in=cotangent[0],
        segments_in=segment_ids,
        random_in=random_blocks[0].transpose(2, 0, 1),
        globals_in=global_blocks,
        gain_one_in=first_gain,
        bias_one_in=first_bias,
        gain_two_in=second_gain,
        bias_two_in=second_bias,
        bias_up_in=up_bias,
        bias_down_in=down_bias,
        joint=joint_weight,
        outw=output_weight,
        up=up_weight,
        down=down_weight,
    )
    outputs = dict(
        layer_out=((local, width), BF16),
        tokens_grad=((local, width), F32),
        totals=((8, width), F32),
        gk=((ctx, part_rows, 2 * columns), BF16),
        gq=((ctx, part_rows, columns), BF16),
        go=((ctx, part_rows, columns), BF16),
        gu=((ctx, part_rows, ff_part), BF16),
        gd=((shard_blocks, LANES, width), BF16),
    )
    dma = lambda n: pltpu.SemaphoreType.DMA((n,))
    v16 = lambda *shape: pltpu.VMEM(shape, BF16)
    v32 = lambda *shape: pltpu.VMEM(shape, F32)
    scatter = (
        v16(ctx, local, width), v16(4, local, width), v16(2, local // 2, width), v16(2, local, width),
        dma(1), dma(4), dma(4),
    )
    gather, swap = (dma(1), dma(ctx)), (dma(1), dma(1))
    line, toward = (dma(2 * planes), dma(planes)), (dma(planes), dma(planes + 1))
    short = max(part_rows, LANES)
    vectors = lambda rows: (
        v16(rows, LANES), v32(rows, LANES), v16(rows, LANES), v16(ctx, rows, LANES),
        v16(planes, rows, LANES), swap, swap,
    )
    copied = lambda name: pltpu.VMEM(inputs[name].shape, inputs[name].dtype)
    scratch = dict(
        segments=copied("segments_in"), random=copied("random_in"), globals=copied("globals_in"),
        gain_one=copied("gain_one_in"), bias_one=copied("bias_one_in"),
        gain_two=copied("gain_two_in"), bias_two=copied("bias_two_in"),
        bias_up=copied("bias_up_in"), bias_down=copied("bias_down_in"), fetch=dma(14),
        layer=v16(local, width), grad=v32(local, width), sums=v32(8, width),
        wj=v16(width, 3 * columns), wo=v16(width, width), wu=v16(width, ff_part),
        wd=v16(ff_part, width), tokg=v16(seq, width), cotg=v16(seq, width),
        x1=v16(seq, width), x2=v16(seq, width), attg=v16(seq, width),
        codes=v32(ctx, 8, LANES), codeg=v32(ctx, 8, LANES), small=v32(16, short),
        smallg=v32(planes, 16, short), params=v32(8, width), wide=v32(8, width),
        ub=v32(1, ff_part), ubg=v32(1, ff_part), q=v16(seq, columns),
        qa=v16(2, seq, columns), ka=v16(2, seq, columns), km=v16(2, seq, columns),
        vm=v16(2, seq, columns), probs=v16(2, seq, seq), att=v16(seq, columns),
        attx=v16(ctx, local, columns), middle=v32(local, width), n2=v32(local, width),
        rate2=v32(local, LANES), hidden=v16(seq, ff_part), slope=v32(seq, ff_part),
        upg=v16(seq, ff_part), dat=v16(ctx, local, columns), brs=v16(ctx, local, columns),
        datg=v16(seq, columns), brg=v16(seq, columns), acc_k=v32(seq, columns),
        acc_v=v32(seq, columns), pg=v16(seq, 3 * columns), early=vectors(64), late=vectors(16),
        dk=v16(width, 2 * columns), dq=v16(width, columns), do=v16(width, columns),
        du=v16(width, ff_part), dwd=v16(ff_blocks, LANES, width),
        rk=v16(planes + 1, part_rows, 2 * columns), rq=v16(planes + 1, part_rows, columns),
        ro=v16(planes + 1, part_rows, columns), ru=v16(planes + 1, part_rows, ff_part),
        rd=v16(ff_blocks + 1, LANES, width),
        ak=v32(part_rows, 2 * columns), aq=v32(part_rows, columns), ao=v32(part_rows, columns),
        au=v32(part_rows, ff_part), ad=v32(LANES, width),
        tk=v16(part_rows, 2 * columns), tq=v16(part_rows, columns), to=v16(part_rows, columns),
        tu=v16(part_rows, ff_part), td=v16(LANES, width),
        stage=dma(5 + ff_blocks), own=dma(5), wd_sem=(dma(2 * ff_blocks), dma(ff_blocks)),
        dwd_sem=(dma(ff_blocks), dma(ff_blocks + 1)), back=scatter, feed=scatter, first=scatter,
        tok_sem=gather, cot_sem=gather, wog_sem=gather, x2_sem=gather, attg_sem=gather,
        gk_sem=gather, gq_sem=gather, go_sem=gather, gu_sem=gather, gd_sem=gather if shard_blocks == ctx else (dma(ctx - 1), dma(ctx)),
        code_sem=swap, att_sem=swap, dat_sem=swap, br_sem=swap,
        small_sem=swap, wj_sem=line, wo_sem=line, wu_sem=line,
        dk_sem=toward, dq_sem=toward, do_sem=toward, du_sem=toward,
    )
    shapes, scratch_tree = jax.tree.flatten(scratch)
    ins, outs = len(inputs), len(outputs)

    def kernel(*refs):
        held = dict(zip([*inputs, *outputs], refs, strict=False))
        held |= jax.tree.unflatten(scratch_tree, refs[ins + outs :])
        layer_kernel(types.SimpleNamespace(**held), planes)

    layer_out, tokens_grad, totals, gk, gq, go, gu, gd = pl.pallas_call(
        kernel,
        out_shape=[jax.ShapeDtypeStruct(shape, dtype) for shape, dtype in outputs.values()],
        in_specs=[hbm] * ins,
        out_specs=[hbm] * outs,
        scratch_shapes=shapes,
        compiler_params=pltpu.CompilerParams(
            collective_id=0, has_side_effects=True, fuse_transposed_lhs_in_matmul=True,
            vmem_limit_bytes=60 * 1024 * 1024
        ),
    )(*inputs.values())

    group = ctx
    quads = ctx // group
    steps = ff_blocks * quads

    def spread(ref, out):
        for q in range(group):
            out[:, q * columns : (q + 1) * columns] = ref[q].astype(F32)

    def finish(out_in, grad_in, totals, gk, gq, go, gu, gd, joint, outw, up, down, out, grad, *vectors):
        step = pl.program_id(0)

        @pl.when(step < quads)
        def _():
            spread(gq, joint)
            spread(go, outw)

        @pl.when((step >= quads) & (step < 3 * quads))
        def _():
            spread(gk, joint)

        spread(gu, up)
        down[...] = gd[...].reshape(down.shape).astype(F32)
        out[...] = out_in[...]
        grad[...] = grad_in[...]
        for i, vector in enumerate(vectors[:5]):
            vector[...] = totals[i : i + 1, 0:part_rows].reshape(part_rows)
        vectors[5][...] = totals[5:6, 0:ff_shard].reshape(ff_shard)

    def from_places(start, count):
        place = lambda i: jnp.clip(i - start, 0, count - 1)
        return pl.BlockSpec(
            (group, part_rows, columns), lambda i: (place(i) % quads, 0, place(i) // quads)
        )

    def to_columns(count):
        return pl.BlockSpec((part_rows, group * columns), lambda i: (0, jnp.minimum(i, count - 1)))

    down_group = max(shard_blocks // steps, 1)
    down_place = lambda i: jnp.minimum(i, shard_blocks // down_group - 1)
    whole = pl.BlockSpec(memory_space=pltpu.VMEM)
    tokens_spec = pl.BlockSpec((local // steps, width), lambda i: (i, 0))
    made = pl.pallas_call(
        finish,
        grid=(steps,),
        out_shape=[
            jax.ShapeDtypeStruct(shape, dtype)
            for shape, dtype in (
                ((part_rows, 3 * width), F32), ((part_rows, width), F32), ((part_rows, ff), F32),
                ((ff_shard, width), F32), ((local, width), BF16), ((local, width), F32),
                *([((part_rows,), F32)] * 5), ((ff_shard,), F32),
            )
        ],
        in_specs=[
            tokens_spec,
            tokens_spec,
            whole,
            from_places(quads, 2 * quads),
            from_places(0, quads),
            from_places(0, quads),
            from_places(0, steps),
            pl.BlockSpec((down_group, LANES, width), lambda i: (down_place(i), 0, 0)),
        ],
        out_specs=[
            to_columns(3 * quads),
            to_columns(quads),
            to_columns(steps),
            pl.BlockSpec((down_group * LANES, width), lambda i: (down_place(i), 0)),
            tokens_spec,
            tokens_spec,
            *([whole] * 6),
        ],
        compiler_params=pltpu.CompilerParams(vmem_limit_bytes=60 * 1024 * 1024),
    )(layer_out, tokens_grad, totals, gk, gq, go, gu, gd)
    return (
        made[4][None],
        made[5][None],
        made[6],
        made[7],
        made[0],
        made[1],
        made[8],
        made[9],
        made[2],
        made[11],
        made[3],
        made[10],
    )


def solution(mesh):
    in_specs = (
        P("fsdp", "ctx", None),
        P("fsdp", "ctx"),
        P("fsdp", "ctx", None, None),
        P("fsdp", None),
        P("fsdp"),
        P("fsdp"),
        P("fsdp", None),
        P("fsdp", None),
        P("fsdp"),
        P("fsdp"),
        P("fsdp", None),
        P("fsdp"),
        P("fsdp", None),
        P("fsdp"),
        P("fsdp", "ctx", None),
    )
    out_specs = (
        P("fsdp", "ctx", None),
        P("fsdp", "ctx", None),
        P("fsdp"),
        P("fsdp"),
        P("fsdp", None),
        P("fsdp", None),
        P("fsdp"),
        P("fsdp"),
        P("fsdp", None),
        P("fsdp"),
        P("fsdp", None),
        P("fsdp"),
    )
    return jax.shard_map(shards, mesh=mesh, in_specs=in_specs, out_specs=out_specs, check_vma=False)
```
